32 devices in a mesh: fsdp: 32 (over z, y, x, core).
Axes of the slice: x: 2, y: 2, z: 4, core: 2. Of those that a mesh axis runs over, the one named last changes fastest.
Arguments:
- inputs: bfloat16 [8192, 2048], P('fsdp'), may hold values from -6 to 6
- doc_ids: int32 [32, 256], P('fsdp'), may hold values from 0 to 63, never falling along the last dimension, each value on 1 to 128 neighbouring positions
- attn_gain: bfloat16 [2048], P('fsdp'), may hold values from 0.5 to 1.5
- attn_shift: bfloat16 [2048], P('fsdp'), may hold values from -1.1953125 to 1.1953125
- ffn_gain: bfloat16 [2048], P('fsdp'), may hold values from 0.5 to 1.5
- ffn_shift: bfloat16 [2048], P('fsdp'), may hold values from -1.1953125 to 1.1953125
- qkv_weight: bfloat16 [2048, 6144], P('fsdp'), may hold values from -0.125 to 0.125
- qkv_bias: bfloat16 [6144], P('fsdp'), may hold values from -1.1953125 to 1.1953125
- proj_weight: bfloat16 [2048, 2048], P('fsdp'), may hold values from -0.5 to 0.5
- proj_bias: bfloat16 [2048], P('fsdp'), may hold values from -1.1953125 to 1.1953125
- up_weight: bfloat16 [2048, 8192], P('fsdp'), may hold values from -0.125 to 0.125
- up_bias: bfloat16 [8192], P('fsdp'), may hold values from -1.1953125 to 1.1953125
- down_weight: bfloat16 [8192, 2048], P('fsdp'), may hold values from -0.09375 to 0.09375
- down_bias: bfloat16 [2048], P('fsdp'), may hold values from -1.1953125 to 1.1953125
- cotangent: bfloat16 [8192, 2048], P('fsdp'), may hold values from -6 to 6
Outputs:
- layer_out: float32 [8192, 2048], P('fsdp')
- grad_inputs: float32 [8192, 2048], P('fsdp')
- grad_attn_gain: float32 [2048], P('fsdp')
- grad_attn_shift: float32 [2048], P('fsdp')
- grad_ffn_gain: float32 [2048], P('fsdp')
- grad_ffn_shift: float32 [2048], P('fsdp')
- grad_qkv_weight: float32 [2048, 6144], P('fsdp')
- grad_qkv_bias: float32 [6144], P('fsdp')
- grad_proj_weight: float32 [2048, 2048], P('fsdp')
- grad_proj_bias: float32 [2048], P('fsdp')
- grad_up_weight: float32 [2048, 8192], P('fsdp')
- grad_up_bias: float32 [8192], P('fsdp')
- grad_down_weight: float32 [8192, 2048], P('fsdp')
- grad_down_bias: float32 [2048], P('fsdp')
The draws below stay inside these ranges and needn't reach their ends.
All inputs are finite; a program needn't handle non-finite values.
Results may differ from the reference program's by a relative error of at most 0.0069.
Values may be sent and summed in bfloat16 or wider, within the bound.
No kernel may reach another device: no remote copies, remote signals or barrier semaphores. Data moves between devices by JAX's collectives and lax.ppermute only.
A program may use at most 704 MiB of HBM per device.

```python
import math
import jax
import jax.numpy as jnp
import numpy as np
from jax import lax

D = 2048
HEADS = 8
HEAD = 256
ROT = 64
FF = 8192
TOK_DEV = 256
BLOCKS = 32
TOKENS = 8192


def raised(drawn, key, source, target, blocks, factor):
    def block_of(axis_at):
        return (jnp.arange(drawn.shape[axis_at]) // (drawn.shape[axis_at] // blocks)).reshape((-1,) + (1,) * (drawn.ndim - 1 - axis_at))

    first = jax.random.permutation(key, blocks)[block_of(target)]
    second = (block_of(target) + blocks // 2) % blocks
    return jnp.where((block_of(source) == first) | (block_of(source) == second), factor * drawn, drawn)


def steps_of(rng, dims, shards, least, high):
    level = 1.0
    for dim, blocks in shards:
        draws = jax.random.uniform(jax.random.fold_in(jax.random.fold_in(rng, 6), dim), (blocks,), jnp.float32, least / len(shards), high / len(shards))
        level = level * jnp.repeat(jnp.exp(draws), dims[dim] // blocks).reshape((-1,) + (1,) * (len(dims) - 1 - dim))
    return level


def length_profile(amount, total, limit, lean):
    loads = [(1 << 20) // math.isqrt(standing ** lean) + 1 for standing in range(2, amount + 1)]
    spare, holding = total - limit - (amount - 1), [1] * (amount - 1)
    while spare > 0:
        free = [i for i in range(amount - 1) if holding[i] < limit]
        mass, budget = sum([loads[i] for i in free]), spare
        for i in free:
            extra = min(limit - holding[i], max(1, budget * loads[i] // mass), spare)
            holding[i] = holding[i] + extra
            spare = spare - extra
    return np.array([limit] + holding)


def ragged(stream_key, amount, total, most, skew):
    if amount == 2:
        one = jax.random.randint(stream_key, (), max(1, total - most), min(most, total - 1) + 1)
        return jnp.stack([one, total - one])
    lengths = jnp.asarray(length_profile(amount, total, most, skew), jnp.int32)
    couples = (amount - 1) // 2
    donor, sink = lengths[1:1 + 2 * couples:2], lengths[2:2 + 2 * couples:2]
    margin = jnp.minimum(donor - 1, most - sink)
    moved = jax.random.randint(jax.random.fold_in(stream_key, 1), (couples,), 0, 1 << 20) % (margin + 1)
    lengths = lengths.at[1:1 + 2 * couples:2].set(donor - moved).at[2:2 + 2 * couples:2].set(sink + moved)
    return lengths[jax.random.permutation(jax.random.fold_in(stream_key, 2), amount)]


def scatter_about(own_key, extent, deviation, bound, pieces=(), kind=jnp.bfloat16):
    factor_of = steps_of(own_key, extent, pieces, -0.22, 0.18) if pieces else 1.0
    drawn = jax.random.normal(own_key, extent, jnp.float32) * deviation * factor_of
    return jnp.minimum(jnp.maximum(drawn, -bound), bound).astype(kind)


def noise_with(own_key, shape, scale, reach, split, heavy, kind=jnp.bfloat16):
    entries = scale * jax.random.normal(own_key, shape, jnp.float32)
    if split:
        entries = entries * steps_of(own_key, shape, split, -0.22, 0.18)
    return jnp.clip(raised(entries, jax.random.fold_in(own_key, 3), *heavy), -reach, reach).astype(kind)


def setup_inputs(seed: int = 0) -> dict:
    streams_of = jax.random.split(jax.random.key(seed), 16)
    return {
        "inputs": noise_with(streams_of[0], (TOKENS, D), 1.0, 6.0, ((0, 32),), (0, 1, 32, 2.75)),
        "doc_ids": jax.vmap(lambda own: jnp.searchsorted(jnp.cumsum(ragged(own, TOK_DEV // 4, TOK_DEV, TOK_DEV // 2, 2)), jnp.arange(TOK_DEV), side="right"))(jax.random.split(streams_of[1], BLOCKS)).reshape((BLOCKS, TOK_DEV)).astype(jnp.int32),
        "attn_gain": jnp.clip(1.0 + 0.1 * jax.random.normal(streams_of[2], (D,), jnp.float32), 0.5, 1.5).astype(jnp.bfloat16),
        "attn_shift": scatter_about(streams_of[3], (D,), 0.2, 1.1953125, ((0, 32),)),
        "ffn_gain": jnp.clip(1.0 + 0.1 * jax.random.normal(streams_of[4], (D,), jnp.float32), 0.5, 1.5).astype(jnp.bfloat16),
        "ffn_shift": scatter_about(streams_of[5], (D,), 0.2, 1.1953125, ((0, 32),)),
        "qkv_weight": scatter_about(streams_of[6], (D, 3 * D), D ** -0.5, 0.125, ((0, 32),)),
        "qkv_bias": scatter_about(streams_of[7], (3 * D,), 0.2, 1.1953125, ((0, 32),)),
        "proj_weight": scatter_about(streams_of[8], (D, D), (D // 16) ** -0.5, 0.5, ((0, 32),)),
        "proj_bias": scatter_about(streams_of[9], (D,), 0.2, 1.1953125, ((0, 32),)),
        "up_weight": scatter_about(streams_of[10], (D, FF), D ** -0.5, 0.125, ((0, 32),)),
        "up_bias": scatter_about(streams_of[11], (FF,), 0.2, 1.1953125, ((0, 32),)),
        "down_weight": scatter_about(streams_of[12], (FF, D), (FF // 2) ** -0.5, 0.09375, ((0, 32),)),
        "down_bias": scatter_about(streams_of[13], (D,), 0.2, 1.1953125, ((0, 32),)),
        "cotangent": noise_with(streams_of[14], (TOKENS, D), 1.0, 6.0, ((0, 32),), (0, 1, 32, 2.75)),
    }


@jax.custom_vjp
def low(v):
    return lax.optimization_barrier(v.astype(jnp.bfloat16)).astype(jnp.float32)

@jax.custom_vjp
def low_back(v):
    return v

def low_keep(v):
    return (low(v), None)

def low_pass(kept, grad):
    return (grad,)

def back_keep(v):
    return (v, None)

def back_low(kept, grad):
    return (low(grad),)
low.defvjp(low_keep, low_pass)
low_back.defvjp(back_keep, back_low)
EPS = 1e-05
MASKED = -1e+30
HIGH = lax.Precision.HIGHEST

def norm(value, gain, shift):
    center = value - lax.optimization_barrier(jnp.mean(value, axis=-1, keepdims=True))
    spread = lax.optimization_barrier(jnp.mean(center * center, axis=-1, keepdims=True))
    return center * lax.rsqrt(spread + EPS) * gain + shift

def rotate(value, position):
    half = ROT // 2
    freq = 10000.0 ** (-2.0 * jnp.arange(half, dtype=jnp.float32) / ROT)
    angle = position.astype(jnp.float32)[:, None] * freq[None, :]
    cosine = jnp.cos(angle)[:, None, :]
    sine = jnp.sin(angle)[:, None, :]
    front = value[..., :half]
    back = value[..., half:ROT]
    return jnp.concatenate([front * cosine - back * sine, back * cosine + front * sine, value[..., ROT:]], axis=-1)

def layout(docs):
    index = jnp.arange(docs.shape[0], dtype=jnp.int32)
    same = docs[:, None] == docs[None, :]
    before = index[None, :] < index[:, None]
    position = lax.optimization_barrier(jnp.sum((same & before).astype(jnp.int32), axis=1)).astype(jnp.int32)
    allowed = same & (index[None, :] <= index[:, None])
    return (position, allowed)

def forward(value, docs, params):
    a_gain, a_shift, f_gain, f_shift, w_qkv, b_qkv, w_proj, b_proj, w_up, b_up, w_down, b_down = params
    count = value.shape[0]
    position, allowed = layout(docs)
    first = low(norm(value, a_gain, a_shift))
    second = low(norm(value, f_gain, f_shift))
    qkv = low_back(jnp.dot(first, w_qkv, precision=HIGH) + b_qkv)
    query = qkv[:, :D].reshape(count, HEADS, HEAD)
    keys = qkv[:, D:2 * D].reshape(count, HEADS, HEAD)
    values = qkv[:, 2 * D:].reshape(count, HEADS, HEAD)
    query = low(rotate(query, position))
    keys = low(rotate(keys, position))
    values = low(values)
    raw = low_back(jnp.einsum('thd,shd->hts', query, keys, precision=HIGH))
    scores = jnp.where(allowed[None], raw * HEAD ** (-0.5), MASKED)
    top = lax.optimization_barrier(jnp.max(scores, axis=-1, keepdims=True))
    expo = jnp.exp(scores - top)
    weights = low(expo / lax.optimization_barrier(jnp.sum(expo, axis=-1, keepdims=True)))
    mixed = jnp.einsum('hts,shd->thd', weights, values, precision=HIGH).reshape(count, D)
    mixed = low_back(low(mixed))
    up = low_back(jnp.dot(second, w_up, precision=HIGH) + b_up)
    act = low(jax.nn.gelu(up, approximate=False))
    attn_branch = jnp.dot(mixed, w_proj, precision=HIGH) + b_proj
    ffn_branch = jnp.dot(act, w_down, precision=HIGH) + b_down
    return value + attn_branch + ffn_branch

def reference(inputs, doc_ids, attn_gain, attn_shift, ffn_gain, ffn_shift, qkv_weight, qkv_bias, proj_weight, proj_bias, up_weight, up_bias, down_weight, down_bias, cotangent):
    params = tuple((p.astype(jnp.float32) for p in (attn_gain, attn_shift, ffn_gain, ffn_shift, qkv_weight, qkv_bias, proj_weight, proj_bias, up_weight, up_bias, down_weight, down_bias)))
    rows = inputs.astype(jnp.float32).reshape(BLOCKS, TOK_DEV, D)
    cots = cotangent.astype(jnp.float32).reshape(BLOCKS, TOK_DEV, D)

    def step(totals, block):
        value, docs, cot = block
        result, pull = jax.vjp(lambda a, b: forward(a, docs, b), value, params)
        grad_value, grad_params = pull(cot)
        totals = jax.tree.map(lambda s, t: s + t, totals, grad_params)
        return (totals, (result, grad_value))
    start = jax.tree.map(jnp.zeros_like, params)
    totals, (results, grads) = lax.scan(step, start, (rows, doc_ids, cots))
    return (results.reshape(TOKENS, D), grads.reshape(TOKENS, D), totals[0], totals[1], totals[2], totals[3], totals[4], totals[5], totals[6], totals[7], totals[8], totals[9], totals[10], totals[11])
```

```python
import functools

import jax
import jax.numpy as jnp
from jax import lax
from jax.experimental import pallas as pl
from jax.experimental.pallas import tpu as pltpu
from jax.sharding import PartitionSpec as P

HEADS = 8
HEAD = 256
ROT = 64
EPS = 1e-05
MASKED = -1e30
AXIS = "fsdp"
BF16 = jnp.bfloat16
F32 = jnp.float32

SPLIT_BITS = {32: (3, 2, 0), 128: (3, 1, 0)}


def attention_kernel(qkv_ref, turn_ref, docs_row_ref, docs_col_ref, d_mixed_ref, mixed_ref, d_qkv_ref, column_ref):
    half = ROT // 2
    cosine = turn_ref[0]
    sine = turn_ref[1]
    lanes = cosine.shape[1]
    lane = lax.broadcasted_iota(jnp.int32, cosine.shape, 1)

    def swap(v):
        return jnp.where(lane < half, pltpu.roll(v, lanes - half, 1), pltpu.roll(v, half, 1))

    def turn(v, sign):
        front = v[:, :lanes]
        front = front * cosine + sign * (swap(front) * sine)
        return jnp.concatenate([front, v[:, lanes:]], axis=1)

    rq = turn(qkv_ref[:, :HEAD], 1.0).astype(BF16)
    rk = turn(qkv_ref[:, HEAD : 2 * HEAD], 1.0).astype(BF16)
    rv = qkv_ref[:, 2 * HEAD :].astype(BF16)
    count = rq.shape[0]
    here = lax.broadcasted_iota(jnp.int32, (count, count), 0)
    there = lax.broadcasted_iota(jnp.int32, (count, count), 1)
    allowed = (docs_row_ref[0] == docs_col_ref[0]) & (there <= here)
    scale = HEAD ** (-0.5)
    rows = (((1,), (1,)), ((), ()))
    firsts = (((0,), (0,)), ((), ()))
    raw = lax.dot_general(rq, rk, rows, preferred_element_type=F32)
    scores = jnp.where(allowed, raw * scale, MASKED)
    expo = jnp.exp(scores - jnp.max(scores, axis=1, keepdims=True))
    probs = expo / jnp.sum(expo, axis=1, keepdims=True)
    weights = probs.astype(BF16)
    mixed_ref[...] = jnp.dot(weights, rv, preferred_element_type=F32).astype(BF16)
    d_mixed = d_mixed_ref[...]
    d_prob = lax.dot_general(d_mixed, rv, rows, preferred_element_type=F32)
    d_score = probs * (d_prob - jnp.sum(probs * d_prob, axis=1, keepdims=True))
    d_raw = (d_score * scale).astype(BF16)
    d_rq = jnp.dot(d_raw, rk, preferred_element_type=F32)
    d_rk = lax.dot_general(d_raw, rq, firsts, preferred_element_type=F32)
    d_rv = lax.dot_general(weights, d_mixed, firsts, preferred_element_type=F32)
    d_qkv = jnp.concatenate([turn(d_rq, -1.0), turn(d_rk, -1.0), d_rv], axis=1).astype(BF16)
    d_qkv_ref[...] = d_qkv

    @pl.when(pl.program_id(0) == 0)
    def _():
        column_ref[...] = jnp.zeros_like(column_ref)

    column_ref[...] += jnp.sum(d_qkv.astype(F32), axis=0, keepdims=True)


def attention(qkv, cosine, sine, docs, d_mixed):
    rows, count = docs.shape
    turns = jnp.stack([cosine, sine])
    lanes = turns.shape[2]
    return pl.pallas_call(
        attention_kernel,
        grid=(rows,),
        in_specs=[
            pl.BlockSpec((count, 3 * HEAD), lambda i: (i, 0)),
            pl.BlockSpec((2, count, lanes), lambda i: (0, i, 0)),
            pl.BlockSpec((1, 1, count), lambda i: (i, 0, 0)),
            pl.BlockSpec((1, count, 1), lambda i: (i, 0, 0)),
            pl.BlockSpec((count, HEAD), lambda i: (i, 0)),
        ],
        out_specs=[
            pl.BlockSpec((count, HEAD), lambda i: (i, 0)),
            pl.BlockSpec((count, 3 * HEAD), lambda i: (i, 0)),
            pl.BlockSpec((1, 3 * HEAD), lambda i: (0, 0)),
        ],
        out_shape=[
            jax.ShapeDtypeStruct((rows * count, HEAD), BF16),
            jax.ShapeDtypeStruct((rows * count, 3 * HEAD), BF16),
            jax.ShapeDtypeStruct((1, 3 * HEAD), F32),
        ],
        compiler_params=pltpu.CompilerParams(vmem_limit_bytes=32 * 1024 * 1024),
        cost_estimate=pl.CostEstimate(
            flops=16 * rows * count * count * HEAD, bytes_accessed=20 * rows * count * HEAD, transcendentals=rows * count * count
        ),
    )(qkv, turns, docs[:, None, :], docs[:, :, None], d_mixed)


def times_rows(left, right):
    return jnp.einsum("tc,nc->tn", left, right, preferred_element_type=F32)


def times_tokens(left, right):
    return jnp.einsum("tn,td->nd", left, right, preferred_element_type=F32)


class Layout:
    def __init__(self, count):
        self.count = count
        self.bits = count.bit_length() - 1
        self.h_bits = SPLIT_BITS.get(count, (2, 1, 0))
        self.t_bits = tuple(b for b in range(self.bits - 1, -1, -1) if b not in self.h_bits)
        head_bits = tuple(range(self.bits - 1, self.bits - 4, -1))
        self.swap = {b: b for b in range(self.bits)}
        for a, b in zip([a for a in head_bits if a not in self.h_bits], [b for b in self.h_bits if b not in head_bits]):
            self.swap[a], self.swap[b] = b, a
        self.groups = []
        for t in range(1 << len(self.t_bits)):
            base = sum(((t >> (len(self.t_bits) - 1 - i)) & 1) << b for i, b in enumerate(self.t_bits))
            self.groups.append(
                [base | sum(((h >> (2 - i)) & 1) << b for i, b in enumerate(self.h_bits)) for h in range(8)]
            )

    def swapped(self, device):
        return sum(((device >> b) & 1) << self.swap[b] for b in range(self.bits))

    def axis(self, bit):
        return self.bits - 1 - bit

    def flip(self, value, bit):
        return lax.ppermute(value, AXIS, [(d, d ^ (1 << bit)) for d in range(self.count)])

    def exchange_heads(self, value):
        return lax.ppermute(value, AXIS, [(d, self.swapped(d)) for d in range(self.count)])

    def mine(self, bit):
        return (lax.axis_index(AXIS) >> bit) & 1

    def gather(self, value):
        pieces = {0: value}
        for bit in self.t_bits:
            pieces.update({key | (1 << bit): self.flip(piece, bit) for key, piece in list(pieces.items())})
        return pieces

    def place(self, pieces, order, shape):
        some = pieces[0]
        whole = jnp.zeros(shape, some.dtype)
        block = tuple(1 if bit is not None else size for bit, size in zip(order, shape))
        block = block + shape[len(order) :]
        for key, piece in pieces.items():
            starts = [0 if bit is None else self.mine(bit) ^ ((key >> bit) & 1) for bit in order]
            starts = starts + [0] * (len(shape) - len(order))
            whole = lax.dynamic_update_slice(whole, piece.reshape(block), starts)
        return whole

    def reduce(self, part, order):
        order = list(order)
        for bit in reversed(self.t_bits):
            axis = order.index(bit)
            mine = self.mine(bit)
            away = lax.dynamic_index_in_dim(part, 1 - mine, axis, keepdims=False).astype(BF16)
            keep = lax.dynamic_index_in_dim(part, mine, axis, keepdims=False)
            part = keep + self.flip(away, bit).astype(F32)
            order.pop(axis)
        return part

    def gather_tokens(self, value):
        pieces = [value]
        for bit in self.h_bits[:-1]:
            pieces = pieces + [self.flip(piece, bit) for piece in pieces]
        own = jnp.concatenate(pieces, axis=0)
        return jnp.concatenate([own, self.flip(own, self.h_bits[-1])], axis=0)

    def reduce_tokens(self, part):
        for bit in reversed(self.h_bits):
            half = part.shape[0] // 2
            away = part[half:].astype(BF16)
            part = part[:half].astype(F32) + self.flip(away, bit).astype(F32)
        return part

    def to_columns(self, value):
        return lax.all_to_all(value, AXIS, split_axis=0, concat_axis=0, tiled=True, axis_index_groups=self.groups)


def local(
    inputs,
    doc_ids,
    attn_gain,
    attn_shift,
    ffn_gain,
    ffn_shift,
    qkv_weight,
    qkv_bias,
    proj_weight,
    proj_bias,
    up_weight,
    up_bias,
    down_weight,
    down_bias,
    cotangent,
):
    n = lax.axis_size(AXIS)
    lay = Layout(n)
    bits = lay.bits
    two = (2,) * bits
    count, width = inputs.shape
    rows = width // n
    unit = up_bias.shape[0]
    hidden = unit * (n // HEADS)
    h_axes = [lay.axis(b) for b in lay.h_bits]
    t_axes = [lay.axis(b) for b in lay.t_bits]

    small = jnp.concatenate(
        [
            attn_gain,
            attn_shift,
            ffn_gain,
            ffn_shift,
            proj_bias,
            down_bias,
            qkv_bias,
            up_bias,
            doc_ids[0].astype(BF16),
        ]
    )
    small = lax.all_to_all(
        jnp.broadcast_to(small[None], (n, small.shape[0])), AXIS, split_axis=0, concat_axis=0, tiled=True
    ).astype(F32)
    sizes = [rows] * 6 + [3 * rows, unit, count]
    vectors, at = [], 0
    for size in sizes:
        vectors.append(small[:, at : at + size])
        at += size
    a_gain, a_shift, f_gain, f_shift, b_proj, b_down = [v.reshape(1, width) for v in vectors[:6]]

    heads_at = [2 + (bits - 1 - lay.swap[b]) for b in lay.h_bits]
    up_cols = up_weight.reshape((rows,) + two + (unit,))
    up_cols = up_cols.transpose([1 + a for a in h_axes] + [0] + [1 + a for a in t_axes] + [bits + 1])
    up_cols = lay.to_columns(up_cols.reshape(HEADS, rows, hidden))
    qkv_cols = qkv_weight.reshape(rows, 3, 2, 2, 2, HEAD).transpose(heads_at + [0, 1, 5])
    qkv_cols = lay.to_columns(qkv_cols.reshape(HEADS, rows, 3 * HEAD))

    x = lay.gather_tokens(inputs)
    row_order = [b if b in lay.t_bits else None for b in range(bits - 1, -1, -1)]
    w_up = lay.place(lay.gather(up_cols), row_order, two + (rows, hidden)).reshape(width, hidden)
    g = lay.gather_tokens(cotangent)
    t_two = (2,) * len(lay.t_bits)
    w_down = lay.place(lay.gather(down_weight), lay.t_bits, t_two + (unit, width)).reshape(hidden, width)
    proj_order = [lay.swap[b] for b in range(bits - 4, -1, -1)]
    w_proj = lay.place(
        lay.gather(lay.exchange_heads(proj_weight)), proj_order, t_two + (rows, width)
    ).reshape(HEAD, width)
    w_qkv = lay.place(lay.gather(qkv_cols), row_order, two + (rows, 3 * HEAD)).reshape(width, 3 * HEAD)

    b_up = vectors[7].reshape(two + (unit,)).transpose(h_axes + t_axes + [bits]).reshape(HEADS, hidden)
    b_qkv = vectors[6].reshape((3, 2, 2, 2, HEAD)).transpose([a - 1 for a in heads_at] + [0, 4]).reshape(HEADS, 3 * HEAD)
    here = sum(lay.mine(b) << (2 - i) for i, b in enumerate(lay.h_bits))
    b_up = lax.dynamic_index_in_dim(b_up, here, 0, keepdims=True)
    b_qkv = lax.dynamic_index_in_dim(b_qkv, here, 0, keepdims=True)
    me = lax.axis_index(AXIS)
    docs = []
    for j in range(HEADS):
        other = me ^ sum(((j >> i) & 1) << b for i, b in enumerate(lay.h_bits))
        docs.append(lax.dynamic_index_in_dim(vectors[8], other, 0, keepdims=True))
    docs = jnp.concatenate(docs, axis=0).astype(jnp.int32)

    index = jnp.arange(count, dtype=jnp.int32)
    same = docs[:, :, None] == docs[:, None, :]
    position = jnp.sum((same & (index[None, None, :] < index[None, :, None])).astype(jnp.int32), axis=2).reshape(-1)
    freq = 10000.0 ** (-2.0 * jnp.arange(ROT // 2, dtype=F32) / ROT)
    angle = position.astype(F32)[:, None] * freq[None, :]
    cosine, sine = jnp.cos(angle), jnp.sin(angle)
    rest = 128 - ROT
    cosine = jnp.concatenate([cosine, cosine, jnp.ones((angle.shape[0], rest), F32)], axis=1)
    sine = jnp.concatenate([-sine, sine, jnp.zeros((angle.shape[0], rest), F32)], axis=1)

    value = x.astype(F32)
    center = value - jnp.mean(value, axis=-1, keepdims=True)
    scale = lax.rsqrt(jnp.mean(center * center, axis=-1, keepdims=True) + EPS)
    xhat = center * scale
    first = (xhat * a_gain + a_shift).astype(BF16)
    second = (xhat * f_gain + f_shift).astype(BF16)

    up = jnp.dot(second, w_up, preferred_element_type=F32) + b_up
    phi_sum = 0.5 * (1.0 + lax.erf(up * (0.5**0.5)))
    act = (up * phi_sum).astype(BF16)
    slope = phi_sum + up * jnp.exp(-0.5 * up * up) * 0.3989422804014327
    part_down = times_tokens(act, g)
    d_act = times_rows(g, w_down)
    d_up = (d_act * slope).astype(BF16)
    part_up = times_tokens(second, d_up)
    d_second = times_rows(d_up, w_up)

    d_mixed = times_rows(g, w_proj).astype(BF16)
    qkv = jnp.dot(first, w_qkv, preferred_element_type=F32) + b_qkv
    mixed, d_qkv, column_qkv = attention(qkv, cosine, sine, docs, d_mixed)
    part_proj = times_tokens(mixed, g)
    part_qkv = times_tokens(first, d_qkv)
    d_first = times_rows(d_qkv, w_qkv)

    branches = jnp.dot(act, w_down, preferred_element_type=F32) + jnp.dot(mixed, w_proj, preferred_element_type=F32)
    value_own = inputs.astype(F32)
    layer_out = lay.reduce_tokens(branches) + value_own + b_proj + b_down

    edge = lay.reduce_tokens(d_first * a_gain + d_second * f_gain)
    center_own = value_own - jnp.mean(value_own, axis=-1, keepdims=True)
    scale_own = lax.rsqrt(jnp.mean(center_own * center_own, axis=-1, keepdims=True) + EPS)
    xhat_own = center_own * scale_own
    back = edge - jnp.mean(edge, axis=-1, keepdims=True) - xhat_own * jnp.mean(edge * xhat_own, axis=-1, keepdims=True)
    grad_inputs = cotangent.astype(F32) + back * scale_own

    grad_down = lay.reduce(part_down.reshape(t_two + (unit, width)), lay.t_bits)
    grad_proj = lay.reduce(part_proj.reshape(t_two + (rows, width)), proj_order)
    grad_proj = lay.exchange_heads(grad_proj.astype(BF16)).astype(F32)
    grad_up = lay.reduce(part_up.reshape(two + (rows, hidden)), row_order).reshape(HEADS, rows, hidden)
    grad_up = lay.to_columns(grad_up.astype(BF16)).astype(F32)
    axes = h_axes + t_axes
    grad_up = grad_up.reshape((2, 2, 2, rows) + t_two + (unit,))
    back_axes = [3] + [
        (axes.index(a) if axes.index(a) < 3 else axes.index(a) + 1) for a in range(bits)
    ] + [bits + 1]
    grad_up = grad_up.transpose(back_axes).reshape(rows, -1)
    grad_qkv = lay.reduce(part_qkv.reshape(two + (rows, 3 * HEAD)), row_order).reshape(HEADS, rows, 3 * HEAD)
    grad_qkv = lay.to_columns(grad_qkv.astype(BF16)).astype(F32)
    grad_qkv = grad_qkv.reshape(2, 2, 2, rows, 3, HEAD)
    grad_qkv = grad_qkv.transpose([3, 4] + [heads_at.index(a) for a in (2, 3, 4)] + [5]).reshape(rows, -1)

    column_up = jnp.sum(d_up.astype(F32), axis=0)
    column_out = jnp.sum(cotangent.astype(F32), axis=0)
    spread_up = lax.dynamic_update_slice(jnp.zeros((HEADS, hidden), F32), column_up[None], (here, 0))
    spread_up = spread_up.reshape((2,) * bits + (unit,)).transpose(
        [(axes.index(a)) for a in range(bits)] + [bits]
    )
    spread_qkv = lax.dynamic_update_slice(jnp.zeros((HEADS, 3 * HEAD), F32), column_qkv, (here, 0))
    spread_qkv = spread_qkv.reshape(2, 2, 2, 3, HEAD).transpose([3] + [heads_at.index(a) for a in (2, 3, 4)] + [4])
    sums = [
        jnp.sum(d_first * xhat, axis=0),
        jnp.sum(d_first, axis=0),
        jnp.sum(d_second * xhat, axis=0),
        jnp.sum(d_second, axis=0),
        column_out,
        spread_qkv,
        spread_up,
    ]
    sums = jnp.concatenate([s.reshape(n, -1) for s in sums], axis=1)
    sums = jnp.sum(lax.all_to_all(sums, AXIS, split_axis=0, concat_axis=0, tiled=True), axis=0)
    got, at = [], 0
    for size in [rows] * 5 + [3 * rows, unit]:
        got.append(sums[at : at + size])
        at += size
    return (
        layer_out,
        grad_inputs,
        got[0],
        got[1],
        got[2],
        got[3],
        grad_qkv,
        got[5],
        grad_proj,
        got[4],
        grad_up,
        got[6],
        grad_down,
        got[4],
    )


def solution(mesh):
    tokens, rows = P(AXIS, None), P(AXIS)
    return jax.shard_map(
        local,
        mesh=mesh,
        in_specs=(tokens, tokens, rows, rows, rows, rows, tokens, rows, tokens, rows, tokens, rows, tokens, rows, tokens),
        out_specs=(tokens, tokens, rows, rows, rows, rows, tokens, rows, tokens, rows, tokens, rows, tokens, rows),
        check_vma=False,
    )
```

```python
import functools

import jax
import jax.numpy as jnp
import numpy as np
from jax import lax
from jax.experimental import pallas as pl
from jax.experimental.pallas import tpu as pltpu
from jax.sharding import PartitionSpec as P

HEADS = 8
HEAD = 256
ROT = 64
EPS = 1e-05
MASKED = -1e30
AXIS = "fsdp"
BF16 = jnp.bfloat16
F32 = jnp.float32

SPLIT_BITS = {32: (3, 2, 0), 128: (3, 1, 0)}


def attention_kernel(qkv_ref, turn_ref, docs_row_ref, docs_col_ref, d_mixed_ref, mixed_ref, d_qkv_ref, column_ref):
    half = ROT // 2
    cosine = turn_ref[0]
    sine = turn_ref[1]
    lanes = cosine.shape[1]
    lane = lax.broadcasted_iota(jnp.int32, cosine.shape, 1)

    def swap(v):
        return jnp.where(lane < half, pltpu.roll(v, lanes - half, 1), pltpu.roll(v, half, 1))

    def turn(v, sign):
        front = v[:, :lanes]
        front = front * cosine + sign * (swap(front) * sine)
        return jnp.concatenate([front, v[:, lanes:]], axis=1)

    rq = turn(qkv_ref[:, :HEAD], 1.0).astype(BF16)
    rk = turn(qkv_ref[:, HEAD : 2 * HEAD], 1.0).astype(BF16)
    rv = qkv_ref[:, 2 * HEAD :].astype(BF16)
    count = rq.shape[0]
    here = lax.broadcasted_iota(jnp.int32, (count, count), 0)
    there = lax.broadcasted_iota(jnp.int32, (count, count), 1)
    allowed = (docs_row_ref[0] == docs_col_ref[0]) & (there <= here)
    scale = HEAD ** (-0.5)
    rows = (((1,), (1,)), ((), ()))
    firsts = (((0,), (0,)), ((), ()))
    raw = lax.dot_general(rq, rk, rows, preferred_element_type=F32)
    scores = jnp.where(allowed, raw * scale, MASKED)
    expo = jnp.exp(scores - jnp.max(scores, axis=1, keepdims=True))
    probs = expo / jnp.sum(expo, axis=1, keepdims=True)
    weights = probs.astype(BF16)
    mixed_ref[...] = jnp.dot(weights, rv, preferred_element_type=F32).astype(BF16)
    d_mixed = d_mixed_ref[...]
    d_prob = lax.dot_general(d_mixed, rv, rows, preferred_element_type=F32)
    d_score = probs * (d_prob - jnp.sum(probs * d_prob, axis=1, keepdims=True))
    d_raw = (d_score * scale).astype(BF16)
    d_rq = jnp.dot(d_raw, rk, preferred_element_type=F32)
    d_rk = lax.dot_general(d_raw, rq, firsts, preferred_element_type=F32)
    d_rv = lax.dot_general(weights, d_mixed, firsts, preferred_element_type=F32)
    d_qkv = jnp.concatenate([turn(d_rq, -1.0), turn(d_rk, -1.0), d_rv], axis=1).astype(BF16)
    d_qkv_ref[...] = d_qkv

    @pl.when(pl.program_id(0) == 0)
    def _():
        column_ref[...] = jnp.zeros_like(column_ref)

    column_ref[...] += jnp.sum(d_qkv.astype(F32), axis=0, keepdims=True)


def attention(qkv, cosine, sine, docs, d_mixed):
    rows, count = docs.shape
    turns = jnp.stack([cosine, sine])
    lanes = turns.shape[2]
    return pl.pallas_call(
        attention_kernel,
        grid=(rows,),
        in_specs=[
            pl.BlockSpec((count, 3 * HEAD), lambda i: (i, 0)),
            pl.BlockSpec((2, count, lanes), lambda i: (0, i, 0)),
            pl.BlockSpec((1, 1, count), lambda i: (i, 0, 0)),
            pl.BlockSpec((1, count, 1), lambda i: (i, 0, 0)),
            pl.BlockSpec((count, HEAD), lambda i: (i, 0)),
        ],
        out_specs=[
            pl.BlockSpec((count, HEAD), lambda i: (i, 0)),
            pl.BlockSpec((count, 3 * HEAD), lambda i: (i, 0)),
            pl.BlockSpec((1, 3 * HEAD), lambda i: (0, 0)),
        ],
        out_shape=[
            jax.ShapeDtypeStruct((rows * count, HEAD), BF16),
            jax.ShapeDtypeStruct((rows * count, 3 * HEAD), BF16),
            jax.ShapeDtypeStruct((1, 3 * HEAD), F32),
        ],
        compiler_params=pltpu.CompilerParams(vmem_limit_bytes=32 * 1024 * 1024),
        cost_estimate=pl.CostEstimate(
            flops=16 * rows * count * count * HEAD, bytes_accessed=20 * rows * count * HEAD, transcendentals=rows * count * count
        ),
    )(qkv, turns, docs[:, None, :], docs[:, :, None], d_mixed)


def times_rows(left, right):
    return jnp.einsum("tc,nc->tn", left, right, preferred_element_type=F32)


def times_tokens(left, right):
    return jnp.einsum("tn,td->nd", left, right, preferred_element_type=F32)


class Layout:
    def __init__(self, count):
        self.count = count
        self.bits = count.bit_length() - 1
        self.h_bits = SPLIT_BITS.get(count, (2, 1, 0))
        self.t_bits = tuple(b for b in range(self.bits - 1, -1, -1) if b not in self.h_bits)
        head_bits = tuple(range(self.bits - 1, self.bits - 4, -1))
        self.swap = {b: b for b in range(self.bits)}
        for a, b in zip([a for a in head_bits if a not in self.h_bits], [b for b in self.h_bits if b not in head_bits]):
            self.swap[a], self.swap[b] = b, a
        self.groups = []
        for t in range(1 << len(self.t_bits)):
            base = sum(((t >> (len(self.t_bits) - 1 - i)) & 1) << b for i, b in enumerate(self.t_bits))
            self.groups.append(
                [base | sum(((h >> (2 - i)) & 1) << b for i, b in enumerate(self.h_bits)) for h in range(8)]
            )

    def swapped(self, device):
        return sum(((device >> b) & 1) << self.swap[b] for b in range(self.bits))

    def axis(self, bit):
        return self.bits - 1 - bit

    def flip(self, value, bit):
        return lax.ppermute(value, AXIS, [(d, d ^ (1 << bit)) for d in range(self.count)])

    def exchange_heads(self, value):
        return lax.ppermute(value, AXIS, [(d, self.swapped(d)) for d in range(self.count)])

    def mine(self, bit):
        return (lax.axis_index(AXIS) >> bit) & 1

    def gather(self, value):
        pieces = {0: value}
        for bit in self.t_bits:
            pieces.update({key | (1 << bit): self.flip(piece, bit) for key, piece in list(pieces.items())})
        return pieces

    def place(self, pieces, order, shape):
        some = pieces[0]
        whole = jnp.zeros(shape, some.dtype)
        block = tuple(1 if bit is not None else size for bit, size in zip(order, shape))
        block = block + shape[len(order) :]
        for key, piece in pieces.items():
            starts = [0 if bit is None else self.mine(bit) ^ ((key >> bit) & 1) for bit in order]
            starts = starts + [0] * (len(shape) - len(order))
            whole = lax.dynamic_update_slice(whole, piece.reshape(block), starts)
        return whole

    def reduce(self, part, order):
        order = list(order)
        for bit in reversed(self.t_bits):
            axis = order.index(bit)
            mine = self.mine(bit)
            away = lax.dynamic_index_in_dim(part, 1 - mine, axis, keepdims=False).astype(BF16)
            keep = lax.dynamic_index_in_dim(part, mine, axis, keepdims=False)
            part = keep + self.flip(away, bit).astype(F32)
            order.pop(axis)
        return part

    def gather_tokens(self, value):
        pieces = [value]
        for bit in self.h_bits[:-1]:
            pieces = pieces + [self.flip(piece, bit) for piece in pieces]
        own = jnp.concatenate(pieces, axis=0)
        return jnp.concatenate([own, self.flip(own, self.h_bits[-1])], axis=0)

    def reduce_tokens(self, part):
        for bit in reversed(self.h_bits):
            half = part.shape[0] // 2
            away = part[half:].astype(BF16)
            part = part[:half].astype(F32) + self.flip(away, bit).astype(F32)
        return part

    def to_columns(self, value):
        return lax.all_to_all(value, AXIS, split_axis=0, concat_axis=0, tiled=True, axis_index_groups=self.groups)


def local_any(
    inputs,
    doc_ids,
    attn_gain,
    attn_shift,
    ffn_gain,
    ffn_shift,
    qkv_weight,
    qkv_bias,
    proj_weight,
    proj_bias,
    up_weight,
    up_bias,
    down_weight,
    down_bias,
    cotangent,
):
    n = lax.axis_size(AXIS)
    lay = Layout(n)
    bits = lay.bits
    two = (2,) * bits
    count, width = inputs.shape
    rows = width // n
    unit = up_bias.shape[0]
    hidden = unit * (n // HEADS)
    h_axes = [lay.axis(b) for b in lay.h_bits]
    t_axes = [lay.axis(b) for b in lay.t_bits]

    small = jnp.concatenate(
        [
            attn_gain,
            attn_shift,
            ffn_gain,
            ffn_shift,
            proj_bias,
            down_bias,
            qkv_bias,
            up_bias,
            doc_ids[0].astype(BF16),
        ]
    )
    small = lax.all_to_all(
        jnp.broadcast_to(small[None], (n, small.shape[0])), AXIS, split_axis=0, concat_axis=0, tiled=True
    ).astype(F32)
    sizes = [rows] * 6 + [3 * rows, unit, count]
    vectors, at = [], 0
    for size in sizes:
        vectors.append(small[:, at : at + size])
        at += size
    a_gain, a_shift, f_gain, f_shift, b_proj, b_down = [v.reshape(1, width) for v in vectors[:6]]

    heads_at = [2 + (bits - 1 - lay.swap[b]) for b in lay.h_bits]
    up_cols = up_weight.reshape((rows,) + two + (unit,))
    up_cols = up_cols.transpose([1 + a for a in h_axes] + [0] + [1 + a for a in t_axes] + [bits + 1])
    up_cols = lay.to_columns(up_cols.reshape(HEADS, rows, hidden))
    qkv_cols = qkv_weight.reshape(rows, 3, 2, 2, 2, HEAD).transpose(heads_at + [0, 1, 5])
    qkv_cols = lay.to_columns(qkv_cols.reshape(HEADS, rows, 3 * HEAD))

    x = lay.gather_tokens(inputs)
    row_order = [b if b in lay.t_bits else None for b in range(bits - 1, -1, -1)]
    w_up = lay.place(lay.gather(up_cols), row_order, two + (rows, hidden)).reshape(width, hidden)
    g = lay.gather_tokens(cotangent)
    t_two = (2,) * len(lay.t_bits)
    w_down = lay.place(lay.gather(down_weight), lay.t_bits, t_two + (unit, width)).reshape(hidden, width)
    proj_order = [lay.swap[b] for b in range(bits - 4, -1, -1)]
    w_proj = lay.place(
        lay.gather(lay.exchange_heads(proj_weight)), proj_order, t_two + (rows, width)
    ).reshape(HEAD, width)
    w_qkv = lay.place(lay.gather(qkv_cols), row_order, two + (rows, 3 * HEAD)).reshape(width, 3 * HEAD)

    b_up = vectors[7].reshape(two + (unit,)).transpose(h_axes + t_axes + [bits]).reshape(HEADS, hidden)
    b_qkv = vectors[6].reshape((3, 2, 2, 2, HEAD)).transpose([a - 1 for a in heads_at] + [0, 4]).reshape(HEADS, 3 * HEAD)
    here = sum(lay.mine(b) << (2 - i) for i, b in enumerate(lay.h_bits))
    b_up = lax.dynamic_index_in_dim(b_up, here, 0, keepdims=True)
    b_qkv = lax.dynamic_index_in_dim(b_qkv, here, 0, keepdims=True)
    me = lax.axis_index(AXIS)
    docs = []
    for j in range(HEADS):
        other = me ^ sum(((j >> i) & 1) << b for i, b in enumerate(lay.h_bits))
        docs.append(lax.dynamic_index_in_dim(vectors[8], other, 0, keepdims=True))
    docs = jnp.concatenate(docs, axis=0).astype(jnp.int32)

    index = jnp.arange(count, dtype=jnp.int32)
    same = docs[:, :, None] == docs[:, None, :]
    position = jnp.sum((same & (index[None, None, :] < index[None, :, None])).astype(jnp.int32), axis=2).reshape(-1)
    freq = 10000.0 ** (-2.0 * jnp.arange(ROT // 2, dtype=F32) / ROT)
    angle = position.astype(F32)[:, None] * freq[None, :]
    cosine, sine = jnp.cos(angle), jnp.sin(angle)
    rest = 128 - ROT
    cosine = jnp.concatenate([cosine, cosine, jnp.ones((angle.shape[0], rest), F32)], axis=1)
    sine = jnp.concatenate([-sine, sine, jnp.zeros((angle.shape[0], rest), F32)], axis=1)

    value = x.astype(F32)
    center = value - jnp.mean(value, axis=-1, keepdims=True)
    scale = lax.rsqrt(jnp.mean(center * center, axis=-1, keepdims=True) + EPS)
    xhat = center * scale
    first = (xhat * a_gain + a_shift).astype(BF16)
    second = (xhat * f_gain + f_shift).astype(BF16)

    up = jnp.dot(second, w_up, preferred_element_type=F32) + b_up
    phi_sum = 0.5 * (1.0 + lax.erf(up * (0.5**0.5)))
    act = (up * phi_sum).astype(BF16)
    slope = phi_sum + up * jnp.exp(-0.5 * up * up) * 0.3989422804014327
    part_down = times_tokens(act, g)
    d_act = times_rows(g, w_down)
    d_up = (d_act * slope).astype(BF16)
    part_up = times_tokens(second, d_up)
    d_second = times_rows(d_up, w_up)

    d_mixed = times_rows(g, w_proj).astype(BF16)
    qkv = jnp.dot(first, w_qkv, preferred_element_type=F32) + b_qkv
    mixed, d_qkv, column_qkv = attention(qkv, cosine, sine, docs, d_mixed)
    part_proj = times_tokens(mixed, g)
    part_qkv = times_tokens(first, d_qkv)
    d_first = times_rows(d_qkv, w_qkv)

    branches = jnp.dot(act, w_down, preferred_element_type=F32) + jnp.dot(mixed, w_proj, preferred_element_type=F32)
    value_own = inputs.astype(F32)
    layer_out = lay.reduce_tokens(branches) + value_own + b_proj + b_down

    edge = lay.reduce_tokens(d_first * a_gain + d_second * f_gain)
    center_own = value_own - jnp.mean(value_own, axis=-1, keepdims=True)
    scale_own = lax.rsqrt(jnp.mean(center_own * center_own, axis=-1, keepdims=True) + EPS)
    xhat_own = center_own * scale_own
    back = edge - jnp.mean(edge, axis=-1, keepdims=True) - xhat_own * jnp.mean(edge * xhat_own, axis=-1, keepdims=True)
    grad_inputs = cotangent.astype(F32) + back * scale_own

    grad_down = lay.reduce(part_down.reshape(t_two + (unit, width)), lay.t_bits)
    grad_proj = lay.reduce(part_proj.reshape(t_two + (rows, width)), proj_order)
    grad_proj = lay.exchange_heads(grad_proj.astype(BF16)).astype(F32)
    grad_up = lay.reduce(part_up.reshape(two + (rows, hidden)), row_order).reshape(HEADS, rows, hidden)
    grad_up = lay.to_columns(grad_up.astype(BF16)).astype(F32)
    axes = h_axes + t_axes
    grad_up = grad_up.reshape((2, 2, 2, rows) + t_two + (unit,))
    back_axes = [3] + [
        (axes.index(a) if axes.index(a) < 3 else axes.index(a) + 1) for a in range(bits)
    ] + [bits + 1]
    grad_up = grad_up.transpose(back_axes).reshape(rows, -1)
    grad_qkv = lay.reduce(part_qkv.reshape(two + (rows, 3 * HEAD)), row_order).reshape(HEADS, rows, 3 * HEAD)
    grad_qkv = lay.to_columns(grad_qkv.astype(BF16)).astype(F32)
    grad_qkv = grad_qkv.reshape(2, 2, 2, rows, 3, HEAD)
    grad_qkv = grad_qkv.transpose([3, 4] + [heads_at.index(a) for a in (2, 3, 4)] + [5]).reshape(rows, -1)

    column_up = jnp.sum(d_up.astype(F32), axis=0)
    column_out = jnp.sum(cotangent.astype(F32), axis=0)
    spread_up = lax.dynamic_update_slice(jnp.zeros((HEADS, hidden), F32), column_up[None], (here, 0))
    spread_up = spread_up.reshape((2,) * bits + (unit,)).transpose(
        [(axes.index(a)) for a in range(bits)] + [bits]
    )
    spread_qkv = lax.dynamic_update_slice(jnp.zeros((HEADS, 3 * HEAD), F32), column_qkv, (here, 0))
    spread_qkv = spread_qkv.reshape(2, 2, 2, 3, HEAD).transpose([3] + [heads_at.index(a) for a in (2, 3, 4)] + [4])
    sums = [
        jnp.sum(d_first * xhat, axis=0),
        jnp.sum(d_first, axis=0),
        jnp.sum(d_second * xhat, axis=0),
        jnp.sum(d_second, axis=0),
        column_out,
        spread_qkv,
        spread_up,
    ]
    sums = jnp.concatenate([s.reshape(n, -1) for s in sums], axis=1)
    sums = jnp.sum(lax.all_to_all(sums, AXIS, split_axis=0, concat_axis=0, tiled=True), axis=0)
    got, at = [], 0
    for size in [rows] * 5 + [3 * rows, unit]:
        got.append(sums[at : at + size])
        at += size
    return (
        layer_out,
        grad_inputs,
        got[0],
        got[1],
        got[2],
        got[3],
        grad_qkv,
        got[5],
        grad_proj,
        got[4],
        grad_up,
        got[6],
        grad_down,
        got[4],
    )


ZH, ZL, Y, X, CORE = 4, 3, 2, 1, 0
ROWS = (((1,), (1,)), ((), ()))
COST = 0.45e9
FIRSTS = (((0,), (0,)), ((), ()))


def after(values, *done):
    return lax.optimization_barrier(tuple(values) + done)[: len(values)]


def flip(value, bit):
    return lax.ppermute(value, AXIS, [(d, d ^ (1 << bit)) for d in range(lax.axis_size(AXIS))])


def call(body, grid, in_specs, out_specs, out_shape, args, scalars=None, limit=40, us=1.0, aliases=None):
    extra = dict(
        out_shape=out_shape,
        compiler_params=pltpu.CompilerParams(vmem_limit_bytes=limit * 1024 * 1024),
        cost_estimate=pl.CostEstimate(flops=int(us * COST), bytes_accessed=1024, transcendentals=0),
        input_output_aliases=aliases or {},
    )
    if scalars is None:
        return pl.pallas_call(body, grid=grid, in_specs=in_specs, out_specs=out_specs, **extra)(*args)
    spec = pltpu.PrefetchScalarGridSpec(num_scalar_prefetch=1, grid=grid, in_specs=in_specs, out_specs=out_specs)
    return pl.pallas_call(body, grid_spec=spec, **extra)(scalars, *args)


def shape(dims, dtype):
    return jax.ShapeDtypeStruct(dims, dtype)


def bits_of(number, count):
    return [(number >> (count - 1 - i)) & 1 for i in range(count)]


def order_columns(value, mine):
    count, width = value.shape
    wide = width // 16

    def body(mine_ref, x_ref, o_ref):
        for j in range(16):
            xr, zr, b, c = bits_of(j, 4)
            source = (zr ^ mine_ref[0]) * 8 + b * 4 + c * 2 + (xr ^ mine_ref[1])
            o_ref[:, j * wide : (j + 1) * wide] = x_ref[:, pl.ds(pl.multiple_of(source * wide, wide), wide)]

    block = pl.BlockSpec((count, width), lambda i, s: (0, 0))
    return call(body, (1,), [block], block, shape((count, width), value.dtype), (value,), mine)


def split_columns(up_weight, qkv_weight):
    rows, ff = up_weight.shape
    unit = ff // 32
    hidden = 4 * unit

    def body(u_ref, q_ref, o_ref):
        for h in range(8):
            zl, y, c = bits_of(h, 3)
            for t in range(4):
                zh, x = bits_of(t, 2)
                e = zh * 16 + zl * 8 + y * 4 + x * 2 + c
                o_ref[h, :, t * unit : (t + 1) * unit] = u_ref[:, e * unit : (e + 1) * unit]
            head = c * 4 + zl * 2 + y
            for k in range(3):
                at = (k * HEADS + head) * HEAD
                o_ref[h, :, hidden + k * HEAD : hidden + (k + 1) * HEAD] = q_ref[:, at : at + HEAD]

    def block(*dims):
        return pl.BlockSpec(dims, lambda i: (0,) * len(dims))

    return call(
        body,
        (1,),
        [block(rows, ff), block(rows, 3 * HEADS * HEAD)],
        block(8, rows, hidden + 3 * HEAD),
        shape((8, rows, hidden + 3 * HEAD), BF16),
        (up_weight, qkv_weight),
    )


def join_up(parts):
    _, rows, hidden = parts.shape
    unit = hidden // 4

    def body(p_ref, o_ref):
        for h in range(8):
            zl, y, c = bits_of(h, 3)
            for t in range(4):
                zh, x = bits_of(t, 2)
                e = zh * 16 + zl * 8 + y * 4 + x * 2 + c
                o_ref[:, e * unit : (e + 1) * unit] = p_ref[h, :, t * unit : (t + 1) * unit].astype(F32)

    return call(
        body,
        (1,),
        [pl.BlockSpec(parts.shape, lambda i: (0, 0, 0))],
        pl.BlockSpec((rows, 8 * hidden), lambda i: (0, 0)),
        shape((rows, 8 * hidden), F32),
        (parts,),
    )


def join_qkv(parts):
    _, rows, _ = parts.shape

    def body(p_ref, o_ref):
        for h in range(8):
            zl, y, c = bits_of(h, 3)
            head = c * 4 + zl * 2 + y
            for k in range(3):
                at = (k * HEADS + head) * HEAD
                o_ref[:, at : at + HEAD] = p_ref[h, :, k * HEAD : (k + 1) * HEAD].astype(F32)

    return call(
        body,
        (1,),
        [pl.BlockSpec(parts.shape, lambda i: (0, 0, 0))],
        pl.BlockSpec((rows, 3 * HEADS * HEAD), lambda i: (0, 0)),
        shape((rows, 3 * HEADS * HEAD), F32),
        (parts,),
    )


def prepare(small, place, freq, sign, rows, unit, count):
    n, _, lanes = small.shape
    width = n * rows
    up_at, gains_at = count // lanes, (count + unit) // lanes
    out_at = gains_at + 2
    qkv_at = out_at + 1

    def body(place_ref, small_ref, f_ref, s_ref, gains_ref, out_ref, up_ref, qkv_ref, docs_ref, cos_ref, sin_ref, all_ref):
        mzh, mx, mzl, my, mc, me = [place_ref[k] for k in range(6)]
        step = pl.program_id(0)

        @pl.when(step == 0)
        def _():
            all_ref[...] = small_ref[...].astype(F32)
            gains_ref[...] = jnp.zeros_like(gains_ref)

            for j in range(16):
                xr, zr, b, c = bits_of(j, 4)
                source = 2 * ((zr ^ mzh) * 8 + b * 4 + c * 2 + (xr ^ mx))
                here = slice(2 * j * rows, 2 * (j + 1) * rows)
                left, right = all_ref[source], all_ref[source + 1]
                for k in range(4):
                    at, part = gains_at + k // 2, slice(k % 2 * rows, (k % 2 + 1) * rows)
                    gains_ref[k : k + 1, here] = jnp.concatenate([left[at : at + 1, part], right[at : at + 1, part]], axis=1)
                left, right = [v[:, :rows] + v[:, rows:] for v in (all_ref[2 * j, out_at : out_at + 1], all_ref[2 * j + 1, out_at : out_at + 1])]
                out_ref[:, here] = jnp.concatenate([left, right], axis=1)
            for t in range(4):
                zh, x = bits_of(t, 2)
                device = zh * 16 + mzl * 8 + my * 4 + x * 2 + mc
                mine_up = all_ref[device]
                for k in range(unit // lanes):
                    up_ref[:, t * unit + k * lanes : t * unit + (k + 1) * lanes] = mine_up[up_at + k : up_at + k + 1]
            head = mc * 4 + mzl * 2 + my
            for k in range(3 * HEAD // rows):
                chunk = (k // (HEAD // rows) * HEADS + head) * (HEAD // rows) + k % (HEAD // rows)
                third = all_ref[chunk // 3]
                part = lax.rem(chunk, 3)
                first, last = third[qkv_at : qkv_at + 1], third[qkv_at + 1 : qkv_at + 2]
                qkv_ref[:, k * rows : (k + 1) * rows] = jnp.where(
                    part == 0, first[:, :rows], jnp.where(part == 1, first[:, rows:], last[:, :rows])
                )

        other = me ^ (((step & 1) << ZL) | (((step >> 1) & 1) << Y) | (((step >> 2) & 1) << CORE))
        held = all_ref[other]
        docs = jnp.concatenate([held[k : k + 1] for k in range(count // lanes)], axis=1)
        docs_ref[0] = docs
        across = jnp.broadcast_to(docs, (count, count))
        here = lax.broadcasted_iota(jnp.int32, (count, count), 0)
        there = lax.broadcasted_iota(jnp.int32, (count, count), 1)
        earlier = (across == across.T) & (there < here)
        position = jnp.sum(earlier.astype(F32), axis=1, keepdims=True)
        angle = position * f_ref[...]
        cos_ref[...] = jnp.cos(angle)
        sin_ref[...] = jnp.sin(angle) * s_ref[...]

    def whole(*dims):
        return pl.BlockSpec(dims, lambda i, s: (0, 0))

    block = pl.BlockSpec((count, lanes), lambda i, s: (i, 0))
    return pl.pallas_call(
        body,
        grid_spec=pltpu.PrefetchScalarGridSpec(
            num_scalar_prefetch=1,
            grid=(8,),
            in_specs=[pl.BlockSpec(small.shape, lambda i, s: (0, 0, 0)), whole(1, lanes), whole(1, lanes)],
            out_specs=[
                whole(8, width),
                whole(1, width),
                whole(1, 4 * unit),
                whole(1, 3 * HEAD),
                pl.BlockSpec((1, 1, count), lambda i, s: (i, 0, 0)),
                block,
                block,
            ],
            scratch_shapes=[pltpu.VMEM(small.shape, F32)],
        ),
        out_shape=[
            shape((8, width), F32),
            shape((1, width), F32),
            shape((1, 4 * unit), F32),
            shape((1, 3 * HEAD), F32),
            shape((8, 1, count), F32),
            shape((8 * count, lanes), F32),
            shape((8 * count, lanes), F32),
        ],
        compiler_params=pltpu.CompilerParams(vmem_limit_bytes=40 * 1024 * 1024),
        cost_estimate=pl.CostEstimate(flops=int(COST), bytes_accessed=1024, transcendentals=0),
    )(place, small, freq, sign)


def join(pieces):
    count, width = pieces[0].shape
    blocks = len(pieces)

    def body(*refs):
        ins, out, held, sems_in, sems_out = refs[:blocks], refs[blocks], *refs[blocks + 1 :]

        def copy_in(k):
            return pltpu.make_async_copy(ins[k], held.at[k], sems_in.at[k])

        def copy_out(k):
            return pltpu.make_async_copy(held.at[k], out.at[pl.ds(k * count, count)], sems_out.at[k])

        for k in range(blocks):
            copy_in(k).start()
        for k in range(blocks):
            copy_in(k).wait()
            copy_out(k).start()
        for k in range(blocks):
            copy_out(k).wait()

    some = pl.BlockSpec(memory_space=pl.ANY)
    return pl.pallas_call(
        body,
        grid=(1,),
        in_specs=[some] * blocks,
        out_specs=some,
        out_shape=shape((blocks * count, width), pieces[0].dtype),
        scratch_shapes=[pltpu.VMEM((blocks, count, width), pieces[0].dtype)] + [pltpu.SemaphoreType.DMA((blocks,))] * 2,
        compiler_params=pltpu.CompilerParams(vmem_limit_bytes=40 * 1024 * 1024),
        cost_estimate=pl.CostEstimate(flops=int(4 * COST), bytes_accessed=1024, transcendentals=0),
    )(*pieces)


def join_heads(pieces, mine):
    rows, width = pieces[0].shape
    rows = rows // 2

    def body(mine_ref, *refs):
        for xr in (0, 1):
            for zr in (0, 1):
                at = ((mine_ref[1] ^ xr) * 2 + (mine_ref[0] ^ zr)) * rows
                refs[2][pl.ds(pl.multiple_of(at, rows), rows), :] = refs[xr][zr * rows : (zr + 1) * rows, :]

    return call(
        body,
        (1,),
        [pl.BlockSpec((2 * rows, width), lambda i, s: (0, 0))] * 2,
        pl.BlockSpec((4 * rows, width), lambda i, s: (0, 0)),
        shape((4 * rows, width), BF16),
        tuple(pieces),
        mine,
    )


def norms(halves, gains, count):
    tokens, width = halves[0].shape
    each = tokens // count
    blocks = 2 * each

    def body(v_ref, a_ref, b_ref, first_ref, second_ref, stats_ref, x_buf, first_buf, second_buf, sems_in, sems_first, sems_second):
        def copy_in(k):
            half = (a_ref, b_ref)[k // each]
            return pltpu.make_async_copy(half.at[pl.ds(k % each * count, count)], x_buf.at[k % 2], sems_in.at[k % 2])

        def copy_first(k):
            return pltpu.make_async_copy(first_buf.at[k % 2], first_ref.at[pl.ds(k * count, count)], sems_first.at[k % 2])

        def copy_second(k):
            return pltpu.make_async_copy(second_buf.at[k % 2], second_ref.at[pl.ds(k * count, count)], sems_second.at[k % 2])

        copy_in(0).start()
        for k in range(blocks):
            slot = k % 2
            copy_in(k).wait()
            if k + 1 < blocks:
                copy_in(k + 1).start()
            if k >= 2:
                copy_first(k - 2).wait()
                copy_second(k - 2).wait()
            value = x_buf[slot].astype(F32)
            mean = jnp.mean(value, axis=-1, keepdims=True)
            center = value - mean
            scale = lax.rsqrt(jnp.mean(center * center, axis=-1, keepdims=True) + EPS)
            xhat = center * scale
            first_buf[slot] = (xhat * v_ref[0:1, :] + v_ref[1:2, :]).astype(BF16)
            second_buf[slot] = (xhat * v_ref[2:3, :] + v_ref[3:4, :]).astype(BF16)
            lane = lax.broadcasted_iota(jnp.int32, (count, 128), 1)
            stats_ref[k * count : (k + 1) * count, :] = jnp.where(lane == 0, mean, scale)
            copy_first(k).start()
            copy_second(k).start()
        for k in (blocks - 2, blocks - 1):
            copy_first(k).wait()
            copy_second(k).wait()

    some = pl.BlockSpec(memory_space=pl.ANY)
    return pl.pallas_call(
        body,
        grid=(1,),
        in_specs=[pl.BlockSpec((8, width), lambda i: (0, 0)), some, some],
        out_specs=[some, some, pl.BlockSpec((2 * tokens, 128), lambda i: (0, 0))],
        out_shape=[shape((2 * tokens, width), BF16)] * 2 + [shape((2 * tokens, 128), F32)],
        scratch_shapes=[pltpu.VMEM((2, count, width), BF16)] * 3 + [pltpu.SemaphoreType.DMA((2,))] * 3,
        compiler_params=pltpu.CompilerParams(vmem_limit_bytes=40 * 1024 * 1024),
        cost_estimate=pl.CostEstimate(flops=int(12 * COST), bytes_accessed=1024, transcendentals=0),
    )(gains, *halves)


def feed_up(second, w_up, bias, tile=256):
    tokens, width = second.shape
    deep, hidden = w_up[0].shape

    def body(s_ref, *refs):
        b_ref, act_ref, slope_ref = refs[4:]
        up = b_ref[...]
        for k in range(4):
            up = up + jnp.dot(s_ref[:, k * deep : (k + 1) * deep], refs[k][...], preferred_element_type=F32)
        phi_sum = 0.5 * (1.0 + lax.erf(up * (0.5**0.5)))
        act_ref[...] = (up * phi_sum).astype(BF16)
        slope_ref[...] = phi_sum + up * jnp.exp(-0.5 * up * up) * 0.3989422804014327

    block = pl.BlockSpec((tile, hidden), lambda i: (i, 0))
    return call(
        body,
        (tokens // tile,),
        [pl.BlockSpec((tile, width), lambda i: (i, 0))]
        + [pl.BlockSpec((deep, hidden), lambda i: (0, 0))] * 4
        + [pl.BlockSpec((1, hidden), lambda i: (0, 0))],
        [block, block],
        [shape((tokens, hidden), BF16), shape((tokens, hidden), F32)],
        (second, *w_up, bias),
        us=16,
    )


def either(steps, first_half, tile, width):
    half = steps // 2

    def spec(low):
        return pl.BlockSpec((tile, width), lambda i: (jnp.minimum(i, half - 1) if low else jnp.maximum(i - half, 0), 0))

    return [spec(first_half), spec(not first_half)]


def join_units(pieces, mine):
    unit, width = pieces[0].shape

    def body(mine_ref, *refs):
        k = 0
        for zr, xr, parts in ((0, 0, 1), (0, 1, 1), (1, 0, 2), (1, 1, 2)):
            size = unit // parts
            for part in range(parts):
                at = ((mine_ref[0] ^ zr) * 2 + (mine_ref[1] ^ xr)) * unit + part * size
                refs[len(pieces)][pl.ds(pl.multiple_of(at, size), size), :] = refs[k][...]
                k += 1

    return call(
        body,
        (1,),
        [pl.BlockSpec(p.shape, lambda i, s: (0, 0)) for p in pieces],
        pl.BlockSpec((4 * unit, width), lambda i, s: (0, 0)),
        shape((4 * unit, width), BF16),
        tuple(pieces),
        mine,
        us=3,
    )


def feed_back(g, w_down, slope, tile=256):
    half, width = g[0].shape
    steps = 2 * half // tile
    hidden = slope.shape[1]

    def body(ga_ref, gb_ref, w_ref, slope_ref, d_ref, column_ref):
        step = pl.program_id(0)

        @pl.when(step == 0)
        def _():
            column_ref[...] = jnp.zeros_like(column_ref)

        def work(g_ref):
            d_act = lax.dot_general(g_ref[...], w_ref[...], ROWS, preferred_element_type=F32)
            d_up = (d_act * slope_ref[...]).astype(BF16)
            d_ref[...] = d_up
            column_ref[...] += jnp.sum(d_up.astype(F32), axis=0, keepdims=True)

        pl.when(step < steps // 2)(lambda: work(ga_ref))
        pl.when(step >= steps // 2)(lambda: work(gb_ref))

    block = pl.BlockSpec((tile, hidden), lambda i: (i, 0))
    return call(
        body,
        (steps,),
        either(steps, True, tile, width) + [pl.BlockSpec((hidden, width), lambda i: (0, 0)), block],
        [block, pl.BlockSpec((1, hidden), lambda i: (0, 0))],
        [shape((2 * half, hidden), BF16), shape((1, hidden), F32)],
        (*g, w_down, slope),
        us=14,
    )


def weight_grad(left, right, mine, source, us=13):
    tokens, width = left.shape
    wide = right[0].shape[1]
    tile = width // 4
    count = len(right)

    def body(mine_ref, l_ref, *refs):
        part = lax.dot_general(l_ref[: tokens // count], refs[0][...], FIRSTS, preferred_element_type=F32)
        if count == 2:
            part = part + lax.dot_general(l_ref[tokens // 2 :], refs[1][...], FIRSTS, preferred_element_type=F32)
        for k, out in enumerate(refs[count:]):

            @pl.when(pl.program_id(0) == k)
            def _():
                out[...] = part.astype(out.dtype)

    return call(
        body,
        (4,),
        [pl.BlockSpec((tokens, tile), lambda i, s: (0, source(i, s)))]
        + [pl.BlockSpec(r.shape, lambda i, s: (0, 0)) for r in right],
        [pl.BlockSpec((tile, wide), lambda i, s: (0, 0))] * 4,
        [shape((tile, wide), BF16)] * 2 + [shape((tile, wide), F32)] * 2,
        (left, *right),
        mine,
        us=us,
    )


def head_grad(mixed, g, mine):
    tokens, head = mixed.shape
    width = g[0].shape[1]

    def body(mine_ref, l_ref, ga_ref, gb_ref, sent_ref, kept_ref):
        part = lax.dot_general(l_ref[: tokens // 2], ga_ref[...], FIRSTS, preferred_element_type=F32)
        part = part + lax.dot_general(l_ref[tokens // 2 :], gb_ref[...], FIRSTS, preferred_element_type=F32)
        upper, lower = part[: head // 2], part[head // 2 :]
        own = mine_ref[1] == 0
        sent_ref[...] = jnp.where(own, lower, upper).astype(BF16)
        kept_ref[...] = jnp.where(own, upper, lower)

    return call(
        body,
        (2,),
        [pl.BlockSpec((tokens, head), lambda i, s: (0, 0))]
        + [pl.BlockSpec((tokens // 2, width // 2), lambda i, s: (0, i))] * 2,
        [pl.BlockSpec((head // 2, width // 2), lambda i, s: (0, i))] * 2,
        [shape((head // 2, width), BF16), shape((head // 2, width), F32)],
        (mixed, *g),
        mine,
        us=5,
    )


def fold_tokens(kept, got):
    count, width = kept.shape
    tile = count // 4

    def body(k_ref, *refs):
        first_ref, second_ref, stays_ref = refs[4:]
        step = pl.program_id(0)
        for j in range(4):

            @pl.when(step == 3 - j)
            def _():
                total = k_ref[...].astype(F32) + refs[j][...].astype(F32)
                out = (stays_ref, stays_ref, second_ref, first_ref)[j]
                out[...] = total.astype(out.dtype)

    fixed = pl.BlockSpec((tile, width), lambda i: (0, 0))
    return call(
        body,
        (4,),
        [pl.BlockSpec((tile, width), lambda i: (3 - i, 0))] + [fixed] * 4,
        [fixed, fixed, pl.BlockSpec((tile, width), lambda i: (jnp.minimum(3 - i, 1), 0))],
        [shape((tile, width), BF16)] * 2 + [shape((2 * tile, width), F32)],
        (kept,) + tuple(got),
        us=5,
    )


def add_half(kept, got, rows, at):
    width = kept.shape[1]

    def body(k_ref, g_ref, o_ref):
        o_ref[...] = (k_ref[...] + g_ref[...].astype(F32)).astype(BF16)

    fixed = pl.BlockSpec((rows, width), lambda i: (0, 0))
    return call(
        body, (1,), [pl.BlockSpec((rows, width), lambda i: (at, 0)), fixed], fixed, shape((rows, width), BF16), (kept, got)
    )


def attend(first, w_qkv, b_qkv, g, w_proj, cosine, sine, docs):
    tokens, width = first.shape
    rows, _, count = docs.shape
    deep = w_qkv[0].shape[0]
    lanes = cosine.shape[1]
    half = ROT // 2
    scale = HEAD ** (-0.5)

    def body(f_ref, w0_ref, w1_ref, w2_ref, w3_ref, b_ref, ga_ref, gb_ref, p_ref, cos_ref, sin_ref, row_ref, mixed_ref, d_qkv_ref, column_ref):
        step = pl.program_id(0)

        @pl.when(step == 0)
        def _():
            column_ref[...] = jnp.zeros_like(column_ref)

        def work(g_ref):
            cos, sin = cos_ref[...], sin_ref[...]
            lane = lax.broadcasted_iota(jnp.int32, cos.shape, 1)

            def turn(v, sign):
                front = v[:, :lanes]
                other = jnp.where(lane < half, pltpu.roll(front, lanes - half, 1), pltpu.roll(front, half, 1))
                return jnp.concatenate([front * cos + sign * (other * sin), v[:, lanes:]], axis=1)

            qkv = b_ref[...]
            for k, w_ref in enumerate((w0_ref, w1_ref, w2_ref, w3_ref)):
                qkv = qkv + jnp.dot(f_ref[:, k * deep : (k + 1) * deep], w_ref[...], preferred_element_type=F32)
            d_mixed = lax.dot_general(g_ref[...], p_ref[...], ROWS, preferred_element_type=F32).astype(BF16)
            rq = turn(qkv[:, :HEAD], 1.0).astype(BF16)
            rk = turn(qkv[:, HEAD : 2 * HEAD], 1.0).astype(BF16)
            rv = qkv[:, 2 * HEAD :].astype(BF16)
            here = lax.broadcasted_iota(jnp.int32, (count, count), 0)
            there = lax.broadcasted_iota(jnp.int32, (count, count), 1)
            across = jnp.broadcast_to(row_ref[0], (count, count))
            allowed = (across == across.T) & (there <= here)
            raw = lax.dot_general(rq, rk, ROWS, preferred_element_type=F32)
            scores = jnp.where(allowed, raw * scale, MASKED)
            expo = jnp.exp(scores - jnp.max(scores, axis=1, keepdims=True))
            probs = expo / jnp.sum(expo, axis=1, keepdims=True)
            weights = probs.astype(BF16)
            mixed_ref[...] = jnp.dot(weights, rv, preferred_element_type=F32).astype(BF16)
            d_prob = lax.dot_general(d_mixed, rv, ROWS, preferred_element_type=F32)
            d_score = probs * (d_prob - jnp.sum(probs * d_prob, axis=1, keepdims=True))
            d_raw = (d_score * scale).astype(BF16)
            d_rq = jnp.dot(d_raw, rk, preferred_element_type=F32)
            d_rk = lax.dot_general(d_raw, rq, FIRSTS, preferred_element_type=F32)
            d_rv = lax.dot_general(weights, d_mixed, FIRSTS, preferred_element_type=F32)
            d_qkv = jnp.concatenate([turn(d_rq, -1.0), turn(d_rk, -1.0), d_rv], axis=1).astype(BF16)
            d_qkv_ref[...] = d_qkv
            column_ref[...] += jnp.sum(d_qkv.astype(F32), axis=0, keepdims=True)

        pl.when(step < rows // 2)(lambda: work(ga_ref))
        pl.when(step >= rows // 2)(lambda: work(gb_ref))

    def row(*dims):
        return pl.BlockSpec(dims, lambda i: (i, 0))

    def whole(*dims):
        return pl.BlockSpec(dims, lambda i: (0, 0))

    return call(
        body,
        (rows,),
        [
            row(count, width),
            *([whole(deep, 3 * HEAD)] * 4),
            whole(1, 3 * HEAD),
            *either(rows, True, count, width),
            whole(HEAD, width),
            row(count, lanes),
            row(count, lanes),
            pl.BlockSpec((1, 1, count), lambda i: (i, 0, 0)),
        ],
        [row(count, HEAD), row(count, 3 * HEAD), whole(1, 3 * HEAD)],
        [shape((tokens, HEAD), BF16), shape((tokens, 3 * HEAD), BF16), shape((1, 3 * HEAD), F32)],
        (first, *w_qkv, b_qkv, *g, w_proj, cosine, sine, docs),
        us=17,
    )


def branch_sum(act, w_down, mixed, w_proj, tile=256):
    tokens, hidden = act.shape
    width = w_down.shape[1]
    steps = tokens // tile
    sent = steps // 2

    def body(a_ref, w_ref, m_ref, p_ref, *outs):
        part = jnp.dot(a_ref[...], w_ref[...], preferred_element_type=F32)
        part = (part + jnp.dot(m_ref[...], p_ref[...], preferred_element_type=F32)).astype(BF16)
        outs[sent][...] = part
        step = pl.program_id(0)
        for k in range(sent):

            @pl.when(step == k)
            def _():
                outs[k][...] = part

    def turned(i):
        return (lax.rem(i + sent, steps), 0)

    fixed = pl.BlockSpec((tile, width), lambda i: (0, 0))
    return call(
        body,
        (steps,),
        [
            pl.BlockSpec((tile, hidden), turned),
            pl.BlockSpec((hidden, width), lambda i: (0, 0)),
            pl.BlockSpec((tile, HEAD), turned),
            pl.BlockSpec((HEAD, width), lambda i: (0, 0)),
        ],
        [fixed] * sent + [pl.BlockSpec((tile, width), lambda i: (jnp.maximum(i - sent, 0), 0))],
        [shape((tile, width), BF16)] * sent + [shape((tokens // 2, width), BF16)],
        (act, w_down, mixed, w_proj),
        us=16,
    )


def edge_sum(d_up, w_up, d_qkv, w_qkv, x, stats, gains, tile=256):
    tokens, hidden = d_up.shape
    deep = w_up[0].shape[0]
    width = 4 * deep
    steps = tokens // tile
    sent = steps // 2

    def body(du_ref, dq_ref, xa_ref, xb_ref, stats_ref, v_ref, *refs):
        outs = refs[8:]
        sums_ref = outs[sent + 1]
        step = pl.program_id(0)

        @pl.when(step == 0)
        def _():
            sums_ref[...] = jnp.zeros_like(sums_ref)

        for k in range(4):
            part = slice(k * deep, (k + 1) * deep)
            d_second = lax.dot_general(du_ref[...], refs[k][...], ROWS, preferred_element_type=F32)
            d_first = lax.dot_general(dq_ref[...], refs[4 + k][...], ROWS, preferred_element_type=F32)
            x = jnp.where(step < sent, xb_ref[:, part], xa_ref[:, part])
            xhat = (x.astype(F32) - stats_ref[:, 0:1]) * stats_ref[:, 1:2]
            outs[sent][:, part] = (d_first * v_ref[0:1, part] + d_second * v_ref[2:3, part]).astype(BF16)
            sums_ref[0:1, part] += jnp.sum(d_first * xhat, axis=0, keepdims=True)
            sums_ref[1:2, part] += jnp.sum(d_first, axis=0, keepdims=True)
            sums_ref[2:3, part] += jnp.sum(d_second * xhat, axis=0, keepdims=True)
            sums_ref[3:4, part] += jnp.sum(d_second, axis=0, keepdims=True)

        for j in range(sent):

            @pl.when(step == j)
            def _():
                outs[j][...] = outs[sent][...]

    def turned(i):
        return (lax.rem(i + sent, steps), 0)

    def whole(*dims):
        return pl.BlockSpec(dims, lambda i: (0, 0))

    return call(
        body,
        (steps,),
        [
            pl.BlockSpec((tile, hidden), turned),
            pl.BlockSpec((tile, 3 * HEAD), turned),
            *either(steps, False, tile, width),
            pl.BlockSpec((tile, 128), turned),
            whole(8, width),
        ]
        + [whole(deep, hidden)] * 4
        + [whole(deep, 3 * HEAD)] * 4,
        [whole(tile, width)] * sent
        + [pl.BlockSpec((tile, width), lambda i: (jnp.maximum(i - sent, 0), 0)), whole(8, width)],
        [shape((tile, width), BF16)] * sent + [shape((tokens // 2, width), BF16), shape((8, width), F32)],
        (d_up, d_qkv, *x, stats, gains, *w_up, *w_qkv),
        us=28,
        limit=48,
    )


def finish(edge_k, edge_g0, edge_got, x0, g, mine):
    count, width = x0.shape
    wide = width // 16

    def body(mine_ref, k_ref, a_ref, b_ref, x_ref, g_ref, o_ref):
        edge = k_ref[...] + a_ref[...].astype(F32) + b_ref[...].astype(F32)
        value = x_ref[...].astype(F32)
        center = value - jnp.mean(value, axis=-1, keepdims=True)
        scale = lax.rsqrt(jnp.mean(center * center, axis=-1, keepdims=True) + EPS)
        xhat = center * scale
        back = edge - jnp.mean(edge, axis=-1, keepdims=True) - xhat * jnp.mean(edge * xhat, axis=-1, keepdims=True)
        back = back * scale
        for j in range(16):
            xr, zr, b, c = bits_of(j, 4)
            source = (zr ^ mine_ref[0]) * 8 + b * 4 + c * 2 + (xr ^ mine_ref[1])
            place = pl.ds(pl.multiple_of(source * wide, wide), wide)
            o_ref[:, place] = g_ref[:, place].astype(F32) + back[:, j * wide : (j + 1) * wide]

    tile = count // 2
    block = pl.BlockSpec((tile, width), lambda i, s: (i, 0))
    return call(
        body, (2,), [block] * 5, block, shape((count, width), F32), (edge_k, edge_g0, edge_got, x0, g), mine, us=5
    )


def local_tuned(
    inputs,
    doc_ids,
    attn_gain,
    attn_shift,
    ffn_gain,
    ffn_shift,
    qkv_weight,
    qkv_bias,
    proj_weight,
    proj_bias,
    up_weight,
    up_bias,
    down_weight,
    down_bias,
    cotangent,
):
    n = lax.axis_size(AXIS)
    lay = Layout(n)
    count, width = inputs.shape
    rows = width // n
    unit = up_bias.shape[0]
    hidden = 4 * unit
    me = lax.axis_index(AXIS)
    mzh, mx = lay.mine(ZH), lay.mine(X)
    mine = jnp.stack([mzh, mx]).astype(jnp.int32)

    small = jnp.concatenate(
        [doc_ids[0].astype(BF16), up_bias, attn_gain, attn_shift, ffn_gain, ffn_shift, proj_bias, down_bias, qkv_bias]
    )
    small = jnp.pad(small, (0, 16 * 128 - small.shape[0])).reshape(16, 128)
    small = jnp.broadcast_to(small[None], (n, 16, 128))
    small = lax.all_to_all(small, AXIS, split_axis=0, concat_axis=0, tiled=True)
    down_a, down_b = down_weight[: unit // 2], down_weight[unit // 2 :]
    cols = split_columns(up_weight, qkv_weight)
    (x0,) = after((inputs,), cols)
    x0 = order_columns(x0, mine)
    down_za = flip(down_a, ZH)
    down_x = flip(down_weight, X)
    (cols,) = after((cols,), small)
    cols = lay.to_columns(cols)
    x1 = flip(x0, ZL)
    x2 = flip(x0, Y)
    proj0 = lay.exchange_heads(proj_weight)

    freq = 10000.0 ** (-2.0 * np.arange(ROT // 2, dtype=np.float32) / ROT)
    rest = np.zeros(128 - ROT, np.float32)
    freq = jnp.asarray(np.concatenate([freq, freq, rest])[None], F32)
    sign = jnp.asarray(np.concatenate([np.full(ROT // 2, -1.0), np.full(ROT // 2, 1.0), rest])[None], F32)
    bit_of = jnp.stack([lay.mine(b) for b in (ZH, X, ZL, Y, CORE)] + [me]).astype(jnp.int32)
    here = lay.mine(ZL) * 4 + lay.mine(Y) * 2 + lay.mine(CORE)
    gains, b_out, b_up, b_qkv, docs, cosine, sine = prepare(small, bit_of, freq, sign, rows, unit, count)

    def restore(v):
        v = v.reshape(v.shape[0], 2, 2, 4, 2 * rows).transpose(0, 2, 3, 1, 4)
        v = jnp.where(mzh == 1, v[:, ::-1], v)
        v = jnp.where(mx == 1, v[:, :, :, ::-1], v)
        return v.reshape(v.shape[0], width)

    cols, down_za, x1, x2, g0, proj0 = after(
        (cols, down_za, x1, x2, cotangent, proj0), cols, down_za, down_x, x1, x2, proj0, gains
    )
    up_cols, qkv_cols = cols[:, :, :hidden], cols[:, :, hidden:]
    up_z = flip(up_cols, ZH)
    up_x = flip(up_cols, X)
    g1 = flip(g0, ZL)
    x3 = flip(x1, Y)
    g2 = flip(g0, Y)

    up_z, x1, x2, x3, g1, down_b, qkv_cols, proj0 = after(
        (up_z, x1, x2, x3, g1, down_b, qkv_cols, proj0), up_x, g2
    )
    xa = join([x0, x1, x2, x3])
    xb = flip(xa, CORE)
    up_xz = flip(up_z, X)
    down_zb = flip(down_b, ZH)
    proj_z = flip(proj0, ZH)
    g3 = flip(g1, Y)
    gains, g0, g1, g2, g3, qkv_cols, proj_z, down_za, down_zb, up_xz = after(
        (gains, g0, g1, g2, g3, qkv_cols, proj_z, down_za, down_zb, up_xz), xb
    )
    ga = join([g0, g1, g2, g3])
    gb = flip(ga, CORE)
    qkv_z = flip(qkv_cols, ZH)
    qkv_x = flip(qkv_cols, X)
    down_xza = flip(down_za, X)
    down_xzb = flip(down_zb, X)
    proj_two = jnp.concatenate([proj0, proj_z], axis=0)
    first, second, stats = norms([xa, xb], gains, count)
    w_up = [v.reshape(-1, hidden) for v in (up_cols, up_z, up_x, up_xz)]
    act, slope = feed_up(second, w_up, b_up)
    act, qkv_z, proj_two, down_xza, down_xzb = after((act, qkv_z, proj_two, down_xza, down_xzb), gb, qkv_x)
    g = [ga, gb]
    x = [xa, xb]
    qkv_xz = flip(qkv_z, X)

    def hidden_block(step, s):
        return (s[0] ^ (1 - lax.rem(step, 2))) * 2 + (s[1] ^ jnp.where(step < 2, 1, 0))

    def feature_block(step, s):
        return 3 - step

    w_down = join_units([down_weight, down_x, down_za, down_zb, down_xza, down_xzb], mine)
    down_s1, down_s0, down_k1, down_k0 = weight_grad(act, g, mine, hidden_block, us=15)
    down_g1 = flip(down_s1, X)
    proj_xtwo = flip(proj_two, X)
    slope, w_down, qkv_xz, proj_xtwo = after((slope, w_down, qkv_xz, proj_xtwo), down_s1)
    d_up, column_up = feed_back(g, w_down, slope)
    d_up, down_s0 = after((d_up, down_s0), d_up)
    down_g0 = flip(down_s0, X)
    up_s1, up_s0, up_k1, up_k0 = weight_grad(second, [d_up], mine, feature_block, us=12)
    up_g1 = flip(up_s1, X)

    (down_g1,) = after((down_g1,), up_s1)
    down_sent = add_half(down_k1, down_g1, unit, 0)
    down_got = flip(down_sent, ZH)
    w_proj = join_heads([proj_two, proj_xtwo], mine)
    w_qkv = [v.reshape(-1, 3 * HEAD) for v in (qkv_cols, qkv_z, qkv_x, qkv_xz)]
    (first_,) = after((first,), down_sent)
    mixed, d_qkv, column_qkv = attend(first_, w_qkv, b_qkv, g, w_proj, cosine, sine, docs)
    act, mixed, d_qkv = after((act, mixed, d_qkv), down_g0, mixed)
    *out_s, out_k = branch_sum(act, w_down, mixed, w_proj)
    out_g = [flip(v, CORE) for v in out_s]
    d_qkv, up_g1, up_s0 = after((d_qkv, up_g1, up_s0), out_k, up_g1, down_got)
    up_g0 = flip(up_s0, X)
    up_sent = add_half(up_k1, up_g1, up_k1.shape[0], 0)
    up_got = flip(up_sent, ZH)
    (d_qkv,) = after((d_qkv,), up_sent)
    qkv_s1, qkv_s0, qkv_k1, qkv_k0 = weight_grad(first, [d_qkv], mine, feature_block, us=10)
    qkv_g1 = flip(qkv_s1, X)
    *out_g, out_k = after((*out_g, out_k), *out_g, qkv_s1)
    out_s1, out_s0, out_k = fold_tokens(out_k, out_g)
    out_g1 = flip(out_s1, Y)

    d_up, d_qkv, out_s0, qkv_s0 = after((d_up, d_qkv, out_s0, qkv_s0), out_s1)
    out_g0 = flip(out_s0, Y)
    qkv_g0 = flip(qkv_s0, X)
    *edge_s, edge_k, sums = edge_sum(d_up, w_up, d_qkv, w_qkv, x, stats, gains)

    *edge_s, out_g1, qkv_g1, mixed, up_got, sums = after(
        (*edge_s, out_g1, qkv_g1, mixed, up_got, sums), out_g1, qkv_g1, edge_k, up_got, up_g0
    )
    edge_g = [flip(v, CORE) for v in edge_s]
    out_sent = add_half(out_k, out_g1, count, 1)
    out_got = flip(out_sent, ZL)
    qkv_sent = add_half(qkv_k1, qkv_g1, qkv_k1.shape[0], 0)
    qkv_got = flip(qkv_sent, ZH)
    (mixed,) = after((mixed,), out_sent, qkv_sent)
    proj_s, proj_k = head_grad(mixed, g, mine)
    *edge_g, edge_k = after((*edge_g, edge_k), *edge_g, proj_s)
    edge_s1, edge_s0, edge_k = fold_tokens(edge_k, edge_g)
    column_out = jnp.sum(cotangent.astype(F32), axis=0)
    spread_up = lax.dynamic_update_slice(jnp.zeros((HEADS, hidden), F32), column_up, (here, 0))
    spread_up = spread_up.reshape(2, 2, 2, 2, 2, unit).transpose(3, 0, 1, 4, 2, 5)
    spread_qkv = lax.dynamic_update_slice(jnp.zeros((HEADS, 3 * HEAD), F32), column_qkv, (here, 0))
    spread_qkv = spread_qkv.reshape(2, 2, 2, 3, HEAD).transpose(3, 2, 0, 1, 4)
    sums = restore(sums[:4])
    flat = [s.reshape(n, -1) for s in (sums[0], sums[1], sums[2], sums[3], column_out, spread_qkv, spread_up)]
    sums = lax.all_to_all(jnp.concatenate(flat, axis=1), AXIS, split_axis=0, concat_axis=0, tiled=True)
    proj_s, edge_s1, edge_s0, up_got, qkv_g0, out_g0, sums, out_k, down_k0 = after(
        (proj_s, edge_s1, edge_s0, up_got, qkv_g0, out_g0, sums, out_k, down_k0)
    )
    edge_g1 = flip(edge_s1, Y)
    proj_g = flip(proj_s, X)
    edge_g0 = flip(edge_s0, Y)
    up_sum = (up_k0 + up_g0.astype(F32) + up_got.astype(F32)).astype(BF16)
    up_back = lay.to_columns(up_sum.reshape(8, rows, hidden))

    value_own = inputs.astype(F32)
    out_half = value_own + b_out + out_k[:count] + out_g0.astype(F32)
    grad_down = down_k0 + down_g0.astype(F32) + down_got.astype(F32)
    proj_g, edge_g1, qkv_got, out_half = after((proj_g, edge_g1, qkv_got, out_half), grad_down)
    edge_sent = add_half(edge_k, edge_g1, count, 1)
    edge_got = flip(edge_sent, ZL)
    proj_sum = (proj_k + proj_g.astype(F32)).reshape(2, rows, width)
    proj_kept = lax.dynamic_index_in_dim(proj_sum, mzh, 0, keepdims=False)
    proj_sent = lax.dynamic_index_in_dim(proj_sum, 1 - mzh, 0, keepdims=False).astype(BF16)
    proj_got = flip(proj_sent, ZH)
    qkv_sum = (qkv_k0 + qkv_g0.astype(F32) + qkv_got.astype(F32)).astype(BF16)
    up_back, edge_sent_, qkv_sum = after((up_back, edge_sent, qkv_sum), up_back, edge_sent, proj_sent, qkv_sum)
    qkv_back = lay.to_columns(qkv_sum.reshape(8, rows, 3 * HEAD))
    grad_up = join_up(up_back)
    layer_out = out_half + out_got.astype(F32)

    sums = jnp.sum(sums, axis=0)
    got, at = [], 0
    for size in [rows] * 5 + [3 * rows, unit]:
        got.append(sums[at : at + size])
        at += size

    proj_got, edge_got = after((proj_got, edge_got), proj_got, edge_got, edge_g0, grad_up, layer_out)
    grad_proj = lay.exchange_heads((proj_kept + proj_got.astype(F32)).astype(BF16)).astype(F32)
    grad_qkv = join_qkv(qkv_back)
    grad_inputs = finish(edge_k, edge_g0, edge_got, x0, cotangent, mine)
    return (
        layer_out,
        grad_inputs,
        got[0],
        got[1],
        got[2],
        got[3],
        grad_qkv,
        got[5],
        grad_proj,
        got[4],
        grad_up,
        got[6],
        grad_down,
        got[4],
    )


def solution(mesh):
    tokens, rows = P(AXIS, None), P(AXIS)
    return jax.shard_map(
        local_tuned if mesh.shape[AXIS] == 32 else local_any,
        mesh=mesh,
        in_specs=(tokens, tokens, rows, rows, rows, rows, tokens, rows, tokens, rows, tokens, rows, tokens, rows, tokens),
        out_specs=(tokens, tokens, rows, rows, rows, rows, tokens, rows, tokens, rows, tokens, rows, tokens, rows),
        check_vma=False,
    )
```

```python
import functools

import jax
import jax.numpy as jnp
import numpy as np
from jax import lax
from jax.experimental import pallas as pl
from jax.experimental.pallas import tpu as pltpu
from jax.sharding import PartitionSpec as P

HEADS = 8
HEAD = 256
ROT = 64
EPS = 1e-05
MASKED = -1e30
AXIS = "fsdp"
BF16 = jnp.bfloat16
F32 = jnp.float32

SPLIT_BITS = {32: (3, 2, 0), 128: (3, 1, 0)}


def attention_kernel(qkv_ref, turn_ref, docs_row_ref, docs_col_ref, d_mixed_ref, mixed_ref, d_qkv_ref, column_ref):
    half = ROT // 2
    cosine = turn_ref[0]
    sine = turn_ref[1]
    lanes = cosine.shape[1]
    lane = lax.broadcasted_iota(jnp.int32, cosine.shape, 1)

    def swap(v):
        return jnp.where(lane < half, pltpu.roll(v, lanes - half, 1), pltpu.roll(v, half, 1))

    def turn(v, sign):
        front = v[:, :lanes]
        front = front * cosine + sign * (swap(front) * sine)
        return jnp.concatenate([front, v[:, lanes:]], axis=1)

    rq = turn(qkv_ref[:, :HEAD], 1.0).astype(BF16)
    rk = turn(qkv_ref[:, HEAD : 2 * HEAD], 1.0).astype(BF16)
    rv = qkv_ref[:, 2 * HEAD :].astype(BF16)
    count = rq.shape[0]
    here = lax.broadcasted_iota(jnp.int32, (count, count), 0)
    there = lax.broadcasted_iota(jnp.int32, (count, count), 1)
    allowed = (docs_row_ref[0] == docs_col_ref[0]) & (there <= here)
    scale = HEAD ** (-0.5)
    rows = (((1,), (1,)), ((), ()))
    firsts = (((0,), (0,)), ((), ()))
    raw = lax.dot_general(rq, rk, rows, preferred_element_type=F32)
    scores = jnp.where(allowed, raw * scale, MASKED)
    expo = jnp.exp(scores - jnp.max(scores, axis=1, keepdims=True))
    probs = expo / jnp.sum(expo, axis=1, keepdims=True)
    weights = probs.astype(BF16)
    mixed_ref[...] = jnp.dot(weights, rv, preferred_element_type=F32).astype(BF16)
    d_mixed = d_mixed_ref[...]
    d_prob = lax.dot_general(d_mixed, rv, rows, preferred_element_type=F32)
    d_score = probs * (d_prob - jnp.sum(probs * d_prob, axis=1, keepdims=True))
    d_raw = (d_score * scale).astype(BF16)
    d_rq = jnp.dot(d_raw, rk, preferred_element_type=F32)
    d_rk = lax.dot_general(d_raw, rq, firsts, preferred_element_type=F32)
    d_rv = lax.dot_general(weights, d_mixed, firsts, preferred_element_type=F32)
    d_qkv = jnp.concatenate([turn(d_rq, -1.0), turn(d_rk, -1.0), d_rv], axis=1).astype(BF16)
    d_qkv_ref[...] = d_qkv

    @pl.when(pl.program_id(0) == 0)
    def _():
        column_ref[...] = jnp.zeros_like(column_ref)

    column_ref[...] += jnp.sum(d_qkv.astype(F32), axis=0, keepdims=True)


def attention(qkv, cosine, sine, docs, d_mixed):
    rows, count = docs.shape
    turns = jnp.stack([cosine, sine])
    lanes = turns.shape[2]
    return pl.pallas_call(
        attention_kernel,
        grid=(rows,),
        in_specs=[
            pl.BlockSpec((count, 3 * HEAD), lambda i: (i, 0)),
            pl.BlockSpec((2, count, lanes), lambda i: (0, i, 0)),
            pl.BlockSpec((1, 1, count), lambda i: (i, 0, 0)),
            pl.BlockSpec((1, count, 1), lambda i: (i, 0, 0)),
            pl.BlockSpec((count, HEAD), lambda i: (i, 0)),
        ],
        out_specs=[
            pl.BlockSpec((count, HEAD), lambda i: (i, 0)),
            pl.BlockSpec((count, 3 * HEAD), lambda i: (i, 0)),
            pl.BlockSpec((1, 3 * HEAD), lambda i: (0, 0)),
        ],
        out_shape=[
            jax.ShapeDtypeStruct((rows * count, HEAD), BF16),
            jax.ShapeDtypeStruct((rows * count, 3 * HEAD), BF16),
            jax.ShapeDtypeStruct((1, 3 * HEAD), F32),
        ],
        compiler_params=pltpu.CompilerParams(vmem_limit_bytes=32 * 1024 * 1024),
        cost_estimate=pl.CostEstimate(
            flops=16 * rows * count * count * HEAD, bytes_accessed=20 * rows * count * HEAD, transcendentals=rows * count * count
        ),
    )(qkv, turns, docs[:, None, :], docs[:, :, None], d_mixed)


def times_rows(left, right):
    return jnp.einsum("tc,nc->tn", left, right, preferred_element_type=F32)


def times_tokens(left, right):
    return jnp.einsum("tn,td->nd", left, right, preferred_element_type=F32)


class Layout:
    def __init__(self, count):
        self.count = count
        self.bits = count.bit_length() - 1
        self.h_bits = SPLIT_BITS.get(count, (2, 1, 0))
        self.t_bits = tuple(b for b in range(self.bits - 1, -1, -1) if b not in self.h_bits)
        head_bits = tuple(range(self.bits - 1, self.bits - 4, -1))
        self.swap = {b: b for b in range(self.bits)}
        for a, b in zip([a for a in head_bits if a not in self.h_bits], [b for b in self.h_bits if b not in head_bits]):
            self.swap[a], self.swap[b] = b, a
        self.groups = []
        for t in range(1 << len(self.t_bits)):
            base = sum(((t >> (len(self.t_bits) - 1 - i)) & 1) << b for i, b in enumerate(self.t_bits))
            self.groups.append(
                [base | sum(((h >> (2 - i)) & 1) << b for i, b in enumerate(self.h_bits)) for h in range(8)]
            )

    def swapped(self, device):
        return sum(((device >> b) & 1) << self.swap[b] for b in range(self.bits))

    def axis(self, bit):
        return self.bits - 1 - bit

    def flip(self, value, bit):
        return lax.ppermute(value, AXIS, [(d, d ^ (1 << bit)) for d in range(self.count)])

    def exchange_heads(self, value):
        return lax.ppermute(value, AXIS, [(d, self.swapped(d)) for d in range(self.count)])

    def mine(self, bit):
        return (lax.axis_index(AXIS) >> bit) & 1

    def gather(self, value):
        pieces = {0: value}
        for bit in self.t_bits:
            pieces.update({key | (1 << bit): self.flip(piece, bit) for key, piece in list(pieces.items())})
        return pieces

    def place(self, pieces, order, shape):
        some = pieces[0]
        whole = jnp.zeros(shape, some.dtype)
        block = tuple(1 if bit is not None else size for bit, size in zip(order, shape))
        block = block + shape[len(order) :]
        for key, piece in pieces.items():
            starts = [0 if bit is None else self.mine(bit) ^ ((key >> bit) & 1) for bit in order]
            starts = starts + [0] * (len(shape) - len(order))
            whole = lax.dynamic_update_slice(whole, piece.reshape(block), starts)
        return whole

    def reduce(self, part, order):
        order = list(order)
        for bit in reversed(self.t_bits):
            axis = order.index(bit)
            mine = self.mine(bit)
            away = lax.dynamic_index_in_dim(part, 1 - mine, axis, keepdims=False).astype(BF16)
            keep = lax.dynamic_index_in_dim(part, mine, axis, keepdims=False)
            part = keep + self.flip(away, bit).astype(F32)
            order.pop(axis)
        return part

    def gather_tokens(self, value):
        pieces = [value]
        for bit in self.h_bits[:-1]:
            pieces = pieces + [self.flip(piece, bit) for piece in pieces]
        own = jnp.concatenate(pieces, axis=0)
        return jnp.concatenate([own, self.flip(own, self.h_bits[-1])], axis=0)

    def reduce_tokens(self, part):
        for bit in reversed(self.h_bits):
            half = part.shape[0] // 2
            away = part[half:].astype(BF16)
            part = part[:half].astype(F32) + self.flip(away, bit).astype(F32)
        return part

    def to_columns(self, value):
        return lax.all_to_all(value, AXIS, split_axis=0, concat_axis=0, tiled=True, axis_index_groups=self.groups)


def local_any(
    inputs,
    doc_ids,
    attn_gain,
    attn_shift,
    ffn_gain,
    ffn_shift,
    qkv_weight,
    qkv_bias,
    proj_weight,
    proj_bias,
    up_weight,
    up_bias,
    down_weight,
    down_bias,
    cotangent,
):
    n = lax.axis_size(AXIS)
    lay = Layout(n)
    bits = lay.bits
    two = (2,) * bits
    count, width = inputs.shape
    rows = width // n
    unit = up_bias.shape[0]
    hidden = unit * (n // HEADS)
    h_axes = [lay.axis(b) for b in lay.h_bits]
    t_axes = [lay.axis(b) for b in lay.t_bits]

    small = jnp.concatenate(
        [
            attn_gain,
            attn_shift,
            ffn_gain,
            ffn_shift,
            proj_bias,
            down_bias,
            qkv_bias,
            up_bias,
            doc_ids[0].astype(BF16),
        ]
    )
    small = lax.all_to_all(
        jnp.broadcast_to(small[None], (n, small.shape[0])), AXIS, split_axis=0, concat_axis=0, tiled=True
    ).astype(F32)
    sizes = [rows] * 6 + [3 * rows, unit, count]
    vectors, at = [], 0
    for size in sizes:
        vectors.append(small[:, at : at + size])
        at += size
    a_gain, a_shift, f_gain, f_shift, b_proj, b_down = [v.reshape(1, width) for v in vectors[:6]]

    heads_at = [2 + (bits - 1 - lay.swap[b]) for b in lay.h_bits]
    up_cols = up_weight.reshape((rows,) + two + (unit,))
    up_cols = up_cols.transpose([1 + a for a in h_axes] + [0] + [1 + a for a in t_axes] + [bits + 1])
    up_cols = lay.to_columns(up_cols.reshape(HEADS, rows, hidden))
    qkv_cols = qkv_weight.reshape(rows, 3, 2, 2, 2, HEAD).transpose(heads_at + [0, 1, 5])
    qkv_cols = lay.to_columns(qkv_cols.reshape(HEADS, rows, 3 * HEAD))

    x = lay.gather_tokens(inputs)
    row_order = [b if b in lay.t_bits else None for b in range(bits - 1, -1, -1)]
    w_up = lay.place(lay.gather(up_cols), row_order, two + (rows, hidden)).reshape(width, hidden)
    g = lay.gather_tokens(cotangent)
    t_two = (2,) * len(lay.t_bits)
    w_down = lay.place(lay.gather(down_weight), lay.t_bits, t_two + (unit, width)).reshape(hidden, width)
    proj_order = [lay.swap[b] for b in range(bits - 4, -1, -1)]
    w_proj = lay.place(
        lay.gather(lay.exchange_heads(proj_weight)), proj_order, t_two + (rows, width)
    ).reshape(HEAD, width)
    w_qkv = lay.place(lay.gather(qkv_cols), row_order, two + (rows, 3 * HEAD)).reshape(width, 3 * HEAD)

    b_up = vectors[7].reshape(two + (unit,)).transpose(h_axes + t_axes + [bits]).reshape(HEADS, hidden)
    b_qkv = vectors[6].reshape((3, 2, 2, 2, HEAD)).transpose([a - 1 for a in heads_at] + [0, 4]).reshape(HEADS, 3 * HEAD)
    here = sum(lay.mine(b) << (2 - i) for i, b in enumerate(lay.h_bits))
    b_up = lax.dynamic_index_in_dim(b_up, here, 0, keepdims=True)
    b_qkv = lax.dynamic_index_in_dim(b_qkv, here, 0, keepdims=True)
    me = lax.axis_index(AXIS)
    docs = []
    for j in range(HEADS):
        other = me ^ sum(((j >> i) & 1) << b for i, b in enumerate(lay.h_bits))
        docs.append(lax.dynamic_index_in_dim(vectors[8], other, 0, keepdims=True))
    docs = jnp.concatenate(docs, axis=0).astype(jnp.int32)

    index = jnp.arange(count, dtype=jnp.int32)
    same = docs[:, :, None] == docs[:, None, :]
    position = jnp.sum((same & (index[None, None, :] < index[None, :, None])).astype(jnp.int32), axis=2).reshape(-1)
    freq = 10000.0 ** (-2.0 * jnp.arange(ROT // 2, dtype=F32) / ROT)
    angle = position.astype(F32)[:, None] * freq[None, :]
    cosine, sine = jnp.cos(angle), jnp.sin(angle)
    rest = 128 - ROT
    cosine = jnp.concatenate([cosine, cosine, jnp.ones((angle.shape[0], rest), F32)], axis=1)
    sine = jnp.concatenate([-sine, sine, jnp.zeros((angle.shape[0], rest), F32)], axis=1)

    value = x.astype(F32)
    center = value - jnp.mean(value, axis=-1, keepdims=True)
    scale = lax.rsqrt(jnp.mean(center * center, axis=-1, keepdims=True) + EPS)
    xhat = center * scale
    first = (xhat * a_gain + a_shift).astype(BF16)
    second = (xhat * f_gain + f_shift).astype(BF16)

    up = jnp.dot(second, w_up, preferred_element_type=F32) + b_up
    phi_sum = 0.5 * (1.0 + lax.erf(up * (0.5**0.5)))
    act = (up * phi_sum).astype(BF16)
    slope = phi_sum + up * jnp.exp(-0.5 * up * up) * 0.3989422804014327
    part_down = times_tokens(act, g)
    d_act = times_rows(g, w_down)
    d_up = (d_act * slope).astype(BF16)
    part_up = times_tokens(second, d_up)
    d_second = times_rows(d_up, w_up)

    d_mixed = times_rows(g, w_proj).astype(BF16)
    qkv = jnp.dot(first, w_qkv, preferred_element_type=F32) + b_qkv
    mixed, d_qkv, column_qkv = attention(qkv, cosine, sine, docs, d_mixed)
    part_proj = times_tokens(mixed, g)
    part_qkv = times_tokens(first, d_qkv)
    d_first = times_rows(d_qkv, w_qkv)

    branches = jnp.dot(act, w_down, preferred_element_type=F32) + jnp.dot(mixed, w_proj, preferred_element_type=F32)
    value_own = inputs.astype(F32)
    layer_out = lay.reduce_tokens(branches) + value_own + b_proj + b_down

    edge = lay.reduce_tokens(d_first * a_gain + d_second * f_gain)
    center_own = value_own - jnp.mean(value_own, axis=-1, keepdims=True)
    scale_own = lax.rsqrt(jnp.mean(center_own * center_own, axis=-1, keepdims=True) + EPS)
    xhat_own = center_own * scale_own
    back = edge - jnp.mean(edge, axis=-1, keepdims=True) - xhat_own * jnp.mean(edge * xhat_own, axis=-1, keepdims=True)
    grad_inputs = cotangent.astype(F32) + back * scale_own

    grad_down = lay.reduce(part_down.reshape(t_two + (unit, width)), lay.t_bits)
    grad_proj = lay.reduce(part_proj.reshape(t_two + (rows, width)), proj_order)
    grad_proj = lay.exchange_heads(grad_proj.astype(BF16)).astype(F32)
    grad_up = lay.reduce(part_up.reshape(two + (rows, hidden)), row_order).reshape(HEADS, rows, hidden)
    grad_up = lay.to_columns(grad_up.astype(BF16)).astype(F32)
    axes = h_axes + t_axes
    grad_up = grad_up.reshape((2, 2, 2, rows) + t_two + (unit,))
    back_axes = [3] + [
        (axes.index(a) if axes.index(a) < 3 else axes.index(a) + 1) for a in range(bits)
    ] + [bits + 1]
    grad_up = grad_up.transpose(back_axes).reshape(rows, -1)
    grad_qkv = lay.reduce(part_qkv.reshape(two + (rows, 3 * HEAD)), row_order).reshape(HEADS, rows, 3 * HEAD)
    grad_qkv = lay.to_columns(grad_qkv.astype(BF16)).astype(F32)
    grad_qkv = grad_qkv.reshape(2, 2, 2, rows, 3, HEAD)
    grad_qkv = grad_qkv.transpose([3, 4] + [heads_at.index(a) for a in (2, 3, 4)] + [5]).reshape(rows, -1)

    column_up = jnp.sum(d_up.astype(F32), axis=0)
    column_out = jnp.sum(cotangent.astype(F32), axis=0)
    spread_up = lax.dynamic_update_slice(jnp.zeros((HEADS, hidden), F32), column_up[None], (here, 0))
    spread_up = spread_up.reshape((2,) * bits + (unit,)).transpose(
        [(axes.index(a)) for a in range(bits)] + [bits]
    )
    spread_qkv = lax.dynamic_update_slice(jnp.zeros((HEADS, 3 * HEAD), F32), column_qkv, (here, 0))
    spread_qkv = spread_qkv.reshape(2, 2, 2, 3, HEAD).transpose([3] + [heads_at.index(a) for a in (2, 3, 4)] + [4])
    sums = [
        jnp.sum(d_first * xhat, axis=0),
        jnp.sum(d_first, axis=0),
        jnp.sum(d_second * xhat, axis=0),
        jnp.sum(d_second, axis=0),
        column_out,
        spread_qkv,
        spread_up,
    ]
    sums = jnp.concatenate([s.reshape(n, -1) for s in sums], axis=1)
    sums = jnp.sum(lax.all_to_all(sums, AXIS, split_axis=0, concat_axis=0, tiled=True), axis=0)
    got, at = [], 0
    for size in [rows] * 5 + [3 * rows, unit]:
        got.append(sums[at : at + size])
        at += size
    return (
        layer_out,
        grad_inputs,
        got[0],
        got[1],
        got[2],
        got[3],
        grad_qkv,
        got[5],
        grad_proj,
        got[4],
        grad_up,
        got[6],
        grad_down,
        got[4],
    )


ZH, ZL, Y, X, CORE = 4, 3, 2, 1, 0
ROWS = (((1,), (1,)), ((), ()))
COST = 0.45e9
FIRSTS = (((0,), (0,)), ((), ()))


def after(values, *done):
    return lax.optimization_barrier(tuple(values) + done)[: len(values)]


def flip(value, bit):
    return lax.ppermute(value, AXIS, [(d, d ^ (1 << bit)) for d in range(lax.axis_size(AXIS))])


def call(body, grid, in_specs, out_specs, out_shape, args, scalars=None, limit=40, us=1.0, aliases=None):
    extra = dict(
        out_shape=out_shape,
        compiler_params=pltpu.CompilerParams(vmem_limit_bytes=limit * 1024 * 1024),
        cost_estimate=pl.CostEstimate(flops=int(us * COST), bytes_accessed=1024, transcendentals=0),
        input_output_aliases=aliases or {},
    )
    if scalars is None:
        return pl.pallas_call(body, grid=grid, in_specs=in_specs, out_specs=out_specs, **extra)(*args)
    spec = pltpu.PrefetchScalarGridSpec(num_scalar_prefetch=1, grid=grid, in_specs=in_specs, out_specs=out_specs)
    return pl.pallas_call(body, grid_spec=spec, **extra)(scalars, *args)


def shape(dims, dtype):
    return jax.ShapeDtypeStruct(dims, dtype)


def bits_of(number, count):
    return [(number >> (count - 1 - i)) & 1 for i in range(count)]


def order_columns(value, mine):
    count, width = value.shape
    wide = width // 16

    def body(mine_ref, x_ref, o_ref):
        for j in range(16):
            xr, zr, b, c = bits_of(j, 4)
            source = (zr ^ mine_ref[0]) * 8 + b * 4 + c * 2 + (xr ^ mine_ref[1])
            o_ref[:, j * wide : (j + 1) * wide] = x_ref[:, pl.ds(pl.multiple_of(source * wide, wide), wide)]

    block = pl.BlockSpec((count, width), lambda i, s: (0, 0))
    return call(body, (1,), [block], block, shape((count, width), value.dtype), (value,), mine)


def split_columns(up_weight, qkv_weight):
    rows, ff = up_weight.shape
    unit = ff // 32
    hidden = 4 * unit

    def body(u_ref, q_ref, o_ref):
        for h in range(8):
            zl, y, c = bits_of(h, 3)
            for t in range(4):
                zh, x = bits_of(t, 2)
                e = zh * 16 + zl * 8 + y * 4 + x * 2 + c
                o_ref[h, :, t * unit : (t + 1) * unit] = u_ref[:, e * unit : (e + 1) * unit]
            head = c * 4 + zl * 2 + y
            for k in range(3):
                at = (k * HEADS + head) * HEAD
                o_ref[h, :, hidden + k * HEAD : hidden + (k + 1) * HEAD] = q_ref[:, at : at + HEAD]

    def block(*dims):
        return pl.BlockSpec(dims, lambda i: (0,) * len(dims))

    return call(
        body,
        (1,),
        [block(rows, ff), block(rows, 3 * HEADS * HEAD)],
        block(8, rows, hidden + 3 * HEAD),
        shape((8, rows, hidden + 3 * HEAD), BF16),
        (up_weight, qkv_weight),
    )


def join_up(parts):
    _, rows, hidden = parts.shape
    unit = hidden // 4

    def body(p_ref, o_ref):
        for h in range(8):
            zl, y, c = bits_of(h, 3)
            for t in range(4):
                zh, x = bits_of(t, 2)
                e = zh * 16 + zl * 8 + y * 4 + x * 2 + c
                o_ref[:, e * unit : (e + 1) * unit] = p_ref[h, :, t * unit : (t + 1) * unit].astype(F32)

    return call(
        body,
        (1,),
        [pl.BlockSpec(parts.shape, lambda i: (0, 0, 0))],
        pl.BlockSpec((rows, 8 * hidden), lambda i: (0, 0)),
        shape((rows, 8 * hidden), F32),
        (parts,),
    )


def join_qkv(parts):
    _, rows, _ = parts.shape

    def body(p_ref, o_ref):
        for h in range(8):
            zl, y, c = bits_of(h, 3)
            head = c * 4 + zl * 2 + y
            for k in range(3):
                at = (k * HEADS + head) * HEAD
                o_ref[:, at : at + HEAD] = p_ref[h, :, k * HEAD : (k + 1) * HEAD].astype(F32)

    return call(
        body,
        (1,),
        [pl.BlockSpec(parts.shape, lambda i: (0, 0, 0))],
        pl.BlockSpec((rows, 3 * HEADS * HEAD), lambda i: (0, 0)),
        shape((rows, 3 * HEADS * HEAD), F32),
        (parts,),
    )


def prepare(small, place, freq, sign, rows, unit, count):
    n, _, lanes = small.shape
    width = n * rows
    up_at, gains_at = count // lanes, (count + unit) // lanes
    out_at = gains_at + 2
    qkv_at = out_at + 1

    def body(place_ref, small_ref, f_ref, s_ref, gains_ref, out_ref, up_ref, qkv_ref, docs_ref, cos_ref, sin_ref, all_ref):
        mzh, mx, mzl, my, mc, me = [place_ref[k] for k in range(6)]
        step = pl.program_id(0)

        @pl.when(step == 0)
        def _():
            all_ref[...] = small_ref[...].astype(F32)
            gains_ref[...] = jnp.zeros_like(gains_ref)

            for j in range(16):
                xr, zr, b, c = bits_of(j, 4)
                source = 2 * ((zr ^ mzh) * 8 + b * 4 + c * 2 + (xr ^ mx))
                here = slice(2 * j * rows, 2 * (j + 1) * rows)
                left, right = all_ref[source], all_ref[source + 1]
                for k in range(4):
                    at, part = gains_at + k // 2, slice(k % 2 * rows, (k % 2 + 1) * rows)
                    gains_ref[k : k + 1, here] = jnp.concatenate([left[at : at + 1, part], right[at : at + 1, part]], axis=1)
                left, right = [v[:, :rows] + v[:, rows:] for v in (all_ref[2 * j, out_at : out_at + 1], all_ref[2 * j + 1, out_at : out_at + 1])]
                out_ref[:, here] = jnp.concatenate([left, right], axis=1)
            for t in range(4):
                zh, x = bits_of(t, 2)
                device = zh * 16 + mzl * 8 + my * 4 + x * 2 + mc
                mine_up = all_ref[device]
                for k in range(unit // lanes):
                    up_ref[:, t * unit + k * lanes : t * unit + (k + 1) * lanes] = mine_up[up_at + k : up_at + k + 1]
            head = mc * 4 + mzl * 2 + my
            for k in range(3 * HEAD // rows):
                chunk = (k // (HEAD // rows) * HEADS + head) * (HEAD // rows) + k % (HEAD // rows)
                third = all_ref[chunk // 3]
                part = lax.rem(chunk, 3)
                first, last = third[qkv_at : qkv_at + 1], third[qkv_at + 1 : qkv_at + 2]
                qkv_ref[:, k * rows : (k + 1) * rows] = jnp.where(
                    part == 0, first[:, :rows], jnp.where(part == 1, first[:, rows:], last[:, :rows])
                )

        other = me ^ (((step & 1) << ZL) | (((step >> 1) & 1) << Y) | (((step >> 2) & 1) << CORE))
        held = all_ref[other]
        docs = jnp.concatenate([held[k : k + 1] for k in range(count // lanes)], axis=1)
        docs_ref[0] = docs
        across = jnp.broadcast_to(docs, (count, count))
        here = lax.broadcasted_iota(jnp.int32, (count, count), 0)
        there = lax.broadcasted_iota(jnp.int32, (count, count), 1)
        earlier = (across == across.T) & (there < here)
        position = jnp.sum(earlier.astype(F32), axis=1, keepdims=True)
        angle = position * f_ref[...]
        cos_ref[...] = jnp.cos(angle)
        sin_ref[...] = jnp.sin(angle) * s_ref[...]

    def whole(*dims):
        return pl.BlockSpec(dims, lambda i, s: (0, 0))

    block = pl.BlockSpec((count, lanes), lambda i, s: (i, 0))
    return pl.pallas_call(
        body,
        grid_spec=pltpu.PrefetchScalarGridSpec(
            num_scalar_prefetch=1,
            grid=(8,),
            in_specs=[pl.BlockSpec(small.shape, lambda i, s: (0, 0, 0)), whole(1, lanes), whole(1, lanes)],
            out_specs=[
                whole(8, width),
                whole(1, width),
                whole(1, 4 * unit),
                whole(1, 3 * HEAD),
                pl.BlockSpec((1, 1, count), lambda i, s: (i, 0, 0)),
                block,
                block,
            ],
            scratch_shapes=[pltpu.VMEM(small.shape, F32)],
        ),
        out_shape=[
            shape((8, width), F32),
            shape((1, width), F32),
            shape((1, 4 * unit), F32),
            shape((1, 3 * HEAD), F32),
            shape((8, 1, count), F32),
            shape((8 * count, lanes), F32),
            shape((8 * count, lanes), F32),
        ],
        compiler_params=pltpu.CompilerParams(vmem_limit_bytes=40 * 1024 * 1024),
        cost_estimate=pl.CostEstimate(flops=int(COST), bytes_accessed=1024, transcendentals=0),
    )(place, small, freq, sign)


def join(pieces):
    count, width = pieces[0].shape
    blocks = len(pieces)

    def body(*refs):
        ins, out, held, sems_in, sems_out = refs[:blocks], refs[blocks], *refs[blocks + 1 :]

        def copy_in(k):
            return pltpu.make_async_copy(ins[k], held.at[k], sems_in.at[k])

        def copy_out(k):
            return pltpu.make_async_copy(held.at[k], out.at[pl.ds(k * count, count)], sems_out.at[k])

        for k in range(blocks):
            copy_in(k).start()
        for k in range(blocks):
            copy_in(k).wait()
            copy_out(k).start()
        for k in range(blocks):
            copy_out(k).wait()

    some = pl.BlockSpec(memory_space=pl.ANY)
    return pl.pallas_call(
        body,
        grid=(1,),
        in_specs=[some] * blocks,
        out_specs=some,
        out_shape=shape((blocks * count, width), pieces[0].dtype),
        scratch_shapes=[pltpu.VMEM((blocks, count, width), pieces[0].dtype)] + [pltpu.SemaphoreType.DMA((blocks,))] * 2,
        compiler_params=pltpu.CompilerParams(vmem_limit_bytes=40 * 1024 * 1024),
        cost_estimate=pl.CostEstimate(flops=int(4 * COST), bytes_accessed=1024, transcendentals=0),
    )(*pieces)


def join_heads(pieces, mine):
    rows, width = pieces[0].shape

    def body(mine_ref, *refs):
        for k, (xr, zr) in enumerate([(0, 0), (0, 1), (1, 0), (1, 1)]):
            at = ((mine_ref[1] ^ xr) * 2 + (mine_ref[0] ^ zr)) * rows
            refs[4][pl.ds(pl.multiple_of(at, rows), rows), :] = refs[k][...]

    return call(
        body,
        (1,),
        [pl.BlockSpec((rows, width), lambda i, s: (0, 0))] * 4,
        pl.BlockSpec((4 * rows, width), lambda i, s: (0, 0)),
        shape((4 * rows, width), BF16),
        tuple(pieces),
        mine,
    )


def norms(halves, gains, count):
    tokens, width = halves[0].shape
    each = tokens // count
    blocks = 2 * each

    def body(v_ref, a_ref, b_ref, first_ref, second_ref, stats_ref, x_buf, first_buf, second_buf, sems_in, sems_first, sems_second):
        def copy_in(k):
            half = (a_ref, b_ref)[k // each]
            return pltpu.make_async_copy(half.at[pl.ds(k % each * count, count)], x_buf.at[k % 2], sems_in.at[k % 2])

        def copy_first(k):
            return pltpu.make_async_copy(first_buf.at[k % 2], first_ref.at[pl.ds(k * count, count)], sems_first.at[k % 2])

        def copy_second(k):
            return pltpu.make_async_copy(second_buf.at[k % 2], second_ref.at[pl.ds(k * count, count)], sems_second.at[k % 2])

        copy_in(0).start()
        for k in range(blocks):
            slot = k % 2
            copy_in(k).wait()
            if k + 1 < blocks:
                copy_in(k + 1).start()
            if k >= 2:
                copy_first(k - 2).wait()
                copy_second(k - 2).wait()
            value = x_buf[slot].astype(F32)
            mean = jnp.mean(value, axis=-1, keepdims=True)
            center = value - mean
            scale = lax.rsqrt(jnp.mean(center * center, axis=-1, keepdims=True) + EPS)
            xhat = center * scale
            first_buf[slot] = (xhat * v_ref[0:1, :] + v_ref[1:2, :]).astype(BF16)
            second_buf[slot] = (xhat * v_ref[2:3, :] + v_ref[3:4, :]).astype(BF16)
            lane = lax.broadcasted_iota(jnp.int32, (count, 128), 1)
            stats_ref[k * count : (k + 1) * count, :] = jnp.where(lane == 0, mean, scale)
            copy_first(k).start()
            copy_second(k).start()
        for k in (blocks - 2, blocks - 1):
            copy_first(k).wait()
            copy_second(k).wait()

    some = pl.BlockSpec(memory_space=pl.ANY)
    return pl.pallas_call(
        body,
        grid=(1,),
        in_specs=[pl.BlockSpec((8, width), lambda i: (0, 0)), some, some],
        out_specs=[some, some, pl.BlockSpec((2 * tokens, 128), lambda i: (0, 0))],
        out_shape=[shape((2 * tokens, width), BF16)] * 2 + [shape((2 * tokens, 128), F32)],
        scratch_shapes=[pltpu.VMEM((2, count, width), BF16)] * 3 + [pltpu.SemaphoreType.DMA((2,))] * 3,
        compiler_params=pltpu.CompilerParams(vmem_limit_bytes=40 * 1024 * 1024),
        cost_estimate=pl.CostEstimate(flops=int(12 * COST), bytes_accessed=1024, transcendentals=0),
    )(gains, *halves)


def feed_up(second, w_up, bias, tile=512):
    tokens, width = second.shape
    deep, hidden = w_up[0].shape

    def body(s_ref, *refs):
        b_ref, act_ref, slope_ref = refs[4:]
        up = b_ref[...]
        for k in range(4):
            up = up + jnp.dot(s_ref[:, k * deep : (k + 1) * deep], refs[k][...], preferred_element_type=F32)
        phi_sum = 0.5 * (1.0 + lax.erf(up * (0.5**0.5)))
        act_ref[...] = (up * phi_sum).astype(BF16)
        slope_ref[...] = phi_sum + up * jnp.exp(-0.5 * up * up) * 0.3989422804014327

    block = pl.BlockSpec((tile, hidden), lambda i: (i, 0))
    return call(
        body,
        (tokens // tile,),
        [pl.BlockSpec((tile, width), lambda i: (i, 0))]
        + [pl.BlockSpec((deep, hidden), lambda i: (0, 0))] * 4
        + [pl.BlockSpec((1, hidden), lambda i: (0, 0))],
        [block, block],
        [shape((tokens, hidden), BF16), shape((tokens, hidden), F32)],
        (second, *w_up, bias),
        us=16,
    )


def either(steps, first_half, tile, width):
    half = steps // 2

    def spec(low):
        return pl.BlockSpec((tile, width), lambda i: (jnp.minimum(i, half - 1) if low else jnp.maximum(i - half, 0), 0))

    return [spec(first_half), spec(not first_half)]


def join_units(pieces, mine):
    unit, width = pieces[0].shape

    def body(mine_ref, *refs):
        for k, (zr, xr) in enumerate([(0, 0), (0, 1), (1, 0), (1, 1)]):
            at = ((mine_ref[0] ^ zr) * 2 + (mine_ref[1] ^ xr)) * unit
            refs[4][pl.ds(pl.multiple_of(at, unit), unit), :] = refs[k][...]

    return call(
        body,
        (1,),
        [pl.BlockSpec(p.shape, lambda i, s: (0, 0)) for p in pieces],
        pl.BlockSpec((4 * unit, width), lambda i, s: (0, 0)),
        shape((4 * unit, width), BF16),
        tuple(pieces),
        mine,
        us=3,
    )


def feed_back(g, w_down, slope, tile=512):
    half, width = g[0].shape
    steps = 2 * half // tile
    hidden = slope.shape[1]

    def body(ga_ref, gb_ref, w_ref, slope_ref, d_ref, column_ref):
        step = pl.program_id(0)

        @pl.when(step == 0)
        def _():
            column_ref[...] = jnp.zeros_like(column_ref)

        def work(g_ref):
            d_act = lax.dot_general(g_ref[...], w_ref[...], ROWS, preferred_element_type=F32)
            d_up = (d_act * slope_ref[...]).astype(BF16)
            d_ref[...] = d_up
            column_ref[...] += jnp.sum(d_up.astype(F32), axis=0, keepdims=True)

        pl.when(step < steps // 2)(lambda: work(ga_ref))
        pl.when(step >= steps // 2)(lambda: work(gb_ref))

    block = pl.BlockSpec((tile, hidden), lambda i: (i, 0))
    return call(
        body,
        (steps,),
        either(steps, True, tile, width) + [pl.BlockSpec((hidden, width), lambda i: (0, 0)), block],
        [block, pl.BlockSpec((1, hidden), lambda i: (0, 0))],
        [shape((2 * half, hidden), BF16), shape((1, hidden), F32)],
        (*g, w_down, slope),
        us=14,
    )


def weight_grad(left, right, mine, source, us=13):
    tokens, width = left.shape
    wide = right[0].shape[1]
    tile = width // 4
    count = len(right)

    def body(mine_ref, l_ref, *refs):
        part = lax.dot_general(l_ref[: tokens // count], refs[0][...], FIRSTS, preferred_element_type=F32)
        if count == 2:
            part = part + lax.dot_general(l_ref[tokens // 2 :], refs[1][...], FIRSTS, preferred_element_type=F32)
        for k, out in enumerate(refs[count:]):

            @pl.when(pl.program_id(0) == k)
            def _():
                out[...] = part.astype(out.dtype)

    return call(
        body,
        (4,),
        [pl.BlockSpec((tokens, tile), lambda i, s: (0, source(i, s)))]
        + [pl.BlockSpec(r.shape, lambda i, s: (0, 0)) for r in right],
        [pl.BlockSpec((tile, wide), lambda i, s: (0, 0))] * 4,
        [shape((tile, wide), BF16)] * 2 + [shape((tile, wide), F32)] * 2,
        (left, *right),
        mine,
        us=us,
    )


def head_grad(mixed, g, mine):
    tokens, head = mixed.shape
    width = g[0].shape[1]

    def body(mine_ref, l_ref, ga_ref, gb_ref, sent_ref, kept_ref):
        part = lax.dot_general(l_ref[: tokens // 2], ga_ref[...], FIRSTS, preferred_element_type=F32)
        part = part + lax.dot_general(l_ref[tokens // 2 :], gb_ref[...], FIRSTS, preferred_element_type=F32)
        upper, lower = part[: head // 2], part[head // 2 :]
        own = mine_ref[1] == 0
        sent_ref[...] = jnp.where(own, lower, upper).astype(BF16)
        kept_ref[...] = jnp.where(own, upper, lower)

    return call(
        body,
        (2,),
        [pl.BlockSpec((tokens, head), lambda i, s: (0, 0))]
        + [pl.BlockSpec((tokens // 2, width // 2), lambda i, s: (0, i))] * 2,
        [pl.BlockSpec((head // 2, width // 2), lambda i, s: (0, i))] * 2,
        [shape((head // 2, width), BF16), shape((head // 2, width), F32)],
        (mixed, *g),
        mine,
        us=5,
    )


def fold_tokens(kept, got):
    count, width = kept.shape
    tile = count // 4

    def body(k_ref, *refs):
        first_ref, second_ref, stays_ref = refs[4:]
        step = pl.program_id(0)
        for j in range(4):

            @pl.when(step == 3 - j)
            def _():
                total = k_ref[...].astype(F32) + refs[j][...].astype(F32)
                out = (stays_ref, stays_ref, second_ref, first_ref)[j]
                out[...] = total.astype(out.dtype)

    fixed = pl.BlockSpec((tile, width), lambda i: (0, 0))
    return call(
        body,
        (4,),
        [pl.BlockSpec((tile, width), lambda i: (3 - i, 0))] + [fixed] * 4,
        [fixed, fixed, pl.BlockSpec((tile, width), lambda i: (jnp.minimum(3 - i, 1), 0))],
        [shape((tile, width), BF16)] * 2 + [shape((2 * tile, width), F32)],
        (kept,) + tuple(got),
        us=5,
    )


def add_half(kept, got, rows, at):
    width = kept.shape[1]

    def body(k_ref, g_ref, o_ref):
        o_ref[...] = (k_ref[...] + g_ref[...].astype(F32)).astype(BF16)

    fixed = pl.BlockSpec((rows, width), lambda i: (0, 0))
    return call(
        body, (1,), [pl.BlockSpec((rows, width), lambda i: (at, 0)), fixed], fixed, shape((rows, width), BF16), (kept, got)
    )


def attend(first, w_qkv, b_qkv, g, w_proj, cosine, sine, docs):
    tokens, width = first.shape
    rows, _, count = docs.shape
    deep = w_qkv[0].shape[0]
    lanes = cosine.shape[1]
    half = ROT // 2
    scale = HEAD ** (-0.5)

    def body(f_ref, w0_ref, w1_ref, w2_ref, w3_ref, b_ref, ga_ref, gb_ref, p_ref, cos_ref, sin_ref, row_ref, mixed_ref, d_qkv_ref, column_ref):
        step = pl.program_id(0)

        @pl.when(step == 0)
        def _():
            column_ref[...] = jnp.zeros_like(column_ref)

        def work(g_ref):
            cos, sin = cos_ref[...], sin_ref[...]
            lane = lax.broadcasted_iota(jnp.int32, cos.shape, 1)

            def turn(v, sign):
                front = v[:, :lanes]
                other = jnp.where(lane < half, pltpu.roll(front, lanes - half, 1), pltpu.roll(front, half, 1))
                return jnp.concatenate([front * cos + sign * (other * sin), v[:, lanes:]], axis=1)

            qkv = b_ref[...]
            for k, w_ref in enumerate((w0_ref, w1_ref, w2_ref, w3_ref)):
                qkv = qkv + jnp.dot(f_ref[:, k * deep : (k + 1) * deep], w_ref[...], preferred_element_type=F32)
            d_mixed = lax.dot_general(g_ref[...], p_ref[...], ROWS, preferred_element_type=F32).astype(BF16)
            rq = turn(qkv[:, :HEAD], 1.0).astype(BF16)
            rk = turn(qkv[:, HEAD : 2 * HEAD], 1.0).astype(BF16)
            rv = qkv[:, 2 * HEAD :].astype(BF16)
            here = lax.broadcasted_iota(jnp.int32, (count, count), 0)
            there = lax.broadcasted_iota(jnp.int32, (count, count), 1)
            across = jnp.broadcast_to(row_ref[0], (count, count))
            allowed = (across == across.T) & (there <= here)
            raw = lax.dot_general(rq, rk, ROWS, preferred_element_type=F32)
            scores = jnp.where(allowed, raw * scale, MASKED)
            expo = jnp.exp(scores - jnp.max(scores, axis=1, keepdims=True))
            probs = expo / jnp.sum(expo, axis=1, keepdims=True)
            weights = probs.astype(BF16)
            mixed_ref[...] = jnp.dot(weights, rv, preferred_element_type=F32).astype(BF16)
            d_prob = lax.dot_general(d_mixed, rv, ROWS, preferred_element_type=F32)
            d_score = probs * (d_prob - jnp.sum(probs * d_prob, axis=1, keepdims=True))
            d_raw = (d_score * scale).astype(BF16)
            d_rq = jnp.dot(d_raw, rk, preferred_element_type=F32)
            d_rk = lax.dot_general(d_raw, rq, FIRSTS, preferred_element_type=F32)
            d_rv = lax.dot_general(weights, d_mixed, FIRSTS, preferred_element_type=F32)
            d_qkv = jnp.concatenate([turn(d_rq, -1.0), turn(d_rk, -1.0), d_rv], axis=1).astype(BF16)
            d_qkv_ref[...] = d_qkv
            column_ref[...] += jnp.sum(d_qkv.astype(F32), axis=0, keepdims=True)

        pl.when(step < rows // 2)(lambda: work(ga_ref))
        pl.when(step >= rows // 2)(lambda: work(gb_ref))

    def row(*dims):
        return pl.BlockSpec(dims, lambda i: (i, 0))

    def whole(*dims):
        return pl.BlockSpec(dims, lambda i: (0, 0))

    return call(
        body,
        (rows,),
        [
            row(count, width),
            *([whole(deep, 3 * HEAD)] * 4),
            whole(1, 3 * HEAD),
            *either(rows, True, count, width),
            whole(HEAD, width),
            row(count, lanes),
            row(count, lanes),
            pl.BlockSpec((1, 1, count), lambda i: (i, 0, 0)),
        ],
        [row(count, HEAD), row(count, 3 * HEAD), whole(1, 3 * HEAD)],
        [shape((tokens, HEAD), BF16), shape((tokens, 3 * HEAD), BF16), shape((1, 3 * HEAD), F32)],
        (first, *w_qkv, b_qkv, *g, w_proj, cosine, sine, docs),
        us=17,
    )


def branch_sum(act, w_down, mixed, w_proj, tile=512, block=256):
    tokens, hidden = act.shape
    width = w_down.shape[1]
    steps = tokens // tile
    sent = steps // 2
    each = tile // block
    blocks = sent * each

    def body(a_ref, w_ref, m_ref, p_ref, *outs):
        part = jnp.dot(a_ref[...], w_ref[...], preferred_element_type=F32)
        part = (part + jnp.dot(m_ref[...], p_ref[...], preferred_element_type=F32)).astype(BF16)
        outs[blocks][...] = part
        step = pl.program_id(0)
        for k in range(sent):

            @pl.when(step == k)
            def _():
                for j in range(each):
                    outs[k * each + j][...] = part[j * block : (j + 1) * block]

    def turned(i):
        return (lax.rem(i + sent, steps), 0)

    fixed = pl.BlockSpec((block, width), lambda i: (0, 0))
    return call(
        body,
        (steps,),
        [
            pl.BlockSpec((tile, hidden), turned),
            pl.BlockSpec((hidden, width), lambda i: (0, 0)),
            pl.BlockSpec((tile, HEAD), turned),
            pl.BlockSpec((HEAD, width), lambda i: (0, 0)),
        ],
        [fixed] * blocks + [pl.BlockSpec((tile, width), lambda i: (jnp.maximum(i - sent, 0), 0))],
        [shape((block, width), BF16)] * blocks + [shape((tokens // 2, width), BF16)],
        (act, w_down, mixed, w_proj),
        us=16,
    )


def edge_sum(d_up, w_up, d_qkv, w_qkv, x, stats, gains, tile=256):
    tokens, hidden = d_up.shape
    deep = w_up[0].shape[0]
    width = 4 * deep
    steps = tokens // tile
    sent = steps // 2

    def body(du_ref, dq_ref, xa_ref, xb_ref, stats_ref, v_ref, *refs):
        outs = refs[8:]
        sums_ref = outs[sent + 1]
        step = pl.program_id(0)

        @pl.when(step == 0)
        def _():
            sums_ref[...] = jnp.zeros_like(sums_ref)

        for k in range(4):
            part = slice(k * deep, (k + 1) * deep)
            d_second = lax.dot_general(du_ref[...], refs[k][...], ROWS, preferred_element_type=F32)
            d_first = lax.dot_general(dq_ref[...], refs[4 + k][...], ROWS, preferred_element_type=F32)
            x = jnp.where(step < sent, xb_ref[:, part], xa_ref[:, part])
            xhat = (x.astype(F32) - stats_ref[:, 0:1]) * stats_ref[:, 1:2]
            outs[sent][:, part] = (d_first * v_ref[0:1, part] + d_second * v_ref[2:3, part]).astype(BF16)
            sums_ref[0:1, part] += jnp.sum(d_first * xhat, axis=0, keepdims=True)
            sums_ref[1:2, part] += jnp.sum(d_first, axis=0, keepdims=True)
            sums_ref[2:3, part] += jnp.sum(d_second * xhat, axis=0, keepdims=True)
            sums_ref[3:4, part] += jnp.sum(d_second, axis=0, keepdims=True)

        for j in range(sent):

            @pl.when(step == j)
            def _():
                outs[j][...] = outs[sent][...]

    def turned(i):
        return (lax.rem(i + sent, steps), 0)

    def whole(*dims):
        return pl.BlockSpec(dims, lambda i: (0, 0))

    return call(
        body,
        (steps,),
        [
            pl.BlockSpec((tile, hidden), turned),
            pl.BlockSpec((tile, 3 * HEAD), turned),
            *either(steps, False, tile, width),
            pl.BlockSpec((tile, 128), turned),
            whole(8, width),
        ]
        + [whole(deep, hidden)] * 4
        + [whole(deep, 3 * HEAD)] * 4,
        [whole(tile, width)] * sent
        + [pl.BlockSpec((tile, width), lambda i: (jnp.maximum(i - sent, 0), 0)), whole(8, width)],
        [shape((tile, width), BF16)] * sent + [shape((tokens // 2, width), BF16), shape((8, width), F32)],
        (d_up, d_qkv, *x, stats, gains, *w_up, *w_qkv),
        us=28,
        limit=48,
    )


def total(parts, rows):
    width = parts[0].shape[1]

    def body(*refs):
        value = refs[0][...].astype(F32)
        for ref in refs[1:-1]:
            value = value + ref[...].astype(F32)
        refs[-1][...] = value

    return call(
        body,
        (1,),
        [pl.BlockSpec((min(rows, p.shape[0]), width), lambda i: (0, 0)) for p in parts],
        pl.BlockSpec((rows, width), lambda i: (0, 0)),
        shape((rows, width), F32),
        tuple(parts),
        us=3,
    )


def finish(edge_k, edge_g0, edge_got, x0, g, mine):
    count, width = x0.shape
    wide = width // 16

    def body(mine_ref, k_ref, a_ref, b_ref, x_ref, g_ref, o_ref):
        edge = k_ref[...] + a_ref[...].astype(F32) + b_ref[...].astype(F32)
        value = x_ref[...].astype(F32)
        center = value - jnp.mean(value, axis=-1, keepdims=True)
        scale = lax.rsqrt(jnp.mean(center * center, axis=-1, keepdims=True) + EPS)
        xhat = center * scale
        back = edge - jnp.mean(edge, axis=-1, keepdims=True) - xhat * jnp.mean(edge * xhat, axis=-1, keepdims=True)
        back = back * scale
        for j in range(16):
            xr, zr, b, c = bits_of(j, 4)
            source = (zr ^ mine_ref[0]) * 8 + b * 4 + c * 2 + (xr ^ mine_ref[1])
            place = pl.ds(pl.multiple_of(source * wide, wide), wide)
            o_ref[:, place] = g_ref[:, place].astype(F32) + back[:, j * wide : (j + 1) * wide]

    tile = count // 2
    block = pl.BlockSpec((tile, width), lambda i, s: (i, 0))
    return call(
        body, (2,), [block] * 5, block, shape((count, width), F32), (edge_k, edge_g0, edge_got, x0, g), mine, us=5
    )


def local_tuned(
    inputs,
    doc_ids,
    attn_gain,
    attn_shift,
    ffn_gain,
    ffn_shift,
    qkv_weight,
    qkv_bias,
    proj_weight,
    proj_bias,
    up_weight,
    up_bias,
    down_weight,
    down_bias,
    cotangent,
):
    n = lax.axis_size(AXIS)
    lay = Layout(n)
    count, width = inputs.shape
    rows = width // n
    unit = up_bias.shape[0]
    hidden = 4 * unit
    me = lax.axis_index(AXIS)
    mzh, mx = lay.mine(ZH), lay.mine(X)
    mine = jnp.stack([mzh, mx]).astype(jnp.int32)

    cols = split_columns(up_weight, qkv_weight)
    (x0,) = after((inputs,), cols)
    x0 = order_columns(x0, mine)
    down_z = flip(down_weight, ZH)
    down_x = flip(down_weight, X)
    cols = lay.to_columns(cols)
    x1 = flip(x0, ZL)
    x2 = flip(x0, Y)
    g2 = flip(cotangent, Y)
    small = jnp.concatenate(
        [doc_ids[0].astype(BF16), up_bias, attn_gain, attn_shift, ffn_gain, ffn_shift, proj_bias, down_bias, qkv_bias]
    )
    small = jnp.pad(small, (0, 16 * 128 - small.shape[0])).reshape(16, 128)
    small = jnp.broadcast_to(small[None], (n, 16, 128))

    cols, down_z, down_x, x1, x2, g2, small, g0 = after((cols, down_z, down_x, x1, x2, g2, small, cotangent))
    up_cols, qkv_cols = cols[:, :, :hidden], cols[:, :, hidden:]
    small = lax.all_to_all(small, AXIS, split_axis=0, concat_axis=0, tiled=True)
    up_z = flip(up_cols, ZH)
    up_x = flip(up_cols, X)
    g1 = flip(g0, ZL)
    x3 = flip(x1, Y)
    down_xz = flip(down_z, X)

    freq = 10000.0 ** (-2.0 * np.arange(ROT // 2, dtype=np.float32) / ROT)
    rest = np.zeros(128 - ROT, np.float32)
    freq = jnp.asarray(np.concatenate([freq, freq, rest])[None], F32)
    sign = jnp.asarray(np.concatenate([np.full(ROT // 2, -1.0), np.full(ROT // 2, 1.0), rest])[None], F32)
    bit_of = jnp.stack([lay.mine(b) for b in (ZH, X, ZL, Y, CORE)] + [me]).astype(jnp.int32)
    here = lay.mine(ZL) * 4 + lay.mine(Y) * 2 + lay.mine(CORE)

    def restore(v):
        v = v.reshape(v.shape[0], 2, 2, 4, 2 * rows).transpose(0, 2, 3, 1, 4)
        v = jnp.where(mzh == 1, v[:, ::-1], v)
        v = jnp.where(mx == 1, v[:, :, :, ::-1], v)
        return v.reshape(v.shape[0], width)

    up_z, up_x, x1, x2, x3, g1, down_xz, small, qkv_cols, proj0 = after(
        (up_z, up_x, x1, x2, x3, g1, down_xz, small, qkv_cols, proj_weight)
    )
    gains, b_out, b_up, b_qkv, docs, cosine, sine = prepare(small, bit_of, freq, sign, rows, unit, count)
    xa = join([x0, x1, x2, x3])
    xb = flip(xa, CORE)
    up_xz = flip(up_z, X)
    g3 = flip(g1, Y)
    proj0 = lay.exchange_heads(proj0)
    w_down = join_units([down_weight, down_x, down_z, down_xz], mine)
    gains, g0, g1, g2, g3, qkv_cols, proj0, up_xz, xb, w_down = after(
        (gains, g0, g1, g2, g3, qkv_cols, proj0, up_xz, xb, w_down)
    )
    ga = join([g0, g1, g2, g3])
    gb = flip(ga, CORE)
    qkv_z = flip(qkv_cols, ZH)
    qkv_x = flip(qkv_cols, X)
    proj_z = flip(proj0, ZH)
    proj_x = flip(proj0, X)
    first, second, stats = norms([xa, xb], gains, count)
    w_up = [v.reshape(-1, hidden) for v in (up_cols, up_z, up_x, up_xz)]
    act, slope = feed_up(second, w_up, b_up)
    act, qkv_z, qkv_x, proj_x, gb = after((act, qkv_z, qkv_x, proj_x, gb))
    g = [ga, gb]
    x = [xa, xb]
    qkv_xz = flip(qkv_z, X)

    def hidden_block(step, s):
        return (s[0] ^ (1 - lax.rem(step, 2))) * 2 + (s[1] ^ jnp.where(step < 2, 1, 0))

    def feature_block(step, s):
        return 3 - step

    down_s1, down_s0, down_k1, down_k0 = weight_grad(act, g, mine, hidden_block, us=15)
    down_g1 = flip(down_s1, X)
    slope, qkv_xz, down_k1, proj_z = after((slope, qkv_xz, down_k1, proj_z))
    proj_xz = flip(proj_z, X)
    d_up, column_up = feed_back(g, w_down, slope)
    d_up, down_s0 = after((d_up, down_s0))
    down_g0 = flip(down_s0, X)
    up_s1, up_s0, up_k1, up_k0 = weight_grad(second, [d_up], mine, feature_block, us=12)
    up_g1 = flip(up_s1, X)

    down_g1, up_k1, proj_xz = after((down_g1, up_k1, proj_xz))
    down_sent = add_half(down_k1, down_g1, unit, 0)
    down_got = flip(down_sent, ZH)
    w_proj = join_heads([proj0, proj_z, proj_x, proj_xz], mine)
    w_qkv = [v.reshape(-1, 3 * HEAD) for v in (qkv_cols, qkv_z, qkv_x, qkv_xz)]
    (first_,) = after((first,), down_sent)
    mixed, d_qkv, column_qkv = attend(first_, w_qkv, b_qkv, g, w_proj, cosine, sine, docs)
    act, mixed, d_qkv, down_g0 = after((act, mixed, d_qkv, down_g0))
    *out_s, out_k = branch_sum(act, w_down, mixed, w_proj)
    out_g = [flip(v, CORE) for v in out_s]
    d_qkv, out_k, up_g1, up_s0, down_got = after((d_qkv, out_k, up_g1, up_s0, down_got))
    up_g0 = flip(up_s0, X)
    up_sent = add_half(up_k1, up_g1, up_k1.shape[0], 0)
    up_got = flip(up_sent, ZH)
    *out_g, out_k = after((*out_g, out_k), up_sent)
    out_s1, out_s0, out_k = fold_tokens(out_k, out_g)
    out_g1 = flip(out_s1, Y)
    out_g0 = flip(out_s0, Y)
    d_qkv, out_k = after((d_qkv, out_k))
    qkv_s1, qkv_s0, qkv_k1, qkv_k0 = weight_grad(first, [d_qkv], mine, feature_block, us=10)
    qkv_g1 = flip(qkv_s1, X)
    mixed, qkv_k1 = after((mixed, qkv_k1))
    proj_s, proj_k = head_grad(mixed, g, mine)
    out_g1, out_k, up_g0, proj_s, qkv_s0 = after((out_g1, out_k, up_g0, proj_s, qkv_s0))
    qkv_g0 = flip(qkv_s0, X)
    proj_g = flip(proj_s, X)
    out_sent = add_half(out_k, out_g1, count, 1)
    out_got = flip(out_sent, ZL)

    d_up, d_qkv = after((d_up, d_qkv), out_sent)
    *edge_s, edge_k, sums = edge_sum(d_up, w_up, d_qkv, w_qkv, x, stats, gains)

    *edge_s, edge_k, qkv_g1, up_got, out_g0, sums = after((*edge_s, edge_k, qkv_g1, up_got, out_g0, sums))
    edge_g = [flip(v, CORE) for v in edge_s]
    qkv_sent = add_half(qkv_k1, qkv_g1, qkv_k1.shape[0], 0)
    qkv_got = flip(qkv_sent, ZH)
    up_got, edge_k = after((up_got, edge_k), qkv_sent)
    up_sum = (up_k0 + up_g0.astype(F32) + up_got.astype(F32)).astype(BF16)
    up_back = lay.to_columns(up_sum.reshape(8, rows, hidden))
    edge_k, up_sum, out_got = after((edge_k, up_sum, out_got))
    *edge_g, edge_k = after((*edge_g, edge_k))
    edge_s1, edge_s0, edge_k = fold_tokens(edge_k, edge_g)
    edge_g1 = flip(edge_s1, Y)

    edge_k, sums, column_up, column_qkv = after((edge_k, sums, column_up, column_qkv))
    column_out = jnp.sum(cotangent.astype(F32), axis=0)
    spread_up = lax.dynamic_update_slice(jnp.zeros((HEADS, hidden), F32), column_up, (here, 0))
    spread_up = spread_up.reshape(2, 2, 2, 2, 2, unit).transpose(3, 0, 1, 4, 2, 5)
    spread_qkv = lax.dynamic_update_slice(jnp.zeros((HEADS, 3 * HEAD), F32), column_qkv, (here, 0))
    spread_qkv = spread_qkv.reshape(2, 2, 2, 3, HEAD).transpose(3, 2, 0, 1, 4)
    sums = restore(sums[:4])
    flat = [v.reshape(n, -1) for v in (sums[0], sums[1], sums[2], sums[3], column_out, spread_qkv, spread_up)]
    flat = jnp.concatenate(flat, axis=1)
    flat, up_back = after((flat, up_back))
    sums = lax.all_to_all(flat, AXIS, split_axis=0, concat_axis=0, tiled=True)
    qkv_got, qkv_g0, sums, proj_g, edge_k = after((qkv_got, qkv_g0, sums, proj_g, edge_k))
    qkv_sum = (qkv_k0 + qkv_g0.astype(F32) + qkv_got.astype(F32)).astype(BF16)
    qkv_back = lay.to_columns(qkv_sum.reshape(8, rows, 3 * HEAD))
    proj_sum = (proj_k + proj_g.astype(F32)).reshape(2, rows, width)
    proj_kept = lax.dynamic_index_in_dim(proj_sum, mzh, 0, keepdims=False)
    proj_sent = lax.dynamic_index_in_dim(proj_sum, 1 - mzh, 0, keepdims=False).astype(BF16)
    proj_got = flip(proj_sent, ZH)
    edge_g1, edge_s0, qkv_sum, proj_sent = after((edge_g1, edge_s0, qkv_sum, proj_sent))
    edge_g0 = flip(edge_s0, Y)
    edge_sent = add_half(edge_k, edge_g1, count, 1)
    edge_got = flip(edge_sent, ZL)
    qkv_back, up_back, out_k, down_k0 = after((qkv_back, up_back, out_k, down_k0), edge_sent)
    grad_up = join_up(up_back)
    grad_qkv = join_qkv(qkv_back)
    layer_out = total([inputs, b_out, out_k, out_g0, out_got], count)
    grad_down = total([down_k0, down_g0, down_got], unit)
    proj_got, edge_k, layer_out, grad_down = after((proj_got, edge_k, layer_out, grad_down))
    proj_back = lay.exchange_heads((proj_kept + proj_got.astype(F32)).astype(BF16))
    edge_got, edge_g0, edge_k = after((edge_got, edge_g0, edge_k))
    grad_inputs = finish(edge_k, edge_g0, edge_got, x0, cotangent, mine)
    proj_back, grad_inputs = after((proj_back, grad_inputs))
    grad_proj = proj_back.astype(F32)
    sums = jnp.sum(sums, axis=0)
    got, at = [], 0
    for size in [rows] * 5 + [3 * rows, unit]:
        got.append(sums[at : at + size])
        at += size
    return (
        layer_out,
        grad_inputs,
        got[0],
        got[1],
        got[2],
        got[3],
        grad_qkv,
        got[5],
        grad_proj,
        got[4],
        grad_up,
        got[6],
        grad_down,
        got[4],
    )


def solution(mesh):
    tokens, rows = P(AXIS, None), P(AXIS)
    return jax.shard_map(
        local_tuned if mesh.shape[AXIS] == 32 else local_any,
        mesh=mesh,
        in_specs=(tokens, tokens, rows, rows, rows, rows, tokens, rows, tokens, rows, tokens, rows, tokens, rows, tokens),
        out_specs=(tokens, tokens, rows, rows, rows, rows, tokens, rows, tokens, rows, tokens, rows, tokens, rows),
        check_vma=False,
    )
```

```python
import functools

import jax
import jax.numpy as jnp
import numpy as np
from jax import lax
from jax.experimental import pallas as pl
from jax.experimental.pallas import tpu as pltpu
from jax.sharding import PartitionSpec as P

HEADS = 8
HEAD = 256
ROT = 64
EPS = 1e-05
MASKED = -1e30
AXIS = "fsdp"
BF16 = jnp.bfloat16
F32 = jnp.float32

SPLIT_BITS = {32: (3, 2, 0), 128: (3, 1, 0)}


def attention_kernel(qkv_ref, turn_ref, docs_row_ref, docs_col_ref, d_mixed_ref, mixed_ref, d_qkv_ref, column_ref):
    half = ROT // 2
    cosine = turn_ref[0]
    sine = turn_ref[1]
    lanes = cosine.shape[1]
    lane = lax.broadcasted_iota(jnp.int32, cosine.shape, 1)

    def swap(v):
        return jnp.where(lane < half, pltpu.roll(v, lanes - half, 1), pltpu.roll(v, half, 1))

    def turn(v, sign):
        front = v[:, :lanes]
        front = front * cosine + sign * (swap(front) * sine)
        return jnp.concatenate([front, v[:, lanes:]], axis=1)

    rq = turn(qkv_ref[:, :HEAD], 1.0).astype(BF16)
    rk = turn(qkv_ref[:, HEAD : 2 * HEAD], 1.0).astype(BF16)
    rv = qkv_ref[:, 2 * HEAD :].astype(BF16)
    count = rq.shape[0]
    here = lax.broadcasted_iota(jnp.int32, (count, count), 0)
    there = lax.broadcasted_iota(jnp.int32, (count, count), 1)
    allowed = (docs_row_ref[0] == docs_col_ref[0]) & (there <= here)
    scale = HEAD ** (-0.5)
    rows = (((1,), (1,)), ((), ()))
    firsts = (((0,), (0,)), ((), ()))
    raw = lax.dot_general(rq, rk, rows, preferred_element_type=F32)
    scores = jnp.where(allowed, raw * scale, MASKED)
    expo = jnp.exp(scores - jnp.max(scores, axis=1, keepdims=True))
    probs = expo / jnp.sum(expo, axis=1, keepdims=True)
    weights = probs.astype(BF16)
    mixed_ref[...] = jnp.dot(weights, rv, preferred_element_type=F32).astype(BF16)
    d_mixed = d_mixed_ref[...]
    d_prob = lax.dot_general(d_mixed, rv, rows, preferred_element_type=F32)
    d_score = probs * (d_prob - jnp.sum(probs * d_prob, axis=1, keepdims=True))
    d_raw = (d_score * scale).astype(BF16)
    d_rq = jnp.dot(d_raw, rk, preferred_element_type=F32)
    d_rk = lax.dot_general(d_raw, rq, firsts, preferred_element_type=F32)
    d_rv = lax.dot_general(weights, d_mixed, firsts, preferred_element_type=F32)
    d_qkv = jnp.concatenate([turn(d_rq, -1.0), turn(d_rk, -1.0), d_rv], axis=1).astype(BF16)
    d_qkv_ref[...] = d_qkv

    @pl.when(pl.program_id(0) == 0)
    def _():
        column_ref[...] = jnp.zeros_like(column_ref)

    column_ref[...] += jnp.sum(d_qkv.astype(F32), axis=0, keepdims=True)


def attention(qkv, cosine, sine, docs, d_mixed):
    rows, count = docs.shape
    turns = jnp.stack([cosine, sine])
    lanes = turns.shape[2]
    return pl.pallas_call(
        attention_kernel,
        grid=(rows,),
        in_specs=[
            pl.BlockSpec((count, 3 * HEAD), lambda i: (i, 0)),
            pl.BlockSpec((2, count, lanes), lambda i: (0, i, 0)),
            pl.BlockSpec((1, 1, count), lambda i: (i, 0, 0)),
            pl.BlockSpec((1, count, 1), lambda i: (i, 0, 0)),
            pl.BlockSpec((count, HEAD), lambda i: (i, 0)),
        ],
        out_specs=[
            pl.BlockSpec((count, HEAD), lambda i: (i, 0)),
            pl.BlockSpec((count, 3 * HEAD), lambda i: (i, 0)),
            pl.BlockSpec((1, 3 * HEAD), lambda i: (0, 0)),
        ],
        out_shape=[
            jax.ShapeDtypeStruct((rows * count, HEAD), BF16),
            jax.ShapeDtypeStruct((rows * count, 3 * HEAD), BF16),
            jax.ShapeDtypeStruct((1, 3 * HEAD), F32),
        ],
        compiler_params=pltpu.CompilerParams(vmem_limit_bytes=32 * 1024 * 1024),
        cost_estimate=pl.CostEstimate(
            flops=16 * rows * count * count * HEAD, bytes_accessed=20 * rows * count * HEAD, transcendentals=rows * count * count
        ),
    )(qkv, turns, docs[:, None, :], docs[:, :, None], d_mixed)


def times_rows(left, right):
    return jnp.einsum("tc,nc->tn", left, right, preferred_element_type=F32)


def times_tokens(left, right):
    return jnp.einsum("tn,td->nd", left, right, preferred_element_type=F32)


class Layout:
    def __init__(self, count):
        self.count = count
        self.bits = count.bit_length() - 1
        self.h_bits = SPLIT_BITS.get(count, (2, 1, 0))
        self.t_bits = tuple(b for b in range(self.bits - 1, -1, -1) if b not in self.h_bits)
        head_bits = tuple(range(self.bits - 1, self.bits - 4, -1))
        self.swap = {b: b for b in range(self.bits)}
        for a, b in zip([a for a in head_bits if a not in self.h_bits], [b for b in self.h_bits if b not in head_bits]):
            self.swap[a], self.swap[b] = b, a
        self.groups = []
        for t in range(1 << len(self.t_bits)):
            base = sum(((t >> (len(self.t_bits) - 1 - i)) & 1) << b for i, b in enumerate(self.t_bits))
            self.groups.append(
                [base | sum(((h >> (2 - i)) & 1) << b for i, b in enumerate(self.h_bits)) for h in range(8)]
            )

    def swapped(self, device):
        return sum(((device >> b) & 1) << self.swap[b] for b in range(self.bits))

    def axis(self, bit):
        return self.bits - 1 - bit

    def flip(self, value, bit):
        return lax.ppermute(value, AXIS, [(d, d ^ (1 << bit)) for d in range(self.count)])

    def exchange_heads(self, value, flipped=0, back=False):
        pairs = [(d, self.swapped(d ^ flipped)) for d in range(self.count)]
        return lax.ppermute(value, AXIS, [(b, a) for a, b in pairs] if back else pairs)

    def mine(self, bit):
        return (lax.axis_index(AXIS) >> bit) & 1

    def gather(self, value):
        pieces = {0: value}
        for bit in self.t_bits:
            pieces.update({key | (1 << bit): self.flip(piece, bit) for key, piece in list(pieces.items())})
        return pieces

    def place(self, pieces, order, shape):
        some = pieces[0]
        whole = jnp.zeros(shape, some.dtype)
        block = tuple(1 if bit is not None else size for bit, size in zip(order, shape))
        block = block + shape[len(order) :]
        for key, piece in pieces.items():
            starts = [0 if bit is None else self.mine(bit) ^ ((key >> bit) & 1) for bit in order]
            starts = starts + [0] * (len(shape) - len(order))
            whole = lax.dynamic_update_slice(whole, piece.reshape(block), starts)
        return whole

    def reduce(self, part, order):
        order = list(order)
        for bit in reversed(self.t_bits):
            axis = order.index(bit)
            mine = self.mine(bit)
            away = lax.dynamic_index_in_dim(part, 1 - mine, axis, keepdims=False).astype(BF16)
            keep = lax.dynamic_index_in_dim(part, mine, axis, keepdims=False)
            part = keep + self.flip(away, bit).astype(F32)
            order.pop(axis)
        return part

    def gather_tokens(self, value):
        pieces = [value]
        for bit in self.h_bits[:-1]:
            pieces = pieces + [self.flip(piece, bit) for piece in pieces]
        own = jnp.concatenate(pieces, axis=0)
        return jnp.concatenate([own, self.flip(own, self.h_bits[-1])], axis=0)

    def reduce_tokens(self, part):
        for bit in reversed(self.h_bits):
            half = part.shape[0] // 2
            away = part[half:].astype(BF16)
            part = part[:half].astype(F32) + self.flip(away, bit).astype(F32)
        return part

    def to_columns(self, value):
        return lax.all_to_all(value, AXIS, split_axis=0, concat_axis=0, tiled=True, axis_index_groups=self.groups)


def local_any(
    inputs,
    doc_ids,
    attn_gain,
    attn_shift,
    ffn_gain,
    ffn_shift,
    qkv_weight,
    qkv_bias,
    proj_weight,
    proj_bias,
    up_weight,
    up_bias,
    down_weight,
    down_bias,
    cotangent,
):
    n = lax.axis_size(AXIS)
    lay = Layout(n)
    bits = lay.bits
    two = (2,) * bits
    count, width = inputs.shape
    rows = width // n
    unit = up_bias.shape[0]
    hidden = unit * (n // HEADS)
    h_axes = [lay.axis(b) for b in lay.h_bits]
    t_axes = [lay.axis(b) for b in lay.t_bits]

    small = jnp.concatenate(
        [
            attn_gain,
            attn_shift,
            ffn_gain,
            ffn_shift,
            proj_bias,
            down_bias,
            qkv_bias,
            up_bias,
            doc_ids[0].astype(BF16),
        ]
    )
    small = lax.all_to_all(
        jnp.broadcast_to(small[None], (n, small.shape[0])), AXIS, split_axis=0, concat_axis=0, tiled=True
    ).astype(F32)
    sizes = [rows] * 6 + [3 * rows, unit, count]
    vectors, at = [], 0
    for size in sizes:
        vectors.append(small[:, at : at + size])
        at += size
    a_gain, a_shift, f_gain, f_shift, b_proj, b_down = [v.reshape(1, width) for v in vectors[:6]]

    heads_at = [2 + (bits - 1 - lay.swap[b]) for b in lay.h_bits]
    up_cols = up_weight.reshape((rows,) + two + (unit,))
    up_cols = up_cols.transpose([1 + a for a in h_axes] + [0] + [1 + a for a in t_axes] + [bits + 1])
    up_cols = lay.to_columns(up_cols.reshape(HEADS, rows, hidden))
    qkv_cols = qkv_weight.reshape(rows, 3, 2, 2, 2, HEAD).transpose(heads_at + [0, 1, 5])
    qkv_cols = lay.to_columns(qkv_cols.reshape(HEADS, rows, 3 * HEAD))

    x = lay.gather_tokens(inputs)
    row_order = [b if b in lay.t_bits else None for b in range(bits - 1, -1, -1)]
    w_up = lay.place(lay.gather(up_cols), row_order, two + (rows, hidden)).reshape(width, hidden)
    g = lay.gather_tokens(cotangent)
    t_two = (2,) * len(lay.t_bits)
    w_down = lay.place(lay.gather(down_weight), lay.t_bits, t_two + (unit, width)).reshape(hidden, width)
    proj_order = [lay.swap[b] for b in range(bits - 4, -1, -1)]
    w_proj = lay.place(
        lay.gather(lay.exchange_heads(proj_weight)), proj_order, t_two + (rows, width)
    ).reshape(HEAD, width)
    w_qkv = lay.place(lay.gather(qkv_cols), row_order, two + (rows, 3 * HEAD)).reshape(width, 3 * HEAD)

    b_up = vectors[7].reshape(two + (unit,)).transpose(h_axes + t_axes + [bits]).reshape(HEADS, hidden)
    b_qkv = vectors[6].reshape((3, 2, 2, 2, HEAD)).transpose([a - 1 for a in heads_at] + [0, 4]).reshape(HEADS, 3 * HEAD)
    here = sum(lay.mine(b) << (2 - i) for i, b in enumerate(lay.h_bits))
    b_up = lax.dynamic_index_in_dim(b_up, here, 0, keepdims=True)
    b_qkv = lax.dynamic_index_in_dim(b_qkv, here, 0, keepdims=True)
    me = lax.axis_index(AXIS)
    docs = []
    for j in range(HEADS):
        other = me ^ sum(((j >> i) & 1) << b for i, b in enumerate(lay.h_bits))
        docs.append(lax.dynamic_index_in_dim(vectors[8], other, 0, keepdims=True))
    docs = jnp.concatenate(docs, axis=0).astype(jnp.int32)

    index = jnp.arange(count, dtype=jnp.int32)
    same = docs[:, :, None] == docs[:, None, :]
    position = jnp.sum((same & (index[None, None, :] < index[None, :, None])).astype(jnp.int32), axis=2).reshape(-1)
    freq = 10000.0 ** (-2.0 * jnp.arange(ROT // 2, dtype=F32) / ROT)
    angle = position.astype(F32)[:, None] * freq[None, :]
    cosine, sine = jnp.cos(angle), jnp.sin(angle)
    rest = 128 - ROT
    cosine = jnp.concatenate([cosine, cosine, jnp.ones((angle.shape[0], rest), F32)], axis=1)
    sine = jnp.concatenate([-sine, sine, jnp.zeros((angle.shape[0], rest), F32)], axis=1)

    value = x.astype(F32)
    center = value - jnp.mean(value, axis=-1, keepdims=True)
    scale = lax.rsqrt(jnp.mean(center * center, axis=-1, keepdims=True) + EPS)
    xhat = center * scale
    first = (xhat * a_gain + a_shift).astype(BF16)
    second = (xhat * f_gain + f_shift).astype(BF16)

    up = jnp.dot(second, w_up, preferred_element_type=F32) + b_up
    phi_sum = 0.5 * (1.0 + lax.erf(up * (0.5**0.5)))
    act = (up * phi_sum).astype(BF16)
    slope = phi_sum + up * jnp.exp(-0.5 * up * up) * 0.3989422804014327
    part_down = times_tokens(act, g)
    d_act = times_rows(g, w_down)
    d_up = (d_act * slope).astype(BF16)
    part_up = times_tokens(second, d_up)
    d_second = times_rows(d_up, w_up)

    d_mixed = times_rows(g, w_proj).astype(BF16)
    qkv = jnp.dot(first, w_qkv, preferred_element_type=F32) + b_qkv
    mixed, d_qkv, column_qkv = attention(qkv, cosine, sine, docs, d_mixed)
    part_proj = times_tokens(mixed, g)
    part_qkv = times_tokens(first, d_qkv)
    d_first = times_rows(d_qkv, w_qkv)

    branches = jnp.dot(act, w_down, preferred_element_type=F32) + jnp.dot(mixed, w_proj, preferred_element_type=F32)
    value_own = inputs.astype(F32)
    layer_out = lay.reduce_tokens(branches) + value_own + b_proj + b_down

    edge = lay.reduce_tokens(d_first * a_gain + d_second * f_gain)
    center_own = value_own - jnp.mean(value_own, axis=-1, keepdims=True)
    scale_own = lax.rsqrt(jnp.mean(center_own * center_own, axis=-1, keepdims=True) + EPS)
    xhat_own = center_own * scale_own
    back = edge - jnp.mean(edge, axis=-1, keepdims=True) - xhat_own * jnp.mean(edge * xhat_own, axis=-1, keepdims=True)
    grad_inputs = cotangent.astype(F32) + back * scale_own

    grad_down = lay.reduce(part_down.reshape(t_two + (unit, width)), lay.t_bits)
    grad_proj = lay.reduce(part_proj.reshape(t_two + (rows, width)), proj_order)
    grad_proj = lay.exchange_heads(grad_proj.astype(BF16)).astype(F32)
    grad_up = lay.reduce(part_up.reshape(two + (rows, hidden)), row_order).reshape(HEADS, rows, hidden)
    grad_up = lay.to_columns(grad_up.astype(BF16)).astype(F32)
    axes = h_axes + t_axes
    grad_up = grad_up.reshape((2, 2, 2, rows) + t_two + (unit,))
    back_axes = [3] + [
        (axes.index(a) if axes.index(a) < 3 else axes.index(a) + 1) for a in range(bits)
    ] + [bits + 1]
    grad_up = grad_up.transpose(back_axes).reshape(rows, -1)
    grad_qkv = lay.reduce(part_qkv.reshape(two + (rows, 3 * HEAD)), row_order).reshape(HEADS, rows, 3 * HEAD)
    grad_qkv = lay.to_columns(grad_qkv.astype(BF16)).astype(F32)
    grad_qkv = grad_qkv.reshape(2, 2, 2, rows, 3, HEAD)
    grad_qkv = grad_qkv.transpose([3, 4] + [heads_at.index(a) for a in (2, 3, 4)] + [5]).reshape(rows, -1)

    column_up = jnp.sum(d_up.astype(F32), axis=0)
    column_out = jnp.sum(cotangent.astype(F32), axis=0)
    spread_up = lax.dynamic_update_slice(jnp.zeros((HEADS, hidden), F32), column_up[None], (here, 0))
    spread_up = spread_up.reshape((2,) * bits + (unit,)).transpose(
        [(axes.index(a)) for a in range(bits)] + [bits]
    )
    spread_qkv = lax.dynamic_update_slice(jnp.zeros((HEADS, 3 * HEAD), F32), column_qkv, (here, 0))
    spread_qkv = spread_qkv.reshape(2, 2, 2, 3, HEAD).transpose([3] + [heads_at.index(a) for a in (2, 3, 4)] + [4])
    sums = [
        jnp.sum(d_first * xhat, axis=0),
        jnp.sum(d_first, axis=0),
        jnp.sum(d_second * xhat, axis=0),
        jnp.sum(d_second, axis=0),
        column_out,
        spread_qkv,
        spread_up,
    ]
    sums = jnp.concatenate([s.reshape(n, -1) for s in sums], axis=1)
    sums = jnp.sum(lax.all_to_all(sums, AXIS, split_axis=0, concat_axis=0, tiled=True), axis=0)
    got, at = [], 0
    for size in [rows] * 5 + [3 * rows, unit]:
        got.append(sums[at : at + size])
        at += size
    return (
        layer_out,
        grad_inputs,
        got[0],
        got[1],
        got[2],
        got[3],
        grad_qkv,
        got[5],
        grad_proj,
        got[4],
        grad_up,
        got[6],
        grad_down,
        got[4],
    )


ZH, ZL, Y, X, CORE = 4, 3, 2, 1, 0
ROWS = (((1,), (1,)), ((), ()))
COST = 0.45e9
FIRSTS = (((0,), (0,)), ((), ()))


def after(values, *done):
    return lax.optimization_barrier(tuple(values) + done)[: len(values)]


def flip(value, bit):
    return lax.ppermute(value, AXIS, [(d, d ^ (1 << bit)) for d in range(lax.axis_size(AXIS))])


def call(body, grid, in_specs, out_specs, out_shape, args, scalars=None, limit=40, us=1.0, aliases=None):
    extra = dict(
        out_shape=out_shape,
        compiler_params=pltpu.CompilerParams(vmem_limit_bytes=limit * 1024 * 1024),
        cost_estimate=pl.CostEstimate(flops=int(us * COST), bytes_accessed=1024, transcendentals=0),
        input_output_aliases=aliases or {},
    )
    if scalars is None:
        return pl.pallas_call(body, grid=grid, in_specs=in_specs, out_specs=out_specs, **extra)(*args)
    spec = pltpu.PrefetchScalarGridSpec(num_scalar_prefetch=1, grid=grid, in_specs=in_specs, out_specs=out_specs)
    return pl.pallas_call(body, grid_spec=spec, **extra)(scalars, *args)


def shape(dims, dtype):
    return jax.ShapeDtypeStruct(dims, dtype)


def bits_of(number, count):
    return [(number >> (count - 1 - i)) & 1 for i in range(count)]


def order_columns(value, mine):
    count, width = value.shape
    wide = width // 16

    def body(mine_ref, x_ref, o_ref):
        for j in range(16):
            xr, zr, b, c = bits_of(j, 4)
            source = (zr ^ mine_ref[0]) * 8 + b * 4 + c * 2 + (xr ^ mine_ref[1])
            o_ref[:, j * wide : (j + 1) * wide] = x_ref[:, pl.ds(pl.multiple_of(source * wide, wide), wide)]

    block = pl.BlockSpec((count, width), lambda i, s: (0, 0))
    return call(body, (1,), [block], block, shape((count, width), value.dtype), (value,), mine)


def split_columns(up_weight, qkv_weight):
    rows, ff = up_weight.shape
    unit = ff // 32
    hidden = 4 * unit

    def body(u_ref, q_ref, o_ref):
        for h in range(8):
            zl, y, c = bits_of(h, 3)
            for t in range(4):
                zh, x = bits_of(t, 2)
                e = zh * 16 + zl * 8 + y * 4 + x * 2 + c
                o_ref[h, :, t * unit : (t + 1) * unit] = u_ref[:, e * unit : (e + 1) * unit]
            head = c * 4 + zl * 2 + y
            for k in range(3):
                at = (k * HEADS + head) * HEAD
                o_ref[h, :, hidden + k * HEAD : hidden + (k + 1) * HEAD] = q_ref[:, at : at + HEAD]

    def block(*dims):
        return pl.BlockSpec(dims, lambda i: (0,) * len(dims))

    return call(
        body,
        (1,),
        [block(rows, ff), block(rows, 3 * HEADS * HEAD)],
        block(8, rows, hidden + 3 * HEAD),
        shape((8, rows, hidden + 3 * HEAD), BF16),
        (up_weight, qkv_weight),
    )


def join_up(parts):
    _, rows, hidden = parts.shape
    unit = hidden // 4

    def body(p_ref, o_ref):
        for h in range(8):
            zl, y, c = bits_of(h, 3)
            for t in range(4):
                zh, x = bits_of(t, 2)
                e = zh * 16 + zl * 8 + y * 4 + x * 2 + c
                o_ref[:, e * unit : (e + 1) * unit] = p_ref[h, :, t * unit : (t + 1) * unit].astype(F32)

    return call(
        body,
        (1,),
        [pl.BlockSpec(parts.shape, lambda i: (0, 0, 0))],
        pl.BlockSpec((rows, 8 * hidden), lambda i: (0, 0)),
        shape((rows, 8 * hidden), F32),
        (parts,),
    )


def join_qkv(parts):
    _, rows, _ = parts.shape

    def body(p_ref, o_ref):
        for h in range(8):
            zl, y, c = bits_of(h, 3)
            head = c * 4 + zl * 2 + y
            for k in range(3):
                at = (k * HEADS + head) * HEAD
                o_ref[:, at : at + HEAD] = p_ref[h, :, k * HEAD : (k + 1) * HEAD].astype(F32)

    return call(
        body,
        (1,),
        [pl.BlockSpec(parts.shape, lambda i: (0, 0, 0))],
        pl.BlockSpec((rows, 3 * HEADS * HEAD), lambda i: (0, 0)),
        shape((rows, 3 * HEADS * HEAD), F32),
        (parts,),
    )


def prepare(small, place, freq, sign, rows, unit, count):
    n, _, lanes = small.shape
    width = n * rows
    up_at, gains_at = count // lanes, (count + unit) // lanes
    out_at = gains_at + 2
    qkv_at = out_at + 1

    def body(place_ref, small_ref, f_ref, s_ref, gains_ref, out_ref, up_ref, qkv_ref, docs_ref, cos_ref, sin_ref, all_ref):
        mzh, mx, mzl, my, mc, me = [place_ref[k] for k in range(6)]
        step = pl.program_id(0)

        @pl.when(step == 0)
        def _():
            all_ref[...] = small_ref[...].astype(F32)
            gains_ref[...] = jnp.zeros_like(gains_ref)

            for j in range(16):
                xr, zr, b, c = bits_of(j, 4)
                source = 2 * ((zr ^ mzh) * 8 + b * 4 + c * 2 + (xr ^ mx))
                here = slice(2 * j * rows, 2 * (j + 1) * rows)
                left, right = all_ref[source], all_ref[source + 1]
                for k in range(4):
                    at, part = gains_at + k // 2, slice(k % 2 * rows, (k % 2 + 1) * rows)
                    gains_ref[k : k + 1, here] = jnp.concatenate([left[at : at + 1, part], right[at : at + 1, part]], axis=1)
                left, right = [v[:, :rows] + v[:, rows:] for v in (all_ref[2 * j, out_at : out_at + 1], all_ref[2 * j + 1, out_at : out_at + 1])]
                out_ref[:, here] = jnp.concatenate([left, right], axis=1)
            for t in range(4):
                zh, x = bits_of(t, 2)
                device = zh * 16 + mzl * 8 + my * 4 + x * 2 + mc
                mine_up = all_ref[device]
                for k in range(unit // lanes):
                    up_ref[:, t * unit + k * lanes : t * unit + (k + 1) * lanes] = mine_up[up_at + k : up_at + k + 1]
            head = mc * 4 + mzl * 2 + my
            for k in range(3 * HEAD // rows):
                chunk = (k // (HEAD // rows) * HEADS + head) * (HEAD // rows) + k % (HEAD // rows)
                third = all_ref[chunk // 3]
                part = lax.rem(chunk, 3)
                first, last = third[qkv_at : qkv_at + 1], third[qkv_at + 1 : qkv_at + 2]
                qkv_ref[:, k * rows : (k + 1) * rows] = jnp.where(
                    part == 0, first[:, :rows], jnp.where(part == 1, first[:, rows:], last[:, :rows])
                )

        other = me ^ (((step & 1) << ZL) | (((step >> 1) & 1) << Y) | (((step >> 2) & 1) << CORE))
        held = all_ref[other]
        docs = jnp.concatenate([held[k : k + 1] for k in range(count // lanes)], axis=1)
        docs_ref[0] = docs
        across = jnp.broadcast_to(docs, (count, count))
        here = lax.broadcasted_iota(jnp.int32, (count, count), 0)
        there = lax.broadcasted_iota(jnp.int32, (count, count), 1)
        earlier = (across == across.T) & (there < here)
        position = jnp.sum(earlier.astype(F32), axis=1, keepdims=True)
        angle = position * f_ref[...]
        cos_ref[...] = jnp.cos(angle)
        sin_ref[...] = jnp.sin(angle) * s_ref[...]

    def whole(*dims):
        return pl.BlockSpec(dims, lambda i, s: (0, 0))

    block = pl.BlockSpec((count, lanes), lambda i, s: (i, 0))
    return pl.pallas_call(
        body,
        grid_spec=pltpu.PrefetchScalarGridSpec(
            num_scalar_prefetch=1,
            grid=(8,),
            in_specs=[pl.BlockSpec(small.shape, lambda i, s: (0, 0, 0)), whole(1, lanes), whole(1, lanes)],
            out_specs=[
                whole(8, width),
                whole(1, width),
                whole(1, 4 * unit),
                whole(1, 3 * HEAD),
                pl.BlockSpec((1, 1, count), lambda i, s: (i, 0, 0)),
                block,
                block,
            ],
            scratch_shapes=[pltpu.VMEM(small.shape, F32)],
        ),
        out_shape=[
            shape((8, width), F32),
            shape((1, width), F32),
            shape((1, 4 * unit), F32),
            shape((1, 3 * HEAD), F32),
            shape((8, 1, count), F32),
            shape((8 * count, lanes), F32),
            shape((8 * count, lanes), F32),
        ],
        compiler_params=pltpu.CompilerParams(vmem_limit_bytes=40 * 1024 * 1024),
        cost_estimate=pl.CostEstimate(flops=int(COST), bytes_accessed=1024, transcendentals=0),
    )(place, small, freq, sign)


def join(pieces):
    count, width = pieces[0].shape
    blocks = len(pieces)

    def body(*refs):
        ins, out, held, sems_in, sems_out = refs[:blocks], refs[blocks], *refs[blocks + 1 :]

        def copy_in(k):
            return pltpu.make_async_copy(ins[k], held.at[k], sems_in.at[k])

        def copy_out(k):
            return pltpu.make_async_copy(held.at[k], out.at[pl.ds(k * count, count)], sems_out.at[k])

        for k in range(blocks):
            copy_in(k).start()
        for k in range(blocks):
            copy_in(k).wait()
            copy_out(k).start()
        for k in range(blocks):
            copy_out(k).wait()

    some = pl.BlockSpec(memory_space=pl.ANY)
    return pl.pallas_call(
        body,
        grid=(1,),
        in_specs=[some] * blocks,
        out_specs=some,
        out_shape=shape((blocks * count, width), pieces[0].dtype),
        scratch_shapes=[pltpu.VMEM((blocks, count, width), pieces[0].dtype)] + [pltpu.SemaphoreType.DMA((blocks,))] * 2,
        compiler_params=pltpu.CompilerParams(vmem_limit_bytes=40 * 1024 * 1024),
        cost_estimate=pl.CostEstimate(flops=int(4 * COST), bytes_accessed=1024, transcendentals=0),
    )(*pieces)


def join_heads(pieces, mine):
    rows, width = pieces[0].shape

    def body(mine_ref, *refs):
        for k, (xr, zr) in enumerate([(0, 0), (0, 1), (1, 0), (1, 1)]):
            at = ((mine_ref[1] ^ xr) * 2 + (mine_ref[0] ^ zr)) * rows
            refs[4][pl.ds(pl.multiple_of(at, rows), rows), :] = refs[k][...]

    return call(
        body,
        (1,),
        [pl.BlockSpec((rows, width), lambda i, s: (0, 0))] * 4,
        pl.BlockSpec((4 * rows, width), lambda i, s: (0, 0)),
        shape((4 * rows, width), BF16),
        tuple(pieces),
        mine,
    )


def norms(halves, gains, count):
    tokens, width = halves[0].shape
    each = tokens // count
    blocks = 2 * each

    def body(v_ref, a_ref, b_ref, first_ref, second_ref, stats_ref, x_buf, first_buf, second_buf, sems_in, sems_first, sems_second):
        def copy_in(k):
            half = (a_ref, b_ref)[k // each]
            return pltpu.make_async_copy(half.at[pl.ds(k % each * count, count)], x_buf.at[k % 2], sems_in.at[k % 2])

        def copy_first(k):
            return pltpu.make_async_copy(first_buf.at[k % 2], first_ref.at[pl.ds(k * count, count)], sems_first.at[k % 2])

        def copy_second(k):
            return pltpu.make_async_copy(second_buf.at[k % 2], second_ref.at[pl.ds(k * count, count)], sems_second.at[k % 2])

        copy_in(0).start()
        for k in range(blocks):
            slot = k % 2
            copy_in(k).wait()
            if k + 1 < blocks:
                copy_in(k + 1).start()
            if k >= 2:
                copy_first(k - 2).wait()
                copy_second(k - 2).wait()
            value = x_buf[slot].astype(F32)
            mean = jnp.mean(value, axis=-1, keepdims=True)
            center = value - mean
            scale = lax.rsqrt(jnp.mean(center * center, axis=-1, keepdims=True) + EPS)
            xhat = center * scale
            first_buf[slot] = (xhat * v_ref[0:1, :] + v_ref[1:2, :]).astype(BF16)
            second_buf[slot] = (xhat * v_ref[2:3, :] + v_ref[3:4, :]).astype(BF16)
            lane = lax.broadcasted_iota(jnp.int32, (count, 128), 1)
            stats_ref[k * count : (k + 1) * count, :] = jnp.where(lane == 0, mean, scale)
            copy_first(k).start()
            copy_second(k).start()
        for k in (blocks - 2, blocks - 1):
            copy_first(k).wait()
            copy_second(k).wait()

    some = pl.BlockSpec(memory_space=pl.ANY)
    return pl.pallas_call(
        body,
        grid=(1,),
        in_specs=[pl.BlockSpec((8, width), lambda i: (0, 0)), some, some],
        out_specs=[some, some, pl.BlockSpec((2 * tokens, 128), lambda i: (0, 0))],
        out_shape=[shape((2 * tokens, width), BF16)] * 2 + [shape((2 * tokens, 128), F32)],
        scratch_shapes=[pltpu.VMEM((2, count, width), BF16)] * 3 + [pltpu.SemaphoreType.DMA((2,))] * 3,
        compiler_params=pltpu.CompilerParams(vmem_limit_bytes=40 * 1024 * 1024),
        cost_estimate=pl.CostEstimate(flops=int(12 * COST), bytes_accessed=1024, transcendentals=0),
    )(gains, *halves)


def feed_up(second, w_up, bias, tile=512):
    tokens, width = second.shape
    deep, hidden = w_up[0].shape

    def body(s_ref, *refs):
        b_ref, act_ref, slope_ref = refs[4:]
        up = b_ref[...]
        for k in range(4):
            up = up + jnp.dot(s_ref[:, k * deep : (k + 1) * deep], refs[k][...], preferred_element_type=F32)
        phi_sum = 0.5 * (1.0 + lax.erf(up * (0.5**0.5)))
        act_ref[...] = (up * phi_sum).astype(BF16)
        slope_ref[...] = phi_sum + up * jnp.exp(-0.5 * up * up) * 0.3989422804014327

    block = pl.BlockSpec((tile, hidden), lambda i: (i, 0))
    return call(
        body,
        (tokens // tile,),
        [pl.BlockSpec((tile, width), lambda i: (i, 0))]
        + [pl.BlockSpec((deep, hidden), lambda i: (0, 0))] * 4
        + [pl.BlockSpec((1, hidden), lambda i: (0, 0))],
        [block, block],
        [shape((tokens, hidden), BF16), shape((tokens, hidden), F32)],
        (second, *w_up, bias),
        us=16,
    )


def either(steps, first_half, tile, width):
    half = steps // 2

    def spec(low):
        return pl.BlockSpec((tile, width), lambda i: (jnp.minimum(i, half - 1) if low else jnp.maximum(i - half, 0), 0))

    return [spec(first_half), spec(not first_half)]


def join_units(pieces, mine):
    unit, width = pieces[0].shape

    def body(mine_ref, *refs):
        for k, (zr, xr) in enumerate([(0, 0), (0, 1), (1, 0), (1, 1)]):
            at = ((mine_ref[0] ^ zr) * 2 + (mine_ref[1] ^ xr)) * unit
            refs[4][pl.ds(pl.multiple_of(at, unit), unit), :] = refs[k][...]

    return call(
        body,
        (1,),
        [pl.BlockSpec(p.shape, lambda i, s: (0, 0)) for p in pieces],
        pl.BlockSpec((4 * unit, width), lambda i, s: (0, 0)),
        shape((4 * unit, width), BF16),
        tuple(pieces),
        mine,
        us=3,
    )


def feed_back(g, w_down, slope, tile=512):
    half, width = g[0].shape
    steps = 2 * half // tile
    hidden = slope.shape[1]

    def body(ga_ref, gb_ref, w_ref, slope_ref, d_ref, column_ref):
        step = pl.program_id(0)

        @pl.when(step == 0)
        def _():
            column_ref[...] = jnp.zeros_like(column_ref)

        def work(g_ref):
            d_act = lax.dot_general(g_ref[...], w_ref[...], ROWS, preferred_element_type=F32)
            d_up = (d_act * slope_ref[...]).astype(BF16)
            d_ref[...] = d_up
            column_ref[...] += jnp.sum(d_up.astype(F32), axis=0, keepdims=True)

        pl.when(step < steps // 2)(lambda: work(ga_ref))
        pl.when(step >= steps // 2)(lambda: work(gb_ref))

    block = pl.BlockSpec((tile, hidden), lambda i: (i, 0))
    return call(
        body,
        (steps,),
        either(steps, True, tile, width) + [pl.BlockSpec((hidden, width), lambda i: (0, 0)), block],
        [block, pl.BlockSpec((1, hidden), lambda i: (0, 0))],
        [shape((2 * half, hidden), BF16), shape((1, hidden), F32)],
        (*g, w_down, slope),
        us=14,
    )


def weight_grad(left, right, mine, source, us=13):
    tokens, width = left.shape
    wide = right[0].shape[1]
    tile = width // 4
    count = len(right)

    def body(mine_ref, l_ref, *refs):
        part = lax.dot_general(l_ref[: tokens // count], refs[0][...], FIRSTS, preferred_element_type=F32)
        if count == 2:
            part = part + lax.dot_general(l_ref[tokens // 2 :], refs[1][...], FIRSTS, preferred_element_type=F32)
        for k, out in enumerate(refs[count:]):

            @pl.when(pl.program_id(0) == k)
            def _():
                out[...] = part.astype(out.dtype)

    return call(
        body,
        (4,),
        [pl.BlockSpec((tokens, tile), lambda i, s: (0, source(i, s)))]
        + [pl.BlockSpec(r.shape, lambda i, s: (0, 0)) for r in right],
        [pl.BlockSpec((tile, wide), lambda i, s: (0, 0))] * 4,
        [shape((tile, wide), BF16)] * 2 + [shape((tile, wide), F32)] * 2,
        (left, *right),
        mine,
        us=us,
    )


def head_grad(mixed, g, mine):
    tokens, head = mixed.shape
    width = g[0].shape[1]

    def body(mine_ref, l_ref, ga_ref, gb_ref, sent_ref, kept_ref):
        part = lax.dot_general(l_ref[: tokens // 2], ga_ref[...], FIRSTS, preferred_element_type=F32)
        part = part + lax.dot_general(l_ref[tokens // 2 :], gb_ref[...], FIRSTS, preferred_element_type=F32)
        upper, lower = part[: head // 2], part[head // 2 :]
        own = mine_ref[1] == 0
        sent_ref[...] = jnp.where(own, lower, upper).astype(BF16)
        kept_ref[...] = jnp.where(own, upper, lower)

    return call(
        body,
        (2,),
        [pl.BlockSpec((tokens, head), lambda i, s: (0, 0))]
        + [pl.BlockSpec((tokens // 2, width // 2), lambda i, s: (0, i))] * 2,
        [pl.BlockSpec((head // 2, width // 2), lambda i, s: (0, i))] * 2,
        [shape((head // 2, width), BF16), shape((head // 2, width), F32)],
        (mixed, *g),
        mine,
        us=5,
    )


def fold_tokens(kept, got):
    count, width = kept.shape
    tile = count // 4

    def body(k_ref, *refs):
        first_ref, second_ref, stays_ref = refs[4:]
        step = pl.program_id(0)
        for j in range(4):

            @pl.when(step == 3 - j)
            def _():
                total = k_ref[...].astype(F32) + refs[j][...].astype(F32)
                out = (stays_ref, stays_ref, second_ref, first_ref)[j]
                out[...] = total.astype(out.dtype)

    fixed = pl.BlockSpec((tile, width), lambda i: (0, 0))
    return call(
        body,
        (4,),
        [pl.BlockSpec((tile, width), lambda i: (3 - i, 0))] + [fixed] * 4,
        [fixed, fixed, pl.BlockSpec((tile, width), lambda i: (jnp.minimum(3 - i, 1), 0))],
        [shape((tile, width), BF16)] * 2 + [shape((2 * tile, width), F32)],
        (kept,) + tuple(got),
        us=5,
    )


def add_half(kept, got, rows, at):
    width = kept.shape[1]

    def body(k_ref, g_ref, o_ref):
        o_ref[...] = (k_ref[...] + g_ref[...].astype(F32)).astype(BF16)

    fixed = pl.BlockSpec((rows, width), lambda i: (0, 0))
    return call(
        body, (1,), [pl.BlockSpec((rows, width), lambda i: (at, 0)), fixed], fixed, shape((rows, width), BF16), (kept, got)
    )


def attend(first, w_qkv, b_qkv, g, w_proj, cosine, sine, docs):
    tokens, width = first.shape
    rows, _, count = docs.shape
    deep = w_qkv[0].shape[0]
    lanes = cosine.shape[1]
    half = ROT // 2
    scale = HEAD ** (-0.5)

    def body(f_ref, w0_ref, w1_ref, w2_ref, w3_ref, b_ref, ga_ref, gb_ref, p_ref, cos_ref, sin_ref, row_ref, mixed_ref, d_qkv_ref, column_ref):
        step = pl.program_id(0)

        @pl.when(step == 0)
        def _():
            column_ref[...] = jnp.zeros_like(column_ref)

        def work(g_ref):
            cos, sin = cos_ref[...], sin_ref[...]
            lane = lax.broadcasted_iota(jnp.int32, cos.shape, 1)

            def turn(v, sign):
                front = v[:, :lanes]
                other = jnp.where(lane < half, pltpu.roll(front, lanes - half, 1), pltpu.roll(front, half, 1))
                return jnp.concatenate([front * cos + sign * (other * sin), v[:, lanes:]], axis=1)

            qkv = b_ref[...]
            for k, w_ref in enumerate((w0_ref, w1_ref, w2_ref, w3_ref)):
                qkv = qkv + jnp.dot(f_ref[:, k * deep : (k + 1) * deep], w_ref[...], preferred_element_type=F32)
            d_mixed = lax.dot_general(g_ref[...], p_ref[...], ROWS, preferred_element_type=F32).astype(BF16)
            rq = turn(qkv[:, :HEAD], 1.0).astype(BF16)
            rk = turn(qkv[:, HEAD : 2 * HEAD], 1.0).astype(BF16)
            rv = qkv[:, 2 * HEAD :].astype(BF16)
            here = lax.broadcasted_iota(jnp.int32, (count, count), 0)
            there = lax.broadcasted_iota(jnp.int32, (count, count), 1)
            across = jnp.broadcast_to(row_ref[0], (count, count))
            allowed = (across == across.T) & (there <= here)
            raw = lax.dot_general(rq, rk, ROWS, preferred_element_type=F32)
            scores = jnp.where(allowed, raw * scale, MASKED)
            expo = jnp.exp(scores - jnp.max(scores, axis=1, keepdims=True))
            probs = expo / jnp.sum(expo, axis=1, keepdims=True)
            weights = probs.astype(BF16)
            mixed_ref[...] = jnp.dot(weights, rv, preferred_element_type=F32).astype(BF16)
            d_prob = lax.dot_general(d_mixed, rv, ROWS, preferred_element_type=F32)
            d_score = probs * (d_prob - jnp.sum(probs * d_prob, axis=1, keepdims=True))
            d_raw = (d_score * scale).astype(BF16)
            d_rq = jnp.dot(d_raw, rk, preferred_element_type=F32)
            d_rk = lax.dot_general(d_raw, rq, FIRSTS, preferred_element_type=F32)
            d_rv = lax.dot_general(weights, d_mixed, FIRSTS, preferred_element_type=F32)
            d_qkv = jnp.concatenate([turn(d_rq, -1.0), turn(d_rk, -1.0), d_rv], axis=1).astype(BF16)
            d_qkv_ref[...] = d_qkv
            column_ref[...] += jnp.sum(d_qkv.astype(F32), axis=0, keepdims=True)

        pl.when(step < rows // 2)(lambda: work(ga_ref))
        pl.when(step >= rows // 2)(lambda: work(gb_ref))

    def row(*dims):
        return pl.BlockSpec(dims, lambda i: (i, 0))

    def whole(*dims):
        return pl.BlockSpec(dims, lambda i: (0, 0))

    return call(
        body,
        (rows,),
        [
            row(count, width),
            *([whole(deep, 3 * HEAD)] * 4),
            whole(1, 3 * HEAD),
            *either(rows, True, count, width),
            whole(HEAD, width),
            row(count, lanes),
            row(count, lanes),
            pl.BlockSpec((1, 1, count), lambda i: (i, 0, 0)),
        ],
        [row(count, HEAD), row(count, 3 * HEAD), whole(1, 3 * HEAD)],
        [shape((tokens, HEAD), BF16), shape((tokens, 3 * HEAD), BF16), shape((1, 3 * HEAD), F32)],
        (first, *w_qkv, b_qkv, *g, w_proj, cosine, sine, docs),
        us=17,
    )


def branch_sum(act, w_down, mixed, w_proj, tile=512, block=256):
    tokens, hidden = act.shape
    width = w_down.shape[1]
    steps = tokens // tile
    sent = steps // 2
    each = tile // block
    blocks = sent * each

    def body(a_ref, w_ref, m_ref, p_ref, *outs):
        part = jnp.dot(a_ref[...], w_ref[...], preferred_element_type=F32)
        part = (part + jnp.dot(m_ref[...], p_ref[...], preferred_element_type=F32)).astype(BF16)
        outs[blocks][...] = part
        step = pl.program_id(0)
        for k in range(sent):

            @pl.when(step == k)
            def _():
                for j in range(each):
                    outs[k * each + j][...] = part[j * block : (j + 1) * block]

    def turned(i):
        return (lax.rem(i + sent, steps), 0)

    fixed = pl.BlockSpec((block, width), lambda i: (0, 0))
    return call(
        body,
        (steps,),
        [
            pl.BlockSpec((tile, hidden), turned),
            pl.BlockSpec((hidden, width), lambda i: (0, 0)),
            pl.BlockSpec((tile, HEAD), turned),
            pl.BlockSpec((HEAD, width), lambda i: (0, 0)),
        ],
        [fixed] * blocks + [pl.BlockSpec((tile, width), lambda i: (jnp.maximum(i - sent, 0), 0))],
        [shape((block, width), BF16)] * blocks + [shape((tokens // 2, width), BF16)],
        (act, w_down, mixed, w_proj),
        us=16,
    )


def edge_sum(d_up, w_up, d_qkv, w_qkv, x, stats, gains, tile=256):
    tokens, hidden = d_up.shape
    deep = w_up[0].shape[0]
    width = 4 * deep
    steps = tokens // tile
    sent = steps // 2

    def body(du_ref, dq_ref, xa_ref, xb_ref, stats_ref, v_ref, *refs):
        outs = refs[8:]
        sums_ref = outs[sent + 1]
        step = pl.program_id(0)

        @pl.when(step == 0)
        def _():
            sums_ref[...] = jnp.zeros_like(sums_ref)

        for k in range(4):
            part = slice(k * deep, (k + 1) * deep)
            d_second = lax.dot_general(du_ref[...], refs[k][...], ROWS, preferred_element_type=F32)
            d_first = lax.dot_general(dq_ref[...], refs[4 + k][...], ROWS, preferred_element_type=F32)
            x = jnp.where(step < sent, xb_ref[:, part], xa_ref[:, part])
            xhat = (x.astype(F32) - stats_ref[:, 0:1]) * stats_ref[:, 1:2]
            outs[sent][:, part] = (d_first * v_ref[0:1, part] + d_second * v_ref[2:3, part]).astype(BF16)
            sums_ref[0:1, part] += jnp.sum(d_first * xhat, axis=0, keepdims=True)
            sums_ref[1:2, part] += jnp.sum(d_first, axis=0, keepdims=True)
            sums_ref[2:3, part] += jnp.sum(d_second * xhat, axis=0, keepdims=True)
            sums_ref[3:4, part] += jnp.sum(d_second, axis=0, keepdims=True)

        for j in range(sent):

            @pl.when(step == j)
            def _():
                outs[j][...] = outs[sent][...]

    def turned(i):
        return (lax.rem(i + sent, steps), 0)

    def whole(*dims):
        return pl.BlockSpec(dims, lambda i: (0, 0))

    return call(
        body,
        (steps,),
        [
            pl.BlockSpec((tile, hidden), turned),
            pl.BlockSpec((tile, 3 * HEAD), turned),
            *either(steps, False, tile, width),
            pl.BlockSpec((tile, 128), turned),
            whole(8, width),
        ]
        + [whole(deep, hidden)] * 4
        + [whole(deep, 3 * HEAD)] * 4,
        [whole(tile, width)] * sent
        + [pl.BlockSpec((tile, width), lambda i: (jnp.maximum(i - sent, 0), 0)), whole(8, width)],
        [shape((tile, width), BF16)] * sent + [shape((tokens // 2, width), BF16), shape((8, width), F32)],
        (d_up, d_qkv, *x, stats, gains, *w_up, *w_qkv),
        us=28,
        limit=48,
    )


def total(parts, rows):
    width = parts[0].shape[1]

    def body(*refs):
        value = refs[0][...].astype(F32)
        for ref in refs[1:-1]:
            value = value + ref[...].astype(F32)
        refs[-1][...] = value

    return call(
        body,
        (1,),
        [pl.BlockSpec((min(rows, p.shape[0]), width), lambda i: (0, 0)) for p in parts],
        pl.BlockSpec((rows, width), lambda i: (0, 0)),
        shape((rows, width), F32),
        tuple(parts),
        us=3,
    )


def finish(edge_k, edge_g0, edge_got, x0, g, mine):
    count, width = x0.shape
    wide = width // 16

    def body(mine_ref, k_ref, a_ref, b_ref, x_ref, g_ref, o_ref):
        edge = k_ref[...] + a_ref[...].astype(F32) + b_ref[...].astype(F32)
        value = x_ref[...].astype(F32)
        center = value - jnp.mean(value, axis=-1, keepdims=True)
        scale = lax.rsqrt(jnp.mean(center * center, axis=-1, keepdims=True) + EPS)
        xhat = center * scale
        back = edge - jnp.mean(edge, axis=-1, keepdims=True) - xhat * jnp.mean(edge * xhat, axis=-1, keepdims=True)
        back = back * scale
        for j in range(16):
            xr, zr, b, c = bits_of(j, 4)
            source = (zr ^ mine_ref[0]) * 8 + b * 4 + c * 2 + (xr ^ mine_ref[1])
            place = pl.ds(pl.multiple_of(source * wide, wide), wide)
            o_ref[:, place] = g_ref[:, place].astype(F32) + back[:, j * wide : (j + 1) * wide]

    tile = count // 2
    block = pl.BlockSpec((tile, width), lambda i, s: (i, 0))
    return call(
        body, (2,), [block] * 5, block, shape((count, width), F32), (edge_k, edge_g0, edge_got, x0, g), mine, us=5
    )


def local_tuned(
    inputs,
    doc_ids,
    attn_gain,
    attn_shift,
    ffn_gain,
    ffn_shift,
    qkv_weight,
    qkv_bias,
    proj_weight,
    proj_bias,
    up_weight,
    up_bias,
    down_weight,
    down_bias,
    cotangent,
):
    n = lax.axis_size(AXIS)
    lay = Layout(n)
    count, width = inputs.shape
    rows = width // n
    unit = up_bias.shape[0]
    hidden = 4 * unit
    me = lax.axis_index(AXIS)
    mzh, mx = lay.mine(ZH), lay.mine(X)
    mine = jnp.stack([mzh, mx]).astype(jnp.int32)

    cols = split_columns(up_weight, qkv_weight)
    (x0,) = after((inputs,), cols)
    x0 = order_columns(x0, mine)
    down_z = flip(down_weight, ZH)
    down_x = flip(down_weight, X)
    cols = lay.to_columns(cols)
    x1 = flip(x0, ZL)
    x2 = flip(x0, Y)
    g2 = flip(cotangent, Y)
    small = jnp.concatenate(
        [doc_ids[0].astype(BF16), up_bias, attn_gain, attn_shift, ffn_gain, ffn_shift, proj_bias, down_bias, qkv_bias]
    )
    small = jnp.pad(small, (0, 16 * 128 - small.shape[0])).reshape(16, 128)
    small = jnp.broadcast_to(small[None], (n, 16, 128))

    cols, down_z, down_x, x1, x2, g2, small, g0 = after((cols, down_z, down_x, x1, x2, g2, small, cotangent))
    up_cols, qkv_cols = cols[:, :, :hidden], cols[:, :, hidden:]
    small = lax.all_to_all(small, AXIS, split_axis=0, concat_axis=0, tiled=True)
    up_z = flip(up_cols, ZH)
    up_x = flip(up_cols, X)
    g1 = flip(g0, ZL)
    x3 = flip(x1, Y)
    down_xz = flip(down_z, X)

    freq = 10000.0 ** (-2.0 * np.arange(ROT // 2, dtype=np.float32) / ROT)
    rest = np.zeros(128 - ROT, np.float32)
    freq = jnp.asarray(np.concatenate([freq, freq, rest])[None], F32)
    sign = jnp.asarray(np.concatenate([np.full(ROT // 2, -1.0), np.full(ROT // 2, 1.0), rest])[None], F32)
    bit_of = jnp.stack([lay.mine(b) for b in (ZH, X, ZL, Y, CORE)] + [me]).astype(jnp.int32)
    here = lay.mine(ZL) * 4 + lay.mine(Y) * 2 + lay.mine(CORE)

    def restore(v):
        v = v.reshape(v.shape[0], 2, 2, 4, 2 * rows).transpose(0, 2, 3, 1, 4)
        v = jnp.where(mzh == 1, v[:, ::-1], v)
        v = jnp.where(mx == 1, v[:, :, :, ::-1], v)
        return v.reshape(v.shape[0], width)

    up_z, up_x, x1, x2, x3, g1, down_xz, small, qkv_cols, proj0 = after(
        (up_z, up_x, x1, x2, x3, g1, down_xz, small, qkv_cols, proj_weight)
    )
    gains, b_out, b_up, b_qkv, docs, cosine, sine = prepare(small, bit_of, freq, sign, rows, unit, count)
    xa = join([x0, x1, x2, x3])
    xb = flip(xa, CORE)
    up_xz = flip(up_z, X)
    g3 = flip(g1, Y)
    proj_z = lay.exchange_heads(proj0, 1 << ZH, back=True)
    proj0 = lay.exchange_heads(proj0)
    w_down = join_units([down_weight, down_x, down_z, down_xz], mine)
    gains, g0, g1, g2, g3, qkv_cols, proj0, proj_z, up_xz, xb, w_down = after(
        (gains, g0, g1, g2, g3, qkv_cols, proj0, proj_z, up_xz, xb, w_down)
    )
    ga = join([g0, g1, g2, g3])
    gb = flip(ga, CORE)
    qkv_z = flip(qkv_cols, ZH)
    qkv_x = flip(qkv_cols, X)
    proj_x = flip(proj0, X)
    first, second, stats = norms([xa, xb], gains, count)
    w_up = [v.reshape(-1, hidden) for v in (up_cols, up_z, up_x, up_xz)]
    act, slope = feed_up(second, w_up, b_up)
    act, qkv_z, qkv_x, proj_x, gb = after((act, qkv_z, qkv_x, proj_x, gb))
    g = [ga, gb]
    x = [xa, xb]
    qkv_xz = flip(qkv_z, X)

    def hidden_block(step, s):
        return (s[0] ^ (1 - lax.rem(step, 2))) * 2 + (s[1] ^ jnp.where(step < 2, 1, 0))

    def feature_block(step, s):
        return 3 - step

    down_s1, down_s0, down_k1, down_k0 = weight_grad(act, g, mine, hidden_block, us=15)
    down_g1 = flip(down_s1, X)
    slope, qkv_xz, down_k1, proj_z = after((slope, qkv_xz, down_k1, proj_z))
    proj_xz = flip(proj_z, X)
    d_up, column_up = feed_back(g, w_down, slope)
    d_up, down_s0 = after((d_up, down_s0))
    down_g0 = flip(down_s0, X)
    up_s1, up_s0, up_k1, up_k0 = weight_grad(second, [d_up], mine, feature_block, us=12)
    up_g1 = flip(up_s1, X)

    down_g1, up_k1, proj_xz = after((down_g1, up_k1, proj_xz))
    down_sent = add_half(down_k1, down_g1, unit, 0)
    down_got = flip(down_sent, ZH)
    w_proj = join_heads([proj0, proj_z, proj_x, proj_xz], mine)
    w_qkv = [v.reshape(-1, 3 * HEAD) for v in (qkv_cols, qkv_z, qkv_x, qkv_xz)]
    (first_,) = after((first,), down_sent)
    mixed, d_qkv, column_qkv = attend(first_, w_qkv, b_qkv, g, w_proj, cosine, sine, docs)
    act, mixed, d_qkv, down_g0 = after((act, mixed, d_qkv, down_g0))
    *out_s, out_k = branch_sum(act, w_down, mixed, w_proj)
    out_g = [flip(v, CORE) for v in out_s]
    d_qkv, out_k, up_g1, up_s0, down_got = after((d_qkv, out_k, up_g1, up_s0, down_got))
    up_g0 = flip(up_s0, X)
    up_sent = add_half(up_k1, up_g1, up_k1.shape[0], 0)
    up_got = flip(up_sent, ZH)
    *out_g, out_k = after((*out_g, out_k), up_sent)
    out_s1, out_s0, out_k = fold_tokens(out_k, out_g)
    out_g1 = flip(out_s1, Y)
    out_g0 = flip(out_s0, Y)
    d_qkv, out_k = after((d_qkv, out_k))
    qkv_s1, qkv_s0, qkv_k1, qkv_k0 = weight_grad(first, [d_qkv], mine, feature_block, us=10)
    qkv_g1 = flip(qkv_s1, X)
    mixed, qkv_k1 = after((mixed, qkv_k1))
    proj_s, proj_k = head_grad(mixed, g, mine)
    out_g1, out_k, up_g0, proj_s, qkv_s0 = after((out_g1, out_k, up_g0, proj_s, qkv_s0))
    qkv_g0 = flip(qkv_s0, X)
    proj_g = flip(proj_s, X)
    out_sent = add_half(out_k, out_g1, count, 1)
    out_got = flip(out_sent, ZL)

    d_up, d_qkv = after((d_up, d_qkv), out_sent)
    *edge_s, edge_k, sums = edge_sum(d_up, w_up, d_qkv, w_qkv, x, stats, gains)

    *edge_s, edge_k, qkv_g1, up_got, out_g0, sums = after((*edge_s, edge_k, qkv_g1, up_got, out_g0, sums))
    edge_g = [flip(v, CORE) for v in edge_s]
    qkv_sent = add_half(qkv_k1, qkv_g1, qkv_k1.shape[0], 0)
    qkv_got = flip(qkv_sent, ZH)
    up_got, edge_k = after((up_got, edge_k), qkv_sent)
    up_sum = (up_k0 + up_g0.astype(F32) + up_got.astype(F32)).astype(BF16)
    up_back = lay.to_columns(up_sum.reshape(8, rows, hidden))
    edge_k, up_sum, out_got = after((edge_k, up_sum, out_got))
    *edge_g, edge_k = after((*edge_g, edge_k))
    edge_s1, edge_s0, edge_k = fold_tokens(edge_k, edge_g)
    edge_g1 = flip(edge_s1, Y)

    edge_k, sums, column_up, column_qkv = after((edge_k, sums, column_up, column_qkv))
    column_out = jnp.sum(cotangent.astype(F32), axis=0)
    spread_up = lax.dynamic_update_slice(jnp.zeros((HEADS, hidden), F32), column_up, (here, 0))
    spread_up = spread_up.reshape(2, 2, 2, 2, 2, unit).transpose(3, 0, 1, 4, 2, 5)
    spread_qkv = lax.dynamic_update_slice(jnp.zeros((HEADS, 3 * HEAD), F32), column_qkv, (here, 0))
    spread_qkv = spread_qkv.reshape(2, 2, 2, 3, HEAD).transpose(3, 2, 0, 1, 4)
    sums = restore(sums[:4])
    flat = [v.reshape(n, -1) for v in (sums[0], sums[1], sums[2], sums[3], column_out, spread_qkv, spread_up)]
    flat = jnp.concatenate(flat, axis=1)
    flat, up_back = after((flat, up_back))
    sums = lax.all_to_all(flat, AXIS, split_axis=0, concat_axis=0, tiled=True)
    qkv_got, qkv_g0, sums, proj_g, edge_k = after((qkv_got, qkv_g0, sums, proj_g, edge_k))
    qkv_sum = (qkv_k0 + qkv_g0.astype(F32) + qkv_got.astype(F32)).astype(BF16)
    qkv_back = lay.to_columns(qkv_sum.reshape(8, rows, 3 * HEAD))
    proj_sum = (proj_k + proj_g.astype(F32)).reshape(2, rows, width)
    proj_kept = lax.dynamic_index_in_dim(proj_sum, mzh, 0, keepdims=False).astype(BF16)
    proj_sent = lax.dynamic_index_in_dim(proj_sum, 1 - mzh, 0, keepdims=False).astype(BF16)
    proj_own = lay.exchange_heads(proj_kept)
    proj_got = lay.exchange_heads(proj_sent, 1 << ZH)
    edge_g1, edge_s0, qkv_sum, proj_sent = after((edge_g1, edge_s0, qkv_sum, proj_sent))
    edge_g0 = flip(edge_s0, Y)
    edge_sent = add_half(edge_k, edge_g1, count, 1)
    edge_got = flip(edge_sent, ZL)
    qkv_back, up_back, out_k, down_k0 = after((qkv_back, up_back, out_k, down_k0), edge_sent)
    grad_up = join_up(up_back)
    grad_qkv = join_qkv(qkv_back)
    layer_out = total([inputs, b_out, out_k, out_g0, out_got], count)
    grad_down = total([down_k0, down_g0, down_got], unit)
    edge_got, edge_g0, edge_k, layer_out, grad_down, grad_up, grad_qkv = after(
        (edge_got, edge_g0, edge_k, layer_out, grad_down, grad_up, grad_qkv)
    )
    grad_inputs = finish(edge_k, edge_g0, edge_got, x0, cotangent, mine)
    proj_own, proj_got, grad_inputs = after((proj_own, proj_got, grad_inputs))
    grad_proj = proj_own.astype(F32) + proj_got.astype(F32)
    sums = jnp.sum(sums, axis=0)
    got, at = [], 0
    for size in [rows] * 5 + [3 * rows, unit]:
        got.append(sums[at : at + size])
        at += size
    return (
        layer_out,
        grad_inputs,
        got[0],
        got[1],
        got[2],
        got[3],
        grad_qkv,
        got[5],
        grad_proj,
        got[4],
        grad_up,
        got[6],
        grad_down,
        got[4],
    )


def solution(mesh):
    tokens, rows = P(AXIS, None), P(AXIS)
    return jax.shard_map(
        local_tuned if mesh.shape[AXIS] == 32 else local_any,
        mesh=mesh,
        in_specs=(tokens, tokens, rows, rows, rows, rows, tokens, rows, tokens, rows, tokens, rows, tokens, rows, tokens),
        out_specs=(tokens, tokens, rows, rows, rows, rows, tokens, rows, tokens, rows, tokens, rows, tokens, rows),
        check_vma=False,
    )
```

```python
import functools

import jax
import jax.numpy as jnp
import numpy as np
from jax import lax
from jax.experimental import pallas as pl
from jax.experimental.pallas import tpu as pltpu
from jax.sharding import PartitionSpec as P

HEADS = 8
HEAD = 256
ROT = 64
EPS = 1e-05
MASKED = -1e30
AXIS = "fsdp"
BF16 = jnp.bfloat16
F32 = jnp.float32

SPLIT_BITS = {32: (3, 2, 0), 128: (3, 1, 0)}


def attention_kernel(qkv_ref, turn_ref, docs_row_ref, docs_col_ref, d_mixed_ref, mixed_ref, d_qkv_ref, column_ref):
    half = ROT // 2
    cosine = turn_ref[0]
    sine = turn_ref[1]
    lanes = cosine.shape[1]
    lane = lax.broadcasted_iota(jnp.int32, cosine.shape, 1)

    def swap(v):
        return jnp.where(lane < half, pltpu.roll(v, lanes - half, 1), pltpu.roll(v, half, 1))

    def turn(v, sign):
        front = v[:, :lanes]
        front = front * cosine + sign * (swap(front) * sine)
        return jnp.concatenate([front, v[:, lanes:]], axis=1)

    rq = turn(qkv_ref[:, :HEAD], 1.0).astype(BF16)
    rk = turn(qkv_ref[:, HEAD : 2 * HEAD], 1.0).astype(BF16)
    rv = qkv_ref[:, 2 * HEAD :].astype(BF16)
    count = rq.shape[0]
    here = lax.broadcasted_iota(jnp.int32, (count, count), 0)
    there = lax.broadcasted_iota(jnp.int32, (count, count), 1)
    allowed = (docs_row_ref[0] == docs_col_ref[0]) & (there <= here)
    scale = HEAD ** (-0.5)
    rows = (((1,), (1,)), ((), ()))
    firsts = (((0,), (0,)), ((), ()))
    raw = lax.dot_general(rq, rk, rows, preferred_element_type=F32)
    scores = jnp.where(allowed, raw * scale, MASKED)
    expo = jnp.exp(scores - jnp.max(scores, axis=1, keepdims=True))
    probs = expo / jnp.sum(expo, axis=1, keepdims=True)
    weights = probs.astype(BF16)
    mixed_ref[...] = jnp.dot(weights, rv, preferred_element_type=F32).astype(BF16)
    d_mixed = d_mixed_ref[...]
    d_prob = lax.dot_general(d_mixed, rv, rows, preferred_element_type=F32)
    d_score = probs * (d_prob - jnp.sum(probs * d_prob, axis=1, keepdims=True))
    d_raw = (d_score * scale).astype(BF16)
    d_rq = jnp.dot(d_raw, rk, preferred_element_type=F32)
    d_rk = lax.dot_general(d_raw, rq, firsts, preferred_element_type=F32)
    d_rv = lax.dot_general(weights, d_mixed, firsts, preferred_element_type=F32)
    d_qkv = jnp.concatenate([turn(d_rq, -1.0), turn(d_rk, -1.0), d_rv], axis=1).astype(BF16)
    d_qkv_ref[...] = d_qkv

    @pl.when(pl.program_id(0) == 0)
    def _():
        column_ref[...] = jnp.zeros_like(column_ref)

    column_ref[...] += jnp.sum(d_qkv.astype(F32), axis=0, keepdims=True)


def attention(qkv, cosine, sine, docs, d_mixed):
    rows, count = docs.shape
    turns = jnp.stack([cosine, sine])
    lanes = turns.shape[2]
    return pl.pallas_call(
        attention_kernel,
        grid=(rows,),
        in_specs=[
            pl.BlockSpec((count, 3 * HEAD), lambda i: (i, 0)),
            pl.BlockSpec((2, count, lanes), lambda i: (0, i, 0)),
            pl.BlockSpec((1, 1, count), lambda i: (i, 0, 0)),
            pl.BlockSpec((1, count, 1), lambda i: (i, 0, 0)),
            pl.BlockSpec((count, HEAD), lambda i: (i, 0)),
        ],
        out_specs=[
            pl.BlockSpec((count, HEAD), lambda i: (i, 0)),
            pl.BlockSpec((count, 3 * HEAD), lambda i: (i, 0)),
            pl.BlockSpec((1, 3 * HEAD), lambda i: (0, 0)),
        ],
        out_shape=[
            jax.ShapeDtypeStruct((rows * count, HEAD), BF16),
            jax.ShapeDtypeStruct((rows * count, 3 * HEAD), BF16),
            jax.ShapeDtypeStruct((1, 3 * HEAD), F32),
        ],
        compiler_params=pltpu.CompilerParams(vmem_limit_bytes=32 * 1024 * 1024),
        cost_estimate=pl.CostEstimate(
            flops=16 * rows * count * count * HEAD, bytes_accessed=20 * rows * count * HEAD, transcendentals=rows * count * count
        ),
    )(qkv, turns, docs[:, None, :], docs[:, :, None], d_mixed)


def times_rows(left, right):
    return jnp.einsum("tc,nc->tn", left, right, preferred_element_type=F32)


def times_tokens(left, right):
    return jnp.einsum("tn,td->nd", left, right, preferred_element_type=F32)


class Layout:
    def __init__(self, count):
        self.count = count
        self.bits = count.bit_length() - 1
        self.h_bits = SPLIT_BITS.get(count, (2, 1, 0))
        self.t_bits = tuple(b for b in range(self.bits - 1, -1, -1) if b not in self.h_bits)
        head_bits = tuple(range(self.bits - 1, self.bits - 4, -1))
        self.swap = {b: b for b in range(self.bits)}
        for a, b in zip([a for a in head_bits if a not in self.h_bits], [b for b in self.h_bits if b not in head_bits]):
            self.swap[a], self.swap[b] = b, a
        self.groups = []
        for t in range(1 << len(self.t_bits)):
            base = sum(((t >> (len(self.t_bits) - 1 - i)) & 1) << b for i, b in enumerate(self.t_bits))
            self.groups.append(
                [base | sum(((h >> (2 - i)) & 1) << b for i, b in enumerate(self.h_bits)) for h in range(8)]
            )

    def swapped(self, device):
        return sum(((device >> b) & 1) << self.swap[b] for b in range(self.bits))

    def axis(self, bit):
        return self.bits - 1 - bit

    def flip(self, value, bit):
        return lax.ppermute(value, AXIS, [(d, d ^ (1 << bit)) for d in range(self.count)])

    def exchange_heads(self, value, flipped=0, back=False):
        pairs = [(d, self.swapped(d ^ flipped)) for d in range(self.count)]
        return lax.ppermute(value, AXIS, [(b, a) for a, b in pairs] if back else pairs)

    def mine(self, bit):
        return (lax.axis_index(AXIS) >> bit) & 1

    def gather(self, value):
        pieces = {0: value}
        for bit in self.t_bits:
            pieces.update({key | (1 << bit): self.flip(piece, bit) for key, piece in list(pieces.items())})
        return pieces

    def place(self, pieces, order, shape):
        some = pieces[0]
        whole = jnp.zeros(shape, some.dtype)
        block = tuple(1 if bit is not None else size for bit, size in zip(order, shape))
        block = block + shape[len(order) :]
        for key, piece in pieces.items():
            starts = [0 if bit is None else self.mine(bit) ^ ((key >> bit) & 1) for bit in order]
            starts = starts + [0] * (len(shape) - len(order))
            whole = lax.dynamic_update_slice(whole, piece.reshape(block), starts)
        return whole

    def reduce(self, part, order):
        order = list(order)
        for bit in reversed(self.t_bits):
            axis = order.index(bit)
            mine = self.mine(bit)
            away = lax.dynamic_index_in_dim(part, 1 - mine, axis, keepdims=False).astype(BF16)
            keep = lax.dynamic_index_in_dim(part, mine, axis, keepdims=False)
            part = keep + self.flip(away, bit).astype(F32)
            order.pop(axis)
        return part

    def gather_tokens(self, value):
        pieces = [value]
        for bit in self.h_bits[:-1]:
            pieces = pieces + [self.flip(piece, bit) for piece in pieces]
        own = jnp.concatenate(pieces, axis=0)
        return jnp.concatenate([own, self.flip(own, self.h_bits[-1])], axis=0)

    def reduce_tokens(self, part):
        for bit in reversed(self.h_bits):
            half = part.shape[0] // 2
            away = part[half:].astype(BF16)
            part = part[:half].astype(F32) + self.flip(away, bit).astype(F32)
        return part

    def to_columns(self, value):
        return lax.all_to_all(value, AXIS, split_axis=0, concat_axis=0, tiled=True, axis_index_groups=self.groups)


def local_any(
    inputs,
    doc_ids,
    attn_gain,
    attn_shift,
    ffn_gain,
    ffn_shift,
    qkv_weight,
    qkv_bias,
    proj_weight,
    proj_bias,
    up_weight,
    up_bias,
    down_weight,
    down_bias,
    cotangent,
):
    n = lax.axis_size(AXIS)
    lay = Layout(n)
    bits = lay.bits
    two = (2,) * bits
    count, width = inputs.shape
    rows = width // n
    unit = up_bias.shape[0]
    hidden = unit * (n // HEADS)
    h_axes = [lay.axis(b) for b in lay.h_bits]
    t_axes = [lay.axis(b) for b in lay.t_bits]

    small = jnp.concatenate(
        [
            attn_gain,
            attn_shift,
            ffn_gain,
            ffn_shift,
            proj_bias,
            down_bias,
            qkv_bias,
            up_bias,
            doc_ids[0].astype(BF16),
        ]
    )
    small = lax.all_to_all(
        jnp.broadcast_to(small[None], (n, small.shape[0])), AXIS, split_axis=0, concat_axis=0, tiled=True
    ).astype(F32)
    sizes = [rows] * 6 + [3 * rows, unit, count]
    vectors, at = [], 0
    for size in sizes:
        vectors.append(small[:, at : at + size])
        at += size
    a_gain, a_shift, f_gain, f_shift, b_proj, b_down = [v.reshape(1, width) for v in vectors[:6]]

    heads_at = [2 + (bits - 1 - lay.swap[b]) for b in lay.h_bits]
    up_cols = up_weight.reshape((rows,) + two + (unit,))
    up_cols = up_cols.transpose([1 + a for a in h_axes] + [0] + [1 + a for a in t_axes] + [bits + 1])
    up_cols = lay.to_columns(up_cols.reshape(HEADS, rows, hidden))
    qkv_cols = qkv_weight.reshape(rows, 3, 2, 2, 2, HEAD).transpose(heads_at + [0, 1, 5])
    qkv_cols = lay.to_columns(qkv_cols.reshape(HEADS, rows, 3 * HEAD))

    x = lay.gather_tokens(inputs)
    row_order = [b if b in lay.t_bits else None for b in range(bits - 1, -1, -1)]
    w_up = lay.place(lay.gather(up_cols), row_order, two + (rows, hidden)).reshape(width, hidden)
    g = lay.gather_tokens(cotangent)
    t_two = (2,) * len(lay.t_bits)
    w_down = lay.place(lay.gather(down_weight), lay.t_bits, t_two + (unit, width)).reshape(hidden, width)
    proj_order = [lay.swap[b] for b in range(bits - 4, -1, -1)]
    w_proj = lay.place(
        lay.gather(lay.exchange_heads(proj_weight)), proj_order, t_two + (rows, width)
    ).reshape(HEAD, width)
    w_qkv = lay.place(lay.gather(qkv_cols), row_order, two + (rows, 3 * HEAD)).reshape(width, 3 * HEAD)

    b_up = vectors[7].reshape(two + (unit,)).transpose(h_axes + t_axes + [bits]).reshape(HEADS, hidden)
    b_qkv = vectors[6].reshape((3, 2, 2, 2, HEAD)).transpose([a - 1 for a in heads_at] + [0, 4]).reshape(HEADS, 3 * HEAD)
    here = sum(lay.mine(b) << (2 - i) for i, b in enumerate(lay.h_bits))
    b_up = lax.dynamic_index_in_dim(b_up, here, 0, keepdims=True)
    b_qkv = lax.dynamic_index_in_dim(b_qkv, here, 0, keepdims=True)
    me = lax.axis_index(AXIS)
    docs = []
    for j in range(HEADS):
        other = me ^ sum(((j >> i) & 1) << b for i, b in enumerate(lay.h_bits))
        docs.append(lax.dynamic_index_in_dim(vectors[8], other, 0, keepdims=True))
    docs = jnp.concatenate(docs, axis=0).astype(jnp.int32)

    index = jnp.arange(count, dtype=jnp.int32)
    same = docs[:, :, None] == docs[:, None, :]
    position = jnp.sum((same & (index[None, None, :] < index[None, :, None])).astype(jnp.int32), axis=2).reshape(-1)
    freq = 10000.0 ** (-2.0 * jnp.arange(ROT // 2, dtype=F32) / ROT)
    angle = position.astype(F32)[:, None] * freq[None, :]
    cosine, sine = jnp.cos(angle), jnp.sin(angle)
    rest = 128 - ROT
    cosine = jnp.concatenate([cosine, cosine, jnp.ones((angle.shape[0], rest), F32)], axis=1)
    sine = jnp.concatenate([-sine, sine, jnp.zeros((angle.shape[0], rest), F32)], axis=1)

    value = x.astype(F32)
    center = value - jnp.mean(value, axis=-1, keepdims=True)
    scale = lax.rsqrt(jnp.mean(center * center, axis=-1, keepdims=True) + EPS)
    xhat = center * scale
    first = (xhat * a_gain + a_shift).astype(BF16)
    second = (xhat * f_gain + f_shift).astype(BF16)

    up = jnp.dot(second, w_up, preferred_element_type=F32) + b_up
    phi_sum = 0.5 * (1.0 + lax.erf(up * (0.5**0.5)))
    act = (up * phi_sum).astype(BF16)
    slope = phi_sum + up * jnp.exp(-0.5 * up * up) * 0.3989422804014327
    part_down = times_tokens(act, g)
    d_act = times_rows(g, w_down)
    d_up = (d_act * slope).astype(BF16)
    part_up = times_tokens(second, d_up)
    d_second = times_rows(d_up, w_up)

    d_mixed = times_rows(g, w_proj).astype(BF16)
    qkv = jnp.dot(first, w_qkv, preferred_element_type=F32) + b_qkv
    mixed, d_qkv, column_qkv = attention(qkv, cosine, sine, docs, d_mixed)
    part_proj = times_tokens(mixed, g)
    part_qkv = times_tokens(first, d_qkv)
    d_first = times_rows(d_qkv, w_qkv)

    branches = jnp.dot(act, w_down, preferred_element_type=F32) + jnp.dot(mixed, w_proj, preferred_element_type=F32)
    value_own = inputs.astype(F32)
    layer_out = lay.reduce_tokens(branches) + value_own + b_proj + b_down

    edge = lay.reduce_tokens(d_first * a_gain + d_second * f_gain)
    center_own = value_own - jnp.mean(value_own, axis=-1, keepdims=True)
    scale_own = lax.rsqrt(jnp.mean(center_own * center_own, axis=-1, keepdims=True) + EPS)
    xhat_own = center_own * scale_own
    back = edge - jnp.mean(edge, axis=-1, keepdims=True) - xhat_own * jnp.mean(edge * xhat_own, axis=-1, keepdims=True)
    grad_inputs = cotangent.astype(F32) + back * scale_own

    grad_down = lay.reduce(part_down.reshape(t_two + (unit, width)), lay.t_bits)
    grad_proj = lay.reduce(part_proj.reshape(t_two + (rows, width)), proj_order)
    grad_proj = lay.exchange_heads(grad_proj.astype(BF16)).astype(F32)
    grad_up = lay.reduce(part_up.reshape(two + (rows, hidden)), row_order).reshape(HEADS, rows, hidden)
    grad_up = lay.to_columns(grad_up.astype(BF16)).astype(F32)
    axes = h_axes + t_axes
    grad_up = grad_up.reshape((2, 2, 2, rows) + t_two + (unit,))
    back_axes = [3] + [
        (axes.index(a) if axes.index(a) < 3 else axes.index(a) + 1) for a in range(bits)
    ] + [bits + 1]
    grad_up = grad_up.transpose(back_axes).reshape(rows, -1)
    grad_qkv = lay.reduce(part_qkv.reshape(two + (rows, 3 * HEAD)), row_order).reshape(HEADS, rows, 3 * HEAD)
    grad_qkv = lay.to_columns(grad_qkv.astype(BF16)).astype(F32)
    grad_qkv = grad_qkv.reshape(2, 2, 2, rows, 3, HEAD)
    grad_qkv = grad_qkv.transpose([3, 4] + [heads_at.index(a) for a in (2, 3, 4)] + [5]).reshape(rows, -1)

    column_up = jnp.sum(d_up.astype(F32), axis=0)
    column_out = jnp.sum(cotangent.astype(F32), axis=0)
    spread_up = lax.dynamic_update_slice(jnp.zeros((HEADS, hidden), F32), column_up[None], (here, 0))
    spread_up = spread_up.reshape((2,) * bits + (unit,)).transpose(
        [(axes.index(a)) for a in range(bits)] + [bits]
    )
    spread_qkv = lax.dynamic_update_slice(jnp.zeros((HEADS, 3 * HEAD), F32), column_qkv, (here, 0))
    spread_qkv = spread_qkv.reshape(2, 2, 2, 3, HEAD).transpose([3] + [heads_at.index(a) for a in (2, 3, 4)] + [4])
    sums = [
        jnp.sum(d_first * xhat, axis=0),
        jnp.sum(d_first, axis=0),
        jnp.sum(d_second * xhat, axis=0),
        jnp.sum(d_second, axis=0),
        column_out,
        spread_qkv,
        spread_up,
    ]
    sums = jnp.concatenate([s.reshape(n, -1) for s in sums], axis=1)
    sums = jnp.sum(lax.all_to_all(sums, AXIS, split_axis=0, concat_axis=0, tiled=True), axis=0)
    got, at = [], 0
    for size in [rows] * 5 + [3 * rows, unit]:
        got.append(sums[at : at + size])
        at += size
    return (
        layer_out,
        grad_inputs,
        got[0],
        got[1],
        got[2],
        got[3],
        grad_qkv,
        got[5],
        grad_proj,
        got[4],
        grad_up,
        got[6],
        grad_down,
        got[4],
    )


ZH, ZL, Y, X, CORE = 4, 3, 2, 1, 0
ROWS = (((1,), (1,)), ((), ()))
COST = 0.45e9
FIRSTS = (((0,), (0,)), ((), ()))


def after(values, *done):
    return lax.optimization_barrier(tuple(values) + done)[: len(values)]


def flip(value, bit):
    return lax.ppermute(value, AXIS, [(d, d ^ (1 << bit)) for d in range(lax.axis_size(AXIS))])


def call(body, grid, in_specs, out_specs, out_shape, args, scalars=None, limit=40, us=1.0, aliases=None):
    extra = dict(
        out_shape=out_shape,
        compiler_params=pltpu.CompilerParams(vmem_limit_bytes=limit * 1024 * 1024),
        cost_estimate=pl.CostEstimate(flops=int(us * COST), bytes_accessed=1024, transcendentals=0),
        input_output_aliases=aliases or {},
    )
    if scalars is None:
        return pl.pallas_call(body, grid=grid, in_specs=in_specs, out_specs=out_specs, **extra)(*args)
    spec = pltpu.PrefetchScalarGridSpec(num_scalar_prefetch=1, grid=grid, in_specs=in_specs, out_specs=out_specs)
    return pl.pallas_call(body, grid_spec=spec, **extra)(scalars, *args)


def shape(dims, dtype):
    return jax.ShapeDtypeStruct(dims, dtype)


def bits_of(number, count):
    return [(number >> (count - 1 - i)) & 1 for i in range(count)]


def order_columns(value, mine):
    count, width = value.shape
    wide = width // 16

    def body(mine_ref, x_ref, o_ref):
        for j in range(16):
            xr, zr, b, c = bits_of(j, 4)
            source = (zr ^ mine_ref[0]) * 8 + b * 4 + c * 2 + (xr ^ mine_ref[1])
            o_ref[:, j * wide : (j + 1) * wide] = x_ref[:, pl.ds(pl.multiple_of(source * wide, wide), wide)]

    block = pl.BlockSpec((count, width), lambda i, s: (0, 0))
    return call(body, (1,), [block], block, shape((count, width), value.dtype), (value,), mine)


def split_columns(up_weight, qkv_weight):
    rows, ff = up_weight.shape
    unit = ff // 32
    hidden = 4 * unit

    def body(u_ref, q_ref, o_ref):
        for h in range(8):
            zl, y, c = bits_of(h, 3)
            for t in range(4):
                zh, x = bits_of(t, 2)
                e = zh * 16 + zl * 8 + y * 4 + x * 2 + c
                o_ref[h, :, t * unit : (t + 1) * unit] = u_ref[:, e * unit : (e + 1) * unit]
            head = c * 4 + zl * 2 + y
            for k in range(3):
                at = (k * HEADS + head) * HEAD
                o_ref[h, :, hidden + k * HEAD : hidden + (k + 1) * HEAD] = q_ref[:, at : at + HEAD]

    def block(*dims):
        return pl.BlockSpec(dims, lambda i: (0,) * len(dims))

    return call(
        body,
        (1,),
        [block(rows, ff), block(rows, 3 * HEADS * HEAD)],
        block(8, rows, hidden + 3 * HEAD),
        shape((8, rows, hidden + 3 * HEAD), BF16),
        (up_weight, qkv_weight),
    )


def join_up(parts):
    _, rows, hidden = parts.shape
    unit = hidden // 4

    def body(p_ref, o_ref):
        for h in range(8):
            zl, y, c = bits_of(h, 3)
            for t in range(4):
                zh, x = bits_of(t, 2)
                e = zh * 16 + zl * 8 + y * 4 + x * 2 + c
                o_ref[:, e * unit : (e + 1) * unit] = p_ref[h, :, t * unit : (t + 1) * unit].astype(F32)

    return call(
        body,
        (1,),
        [pl.BlockSpec(parts.shape, lambda i: (0, 0, 0))],
        pl.BlockSpec((rows, 8 * hidden), lambda i: (0, 0)),
        shape((rows, 8 * hidden), F32),
        (parts,),
    )


def join_qkv(parts):
    _, rows, _ = parts.shape

    def body(p_ref, o_ref):
        for h in range(8):
            zl, y, c = bits_of(h, 3)
            head = c * 4 + zl * 2 + y
            for k in range(3):
                at = (k * HEADS + head) * HEAD
                o_ref[:, at : at + HEAD] = p_ref[h, :, k * HEAD : (k + 1) * HEAD].astype(F32)

    return call(
        body,
        (1,),
        [pl.BlockSpec(parts.shape, lambda i: (0, 0, 0))],
        pl.BlockSpec((rows, 3 * HEADS * HEAD), lambda i: (0, 0)),
        shape((rows, 3 * HEADS * HEAD), F32),
        (parts,),
    )


def prepare(small, place, freq, sign, rows, unit, count):
    n, _, lanes = small.shape
    width = n * rows
    up_at, gains_at = count // lanes, (count + unit) // lanes
    out_at = gains_at + 2
    qkv_at = out_at + 1

    def body(place_ref, small_ref, f_ref, s_ref, gains_ref, out_ref, up_ref, qkv_ref, docs_ref, cos_ref, sin_ref, all_ref):
        mzh, mx, mzl, my, mc, me = [place_ref[k] for k in range(6)]
        step = pl.program_id(0)

        @pl.when(step == 0)
        def _():
            all_ref[...] = small_ref[...].astype(F32)
            gains_ref[...] = jnp.zeros_like(gains_ref)

            for j in range(16):
                xr, zr, b, c = bits_of(j, 4)
                source = 2 * ((zr ^ mzh) * 8 + b * 4 + c * 2 + (xr ^ mx))
                here = slice(2 * j * rows, 2 * (j + 1) * rows)
                left, right = all_ref[source], all_ref[source + 1]
                for k in range(4):
                    at, part = gains_at + k // 2, slice(k % 2 * rows, (k % 2 + 1) * rows)
                    gains_ref[k : k + 1, here] = jnp.concatenate([left[at : at + 1, part], right[at : at + 1, part]], axis=1)
                left, right = [v[:, :rows] + v[:, rows:] for v in (all_ref[2 * j, out_at : out_at + 1], all_ref[2 * j + 1, out_at : out_at + 1])]
                out_ref[:, here] = jnp.concatenate([left, right], axis=1)
            for t in range(4):
                zh, x = bits_of(t, 2)
                device = zh * 16 + mzl * 8 + my * 4 + x * 2 + mc
                mine_up = all_ref[device]
                for k in range(unit // lanes):
                    up_ref[:, t * unit + k * lanes : t * unit + (k + 1) * lanes] = mine_up[up_at + k : up_at + k + 1]
            head = mc * 4 + mzl * 2 + my
            for k in range(3 * HEAD // rows):
                chunk = (k // (HEAD // rows) * HEADS + head) * (HEAD // rows) + k % (HEAD // rows)
                third = all_ref[chunk // 3]
                part = lax.rem(chunk, 3)
                first, last = third[qkv_at : qkv_at + 1], third[qkv_at + 1 : qkv_at + 2]
                qkv_ref[:, k * rows : (k + 1) * rows] = jnp.where(
                    part == 0, first[:, :rows], jnp.where(part == 1, first[:, rows:], last[:, :rows])
                )

        other = me ^ (((step & 1) << ZL) | (((step >> 1) & 1) << Y) | (((step >> 2) & 1) << CORE))
        held = all_ref[other]
        docs = jnp.concatenate([held[k : k + 1] for k in range(count // lanes)], axis=1)
        docs_ref[0] = docs
        across = jnp.broadcast_to(docs, (count, count))
        here = lax.broadcasted_iota(jnp.int32, (count, count), 0)
        there = lax.broadcasted_iota(jnp.int32, (count, count), 1)
        earlier = (across == across.T) & (there < here)
        position = jnp.sum(earlier.astype(F32), axis=1, keepdims=True)
        angle = position * f_ref[...]
        cos_ref[...] = jnp.cos(angle)
        sin_ref[...] = jnp.sin(angle) * s_ref[...]

    def whole(*dims):
        return pl.BlockSpec(dims, lambda i, s: (0, 0))

    block = pl.BlockSpec((count, lanes), lambda i, s: (i, 0))
    return pl.pallas_call(
        body,
        grid_spec=pltpu.PrefetchScalarGridSpec(
            num_scalar_prefetch=1,
            grid=(8,),
            in_specs=[pl.BlockSpec(small.shape, lambda i, s: (0, 0, 0)), whole(1, lanes), whole(1, lanes)],
            out_specs=[
                whole(8, width),
                whole(1, width),
                whole(1, 4 * unit),
                whole(1, 3 * HEAD),
                pl.BlockSpec((1, 1, count), lambda i, s: (i, 0, 0)),
                block,
                block,
            ],
            scratch_shapes=[pltpu.VMEM(small.shape, F32)],
        ),
        out_shape=[
            shape((8, width), F32),
            shape((1, width), F32),
            shape((1, 4 * unit), F32),
            shape((1, 3 * HEAD), F32),
            shape((8, 1, count), F32),
            shape((8 * count, lanes), F32),
            shape((8 * count, lanes), F32),
        ],
        compiler_params=pltpu.CompilerParams(vmem_limit_bytes=40 * 1024 * 1024),
        cost_estimate=pl.CostEstimate(flops=int(COST), bytes_accessed=1024, transcendentals=0),
    )(place, small, freq, sign)


def join(pieces):
    count, width = pieces[0].shape
    blocks = len(pieces)

    def body(*refs):
        ins, out, held, sems_in, sems_out = refs[:blocks], refs[blocks], *refs[blocks + 1 :]

        def copy_in(k):
            return pltpu.make_async_copy(ins[k], held.at[k], sems_in.at[k])

        def copy_out(k):
            return pltpu.make_async_copy(held.at[k], out.at[pl.ds(k * count, count)], sems_out.at[k])

        for k in range(blocks):
            copy_in(k).start()
        for k in range(blocks):
            copy_in(k).wait()
            copy_out(k).start()
        for k in range(blocks):
            copy_out(k).wait()

    some = pl.BlockSpec(memory_space=pl.ANY)
    return pl.pallas_call(
        body,
        grid=(1,),
        in_specs=[some] * blocks,
        out_specs=some,
        out_shape=shape((blocks * count, width), pieces[0].dtype),
        scratch_shapes=[pltpu.VMEM((blocks, count, width), pieces[0].dtype)] + [pltpu.SemaphoreType.DMA((blocks,))] * 2,
        compiler_params=pltpu.CompilerParams(vmem_limit_bytes=40 * 1024 * 1024),
        cost_estimate=pl.CostEstimate(flops=int(4 * COST), bytes_accessed=1024, transcendentals=0),
    )(*pieces)


def join_heads(pieces, mine):
    rows, width = pieces[0].shape

    def body(mine_ref, *refs):
        for k, (xr, zr) in enumerate([(0, 0), (0, 1), (1, 0), (1, 1)]):
            at = ((mine_ref[1] ^ xr) * 2 + (mine_ref[0] ^ zr)) * rows
            refs[4][pl.ds(pl.multiple_of(at, rows), rows), :] = refs[k][...]

    return call(
        body,
        (1,),
        [pl.BlockSpec((rows, width), lambda i, s: (0, 0))] * 4,
        pl.BlockSpec((4 * rows, width), lambda i, s: (0, 0)),
        shape((4 * rows, width), BF16),
        tuple(pieces),
        mine,
    )


def norms(halves, gains, count):
    tokens, width = halves[0].shape
    each = tokens // count
    blocks = 2 * each

    def body(v_ref, a_ref, b_ref, first_ref, second_ref, stats_ref, x_buf, first_buf, second_buf, sems_in, sems_first, sems_second):
        def copy_in(k):
            half = (a_ref, b_ref)[k // each]
            return pltpu.make_async_copy(half.at[pl.ds(k % each * count, count)], x_buf.at[k % 2], sems_in.at[k % 2])

        def copy_first(k):
            return pltpu.make_async_copy(first_buf.at[k % 2], first_ref.at[pl.ds(k * count, count)], sems_first.at[k % 2])

        def copy_second(k):
            return pltpu.make_async_copy(second_buf.at[k % 2], second_ref.at[pl.ds(k * count, count)], sems_second.at[k % 2])

        copy_in(0).start()
        for k in range(blocks):
            slot = k % 2
            copy_in(k).wait()
            if k + 1 < blocks:
                copy_in(k + 1).start()
            if k >= 2:
                copy_first(k - 2).wait()
                copy_second(k - 2).wait()
            value = x_buf[slot].astype(F32)
            mean = jnp.mean(value, axis=-1, keepdims=True)
            center = value - mean
            scale = lax.rsqrt(jnp.mean(center * center, axis=-1, keepdims=True) + EPS)
            xhat = center * scale
            first_buf[slot] = (xhat * v_ref[0:1, :] + v_ref[1:2, :]).astype(BF16)
            second_buf[slot] = (xhat * v_ref[2:3, :] + v_ref[3:4, :]).astype(BF16)
            lane = lax.broadcasted_iota(jnp.int32, (count, 128), 1)
            stats_ref[k * count : (k + 1) * count, :] = jnp.where(lane == 0, mean, scale)
            copy_first(k).start()
            copy_second(k).start()
        for k in (blocks - 2, blocks - 1):
            copy_first(k).wait()
            copy_second(k).wait()

    some = pl.BlockSpec(memory_space=pl.ANY)
    return pl.pallas_call(
        body,
        grid=(1,),
        in_specs=[pl.BlockSpec((8, width), lambda i: (0, 0)), some, some],
        out_specs=[some, some, pl.BlockSpec((2 * tokens, 128), lambda i: (0, 0))],
        out_shape=[shape((2 * tokens, width), BF16)] * 2 + [shape((2 * tokens, 128), F32)],
        scratch_shapes=[pltpu.VMEM((2, count, width), BF16)] * 3 + [pltpu.SemaphoreType.DMA((2,))] * 3,
        compiler_params=pltpu.CompilerParams(vmem_limit_bytes=40 * 1024 * 1024),
        cost_estimate=pl.CostEstimate(flops=int(12 * COST), bytes_accessed=1024, transcendentals=0),
    )(gains, *halves)


def feed_up(second, w_up, bias, tile=512):
    tokens, width = second.shape
    deep, hidden = w_up[0].shape

    def body(s_ref, *refs):
        b_ref, act_ref, slope_ref = refs[4:]
        up = b_ref[...]
        for k in range(4):
            up = up + jnp.dot(s_ref[:, k * deep : (k + 1) * deep], refs[k][...], preferred_element_type=F32)
        phi_sum = 0.5 * (1.0 + lax.erf(up * (0.5**0.5)))
        act_ref[...] = (up * phi_sum).astype(BF16)
        slope_ref[...] = phi_sum + up * jnp.exp(-0.5 * up * up) * 0.3989422804014327

    block = pl.BlockSpec((tile, hidden), lambda i: (i, 0))
    return call(
        body,
        (tokens // tile,),
        [pl.BlockSpec((tile, width), lambda i: (i, 0))]
        + [pl.BlockSpec((deep, hidden), lambda i: (0, 0))] * 4
        + [pl.BlockSpec((1, hidden), lambda i: (0, 0))],
        [block, block],
        [shape((tokens, hidden), BF16), shape((tokens, hidden), F32)],
        (second, *w_up, bias),
        us=16,
    )


def either(steps, first_half, tile, width):
    half = steps // 2

    def spec(low):
        return pl.BlockSpec((tile, width), lambda i: (jnp.minimum(i, half - 1) if low else jnp.maximum(i - half, 0), 0))

    return [spec(first_half), spec(not first_half)]


def join_units(pieces, mine):
    unit, width = pieces[0].shape

    def body(mine_ref, *refs):
        for k, (zr, xr) in enumerate([(0, 0), (0, 1), (1, 0), (1, 1)]):
            at = ((mine_ref[0] ^ zr) * 2 + (mine_ref[1] ^ xr)) * unit
            refs[4][pl.ds(pl.multiple_of(at, unit), unit), :] = refs[k][...]

    return call(
        body,
        (1,),
        [pl.BlockSpec(p.shape, lambda i, s: (0, 0)) for p in pieces],
        pl.BlockSpec((4 * unit, width), lambda i, s: (0, 0)),
        shape((4 * unit, width), BF16),
        tuple(pieces),
        mine,
        us=3,
    )


def feed_back(g, w_down, slope, tile=512):
    half, width = g[0].shape
    steps = 2 * half // tile
    hidden = slope.shape[1]

    def body(ga_ref, gb_ref, w_ref, slope_ref, d_ref, column_ref):
        step = pl.program_id(0)

        @pl.when(step == 0)
        def _():
            column_ref[...] = jnp.zeros_like(column_ref)

        def work(g_ref):
            d_act = lax.dot_general(g_ref[...], w_ref[...], ROWS, preferred_element_type=F32)
            d_up = (d_act * slope_ref[...]).astype(BF16)
            d_ref[...] = d_up
            column_ref[...] += jnp.sum(d_up.astype(F32), axis=0, keepdims=True)

        pl.when(step < steps // 2)(lambda: work(ga_ref))
        pl.when(step >= steps // 2)(lambda: work(gb_ref))

    block = pl.BlockSpec((tile, hidden), lambda i: (i, 0))
    return call(
        body,
        (steps,),
        either(steps, True, tile, width) + [pl.BlockSpec((hidden, width), lambda i: (0, 0)), block],
        [block, pl.BlockSpec((1, hidden), lambda i: (0, 0))],
        [shape((2 * half, hidden), BF16), shape((1, hidden), F32)],
        (*g, w_down, slope),
        us=14,
    )


def weight_grad(left, right, mine, source, us=13):
    tokens, width = left.shape
    wide = right[0].shape[1]
    tile = width // 4
    count = len(right)

    def body(mine_ref, l_ref, *refs):
        part = lax.dot_general(l_ref[: tokens // count], refs[0][...], FIRSTS, preferred_element_type=F32)
        if count == 2:
            part = part + lax.dot_general(l_ref[tokens // 2 :], refs[1][...], FIRSTS, preferred_element_type=F32)
        for k, out in enumerate(refs[count:]):

            @pl.when(pl.program_id(0) == k)
            def _():
                out[...] = part.astype(out.dtype)

    return call(
        body,
        (4,),
        [pl.BlockSpec((tokens, tile), lambda i, s: (0, source(i, s)))]
        + [pl.BlockSpec(r.shape, lambda i, s: (0, 0)) for r in right],
        [pl.BlockSpec((tile, wide), lambda i, s: (0, 0))] * 4,
        [shape((tile, wide), BF16)] * 2 + [shape((tile, wide), F32)] * 2,
        (left, *right),
        mine,
        us=us,
    )


def head_grad(mixed, g, mine):
    tokens, head = mixed.shape
    width = g[0].shape[1]

    def body(mine_ref, l_ref, ga_ref, gb_ref, sent_ref, kept_ref):
        part = lax.dot_general(l_ref[: tokens // 2], ga_ref[...], FIRSTS, preferred_element_type=F32)
        part = part + lax.dot_general(l_ref[tokens // 2 :], gb_ref[...], FIRSTS, preferred_element_type=F32)
        upper, lower = part[: head // 2], part[head // 2 :]
        own = mine_ref[1] == 0
        sent_ref[...] = jnp.where(own, lower, upper).astype(BF16)
        kept_ref[...] = jnp.where(own, upper, lower)

    return call(
        body,
        (2,),
        [pl.BlockSpec((tokens, head), lambda i, s: (0, 0))]
        + [pl.BlockSpec((tokens // 2, width // 2), lambda i, s: (0, i))] * 2,
        [pl.BlockSpec((head // 2, width // 2), lambda i, s: (0, i))] * 2,
        [shape((head // 2, width), BF16), shape((head // 2, width), F32)],
        (mixed, *g),
        mine,
        us=5,
    )


def fold_tokens(kept, got):
    count, width = kept.shape
    tile = count // 4

    def body(k_ref, *refs):
        first_ref, second_ref, stays_ref = refs[4:]
        step = pl.program_id(0)
        for j in range(4):

            @pl.when(step == 3 - j)
            def _():
                total = k_ref[...].astype(F32) + refs[j][...].astype(F32)
                out = (stays_ref, stays_ref, second_ref, first_ref)[j]
                out[...] = total.astype(out.dtype)

    fixed = pl.BlockSpec((tile, width), lambda i: (0, 0))
    return call(
        body,
        (4,),
        [pl.BlockSpec((tile, width), lambda i: (3 - i, 0))] + [fixed] * 4,
        [fixed, fixed, pl.BlockSpec((tile, width), lambda i: (jnp.minimum(3 - i, 1), 0))],
        [shape((tile, width), BF16)] * 2 + [shape((2 * tile, width), F32)],
        (kept,) + tuple(got),
        us=5,
    )


def add_half(kept, got, rows, at):
    width = kept.shape[1]

    def body(k_ref, g_ref, o_ref):
        o_ref[...] = (k_ref[...] + g_ref[...].astype(F32)).astype(BF16)

    fixed = pl.BlockSpec((rows, width), lambda i: (0, 0))
    return call(
        body, (1,), [pl.BlockSpec((rows, width), lambda i: (at, 0)), fixed], fixed, shape((rows, width), BF16), (kept, got)
    )


def attend(first, w_qkv, b_qkv, g, w_proj, cosine, sine, docs):
    tokens, width = first.shape
    rows, _, count = docs.shape
    deep = w_qkv[0].shape[0]
    lanes = cosine.shape[1]
    half = ROT // 2
    scale = HEAD ** (-0.5)

    def body(f_ref, w0_ref, w1_ref, w2_ref, w3_ref, b_ref, ga_ref, gb_ref, p_ref, cos_ref, sin_ref, row_ref, mixed_ref, d_qkv_ref, column_ref):
        step = pl.program_id(0)

        @pl.when(step == 0)
        def _():
            column_ref[...] = jnp.zeros_like(column_ref)

        def work(g_ref):
            cos, sin = cos_ref[...], sin_ref[...]
            lane = lax.broadcasted_iota(jnp.int32, cos.shape, 1)

            def turn(v, sign):
                front = v[:, :lanes]
                other = jnp.where(lane < half, pltpu.roll(front, lanes - half, 1), pltpu.roll(front, half, 1))
                return jnp.concatenate([front * cos + sign * (other * sin), v[:, lanes:]], axis=1)

            qkv = b_ref[...]
            for k, w_ref in enumerate((w0_ref, w1_ref, w2_ref, w3_ref)):
                qkv = qkv + jnp.dot(f_ref[:, k * deep : (k + 1) * deep], w_ref[...], preferred_element_type=F32)
            d_mixed = lax.dot_general(g_ref[...], p_ref[...], ROWS, preferred_element_type=F32).astype(BF16)
            rq = turn(qkv[:, :HEAD], 1.0).astype(BF16)
            rk = turn(qkv[:, HEAD : 2 * HEAD], 1.0).astype(BF16)
            rv = qkv[:, 2 * HEAD :].astype(BF16)
            here = lax.broadcasted_iota(jnp.int32, (count, count), 0)
            there = lax.broadcasted_iota(jnp.int32, (count, count), 1)
            across = jnp.broadcast_to(row_ref[0], (count, count))
            allowed = (across == across.T) & (there <= here)
            raw = lax.dot_general(rq, rk, ROWS, preferred_element_type=F32)
            scores = jnp.where(allowed, raw * scale, MASKED)
            expo = jnp.exp(scores - jnp.max(scores, axis=1, keepdims=True))
            probs = expo / jnp.sum(expo, axis=1, keepdims=True)
            weights = probs.astype(BF16)
            mixed_ref[...] = jnp.dot(weights, rv, preferred_element_type=F32).astype(BF16)
            d_prob = lax.dot_general(d_mixed, rv, ROWS, preferred_element_type=F32)
            d_score = probs * (d_prob - jnp.sum(probs * d_prob, axis=1, keepdims=True))
            d_raw = (d_score * scale).astype(BF16)
            d_rq = jnp.dot(d_raw, rk, preferred_element_type=F32)
            d_rk = lax.dot_general(d_raw, rq, FIRSTS, preferred_element_type=F32)
            d_rv = lax.dot_general(weights, d_mixed, FIRSTS, preferred_element_type=F32)
            d_qkv = jnp.concatenate([turn(d_rq, -1.0), turn(d_rk, -1.0), d_rv], axis=1).astype(BF16)
            d_qkv_ref[...] = d_qkv
            column_ref[...] += jnp.sum(d_qkv.astype(F32), axis=0, keepdims=True)

        pl.when(step < rows // 2)(lambda: work(ga_ref))
        pl.when(step >= rows // 2)(lambda: work(gb_ref))

    def row(*dims):
        return pl.BlockSpec(dims, lambda i: (i, 0))

    def whole(*dims):
        return pl.BlockSpec(dims, lambda i: (0, 0))

    return call(
        body,
        (rows,),
        [
            row(count, width),
            *([whole(deep, 3 * HEAD)] * 4),
            whole(1, 3 * HEAD),
            *either(rows, True, count, width),
            whole(HEAD, width),
            row(count, lanes),
            row(count, lanes),
            pl.BlockSpec((1, 1, count), lambda i: (i, 0, 0)),
        ],
        [row(count, HEAD), row(count, 3 * HEAD), whole(1, 3 * HEAD)],
        [shape((tokens, HEAD), BF16), shape((tokens, 3 * HEAD), BF16), shape((1, 3 * HEAD), F32)],
        (first, *w_qkv, b_qkv, *g, w_proj, cosine, sine, docs),
        us=17,
    )


def branch_sum(act, w_down, mixed, w_proj, tile=512, block=256):
    tokens, hidden = act.shape
    width = w_down.shape[1]
    steps = tokens // tile
    sent = steps // 2
    each = tile // block
    blocks = sent * each

    def body(a_ref, w_ref, m_ref, p_ref, *outs):
        part = jnp.dot(a_ref[...], w_ref[...], preferred_element_type=F32)
        part = (part + jnp.dot(m_ref[...], p_ref[...], preferred_element_type=F32)).astype(BF16)
        outs[blocks][...] = part
        step = pl.program_id(0)
        for k in range(sent):

            @pl.when(step == k)
            def _():
                for j in range(each):
                    outs[k * each + j][...] = part[j * block : (j + 1) * block]

    def turned(i):
        return (lax.rem(i + sent, steps), 0)

    fixed = pl.BlockSpec((block, width), lambda i: (0, 0))
    return call(
        body,
        (steps,),
        [
            pl.BlockSpec((tile, hidden), turned),
            pl.BlockSpec((hidden, width), lambda i: (0, 0)),
            pl.BlockSpec((tile, HEAD), turned),
            pl.BlockSpec((HEAD, width), lambda i: (0, 0)),
        ],
        [fixed] * blocks + [pl.BlockSpec((tile, width), lambda i: (jnp.maximum(i - sent, 0), 0))],
        [shape((block, width), BF16)] * blocks + [shape((tokens // 2, width), BF16)],
        (act, w_down, mixed, w_proj),
        us=16,
    )


def edge_sum(d_up, w_up, d_qkv, w_qkv, x, stats, gains, tile=256):
    tokens, hidden = d_up.shape
    deep = w_up[0].shape[0]
    width = 4 * deep
    steps = tokens // tile
    sent = steps // 2

    def body(du_ref, dq_ref, xa_ref, xb_ref, stats_ref, v_ref, *refs):
        outs = refs[8:]
        sums_ref = outs[sent + 1]
        step = pl.program_id(0)

        @pl.when(step == 0)
        def _():
            sums_ref[...] = jnp.zeros_like(sums_ref)

        for k in range(4):
            part = slice(k * deep, (k + 1) * deep)
            d_second = lax.dot_general(du_ref[...], refs[k][...], ROWS, preferred_element_type=F32)
            d_first = lax.dot_general(dq_ref[...], refs[4 + k][...], ROWS, preferred_element_type=F32)
            x = jnp.where(step < sent, xb_ref[:, part], xa_ref[:, part])
            xhat = (x.astype(F32) - stats_ref[:, 0:1]) * stats_ref[:, 1:2]
            outs[sent][:, part] = (d_first * v_ref[0:1, part] + d_second * v_ref[2:3, part]).astype(BF16)
            sums_ref[0:1, part] += jnp.sum(d_first * xhat, axis=0, keepdims=True)
            sums_ref[1:2, part] += jnp.sum(d_first, axis=0, keepdims=True)
            sums_ref[2:3, part] += jnp.sum(d_second * xhat, axis=0, keepdims=True)
            sums_ref[3:4, part] += jnp.sum(d_second, axis=0, keepdims=True)

        for j in range(sent):

            @pl.when(step == j)
            def _():
                outs[j][...] = outs[sent][...]

    def turned(i):
        return (lax.rem(i + sent, steps), 0)

    def whole(*dims):
        return pl.BlockSpec(dims, lambda i: (0, 0))

    return call(
        body,
        (steps,),
        [
            pl.BlockSpec((tile, hidden), turned),
            pl.BlockSpec((tile, 3 * HEAD), turned),
            *either(steps, False, tile, width),
            pl.BlockSpec((tile, 128), turned),
            whole(8, width),
        ]
        + [whole(deep, hidden)] * 4
        + [whole(deep, 3 * HEAD)] * 4,
        [whole(tile, width)] * sent
        + [pl.BlockSpec((tile, width), lambda i: (jnp.maximum(i - sent, 0), 0)), whole(8, width)],
        [shape((tile, width), BF16)] * sent + [shape((tokens // 2, width), BF16), shape((8, width), F32)],
        (d_up, d_qkv, *x, stats, gains, *w_up, *w_qkv),
        us=28,
        limit=48,
    )


def total(parts, rows):
    width = parts[0].shape[1]

    def body(*refs):
        value = refs[0][...].astype(F32)
        for ref in refs[1:-1]:
            value = value + ref[...].astype(F32)
        refs[-1][...] = value

    return call(
        body,
        (1,),
        [pl.BlockSpec((min(rows, p.shape[0]), width), lambda i: (0, 0)) for p in parts],
        pl.BlockSpec((rows, width), lambda i: (0, 0)),
        shape((rows, width), F32),
        tuple(parts),
        us=3,
    )


def finish(edge_k, edge_g0, edge_got, x0, g, mine):
    count, width = x0.shape
    wide = width // 16

    def body(mine_ref, k_ref, a_ref, b_ref, x_ref, g_ref, o_ref):
        edge = k_ref[...] + a_ref[...].astype(F32) + b_ref[...].astype(F32)
        value = x_ref[...].astype(F32)
        center = value - jnp.mean(value, axis=-1, keepdims=True)
        scale = lax.rsqrt(jnp.mean(center * center, axis=-1, keepdims=True) + EPS)
        xhat = center * scale
        back = edge - jnp.mean(edge, axis=-1, keepdims=True) - xhat * jnp.mean(edge * xhat, axis=-1, keepdims=True)
        back = back * scale
        for j in range(16):
            xr, zr, b, c = bits_of(j, 4)
            source = (zr ^ mine_ref[0]) * 8 + b * 4 + c * 2 + (xr ^ mine_ref[1])
            place = pl.ds(pl.multiple_of(source * wide, wide), wide)
            o_ref[:, place] = g_ref[:, place].astype(F32) + back[:, j * wide : (j + 1) * wide]

    tile = count // 2
    block = pl.BlockSpec((tile, width), lambda i, s: (i, 0))
    return call(
        body, (2,), [block] * 5, block, shape((count, width), F32), (edge_k, edge_g0, edge_got, x0, g), mine, us=5
    )


def local_tuned(
    inputs,
    doc_ids,
    attn_gain,
    attn_shift,
    ffn_gain,
    ffn_shift,
    qkv_weight,
    qkv_bias,
    proj_weight,
    proj_bias,
    up_weight,
    up_bias,
    down_weight,
    down_bias,
    cotangent,
):
    n = lax.axis_size(AXIS)
    lay = Layout(n)
    count, width = inputs.shape
    rows = width // n
    unit = up_bias.shape[0]
    hidden = 4 * unit
    me = lax.axis_index(AXIS)
    mzh, mx = lay.mine(ZH), lay.mine(X)
    mine = jnp.stack([mzh, mx]).astype(jnp.int32)

    cols = split_columns(up_weight, qkv_weight)
    (x0,) = after((inputs,), cols)
    x0 = order_columns(x0, mine)
    down_z = flip(down_weight, ZH)
    down_x = flip(down_weight, X)
    cols = lay.to_columns(cols)
    x1 = flip(x0, ZL)
    x2 = flip(x0, Y)
    g2 = flip(cotangent, Y)
    small = jnp.concatenate(
        [doc_ids[0].astype(BF16), up_bias, attn_gain, attn_shift, ffn_gain, ffn_shift, proj_bias, down_bias, qkv_bias]
    )
    small = jnp.pad(small, (0, 16 * 128 - small.shape[0])).reshape(16, 128)
    small = jnp.broadcast_to(small[None], (n, 16, 128))

    cols, down_z, down_x, x1, x2, g2, small, g0 = after((cols, down_z, down_x, x1, x2, g2, small, cotangent))
    up_cols, qkv_cols = cols[:, :, :hidden], cols[:, :, hidden:]
    small = lax.all_to_all(small, AXIS, split_axis=0, concat_axis=0, tiled=True)
    up_z = flip(up_cols, ZH)
    up_x = flip(up_cols, X)
    g1 = flip(g0, ZL)
    x3 = flip(x1, Y)
    down_xz = flip(down_z, X)

    freq = 10000.0 ** (-2.0 * np.arange(ROT // 2, dtype=np.float32) / ROT)
    rest = np.zeros(128 - ROT, np.float32)
    freq = jnp.asarray(np.concatenate([freq, freq, rest])[None], F32)
    sign = jnp.asarray(np.concatenate([np.full(ROT // 2, -1.0), np.full(ROT // 2, 1.0), rest])[None], F32)
    bit_of = jnp.stack([lay.mine(b) for b in (ZH, X, ZL, Y, CORE)] + [me]).astype(jnp.int32)
    here = lay.mine(ZL) * 4 + lay.mine(Y) * 2 + lay.mine(CORE)

    def restore(v):
        v = v.reshape(v.shape[0], 2, 2, 4, 2 * rows).transpose(0, 2, 3, 1, 4)
        v = jnp.where(mzh == 1, v[:, ::-1], v)
        v = jnp.where(mx == 1, v[:, :, :, ::-1], v)
        return v.reshape(v.shape[0], width)

    up_z, up_x, x1, x2, x3, g1, down_xz, small, qkv_cols, proj0 = after(
        (up_z, up_x, x1, x2, x3, g1, down_xz, small, qkv_cols, proj_weight)
    )
    gains, b_out, b_up, b_qkv, docs, cosine, sine = prepare(small, bit_of, freq, sign, rows, unit, count)
    xa = join([x0, x1, x2, x3])
    xb = flip(xa, CORE)
    up_xz = flip(up_z, X)
    g3 = flip(g1, Y)
    proj_z = lay.exchange_heads(proj0, 1 << ZH, back=True)
    proj0 = lay.exchange_heads(proj0)
    w_down = join_units([down_weight, down_x, down_z, down_xz], mine)
    gains, g0, g1, g2, g3, qkv_cols, proj0, proj_z, up_xz, xb, w_down = after(
        (gains, g0, g1, g2, g3, qkv_cols, proj0, proj_z, up_xz, xb, w_down)
    )
    ga = join([g0, g1, g2, g3])
    gb = flip(ga, CORE)
    qkv_z = flip(qkv_cols, ZH)
    qkv_x = flip(qkv_cols, X)
    proj_x = flip(proj0, X)
    first, second, stats = norms([xa, xb], gains, count)
    w_up = [v.reshape(-1, hidden) for v in (up_cols, up_z, up_x, up_xz)]
    act, slope = feed_up(second, w_up, b_up)
    act, qkv_z, qkv_x, proj_x, gb = after((act, qkv_z, qkv_x, proj_x, gb))
    g = [ga, gb]
    x = [xa, xb]
    qkv_xz = flip(qkv_z, X)

    def hidden_block(step, s):
        return (s[0] ^ (1 - lax.rem(step, 2))) * 2 + (s[1] ^ jnp.where(step < 2, 1, 0))

    def feature_block(step, s):
        return 3 - step

    down_s1, down_s0, down_k1, down_k0 = weight_grad(act, g, mine, hidden_block, us=15)
    down_g1 = flip(down_s1, X)
    slope, qkv_xz, down_k1, proj_z = after((slope, qkv_xz, down_k1, proj_z))
    proj_xz = flip(proj_z, X)
    d_up, column_up = feed_back(g, w_down, slope)
    d_up, down_s0 = after((d_up, down_s0))
    down_g0 = flip(down_s0, X)
    up_s1, up_s0, up_k1, up_k0 = weight_grad(second, [d_up], mine, feature_block, us=12)
    up_g1 = flip(up_s1, X)

    down_g1, up_k1, proj_xz = after((down_g1, up_k1, proj_xz))
    down_sent = add_half(down_k1, down_g1, unit, 0)
    down_got = flip(down_sent, ZH)
    w_proj = join_heads([proj0, proj_z, proj_x, proj_xz], mine)
    w_qkv = [v.reshape(-1, 3 * HEAD) for v in (qkv_cols, qkv_z, qkv_x, qkv_xz)]
    (first_,) = after((first,), down_sent)
    mixed, d_qkv, column_qkv = attend(first_, w_qkv, b_qkv, g, w_proj, cosine, sine, docs)
    act, mixed, d_qkv, down_g0 = after((act, mixed, d_qkv, down_g0))
    *out_s, out_k = branch_sum(act, w_down, mixed, w_proj)
    out_g = [flip(v, CORE) for v in out_s]
    d_qkv, out_k, up_g1, up_s0, down_got = after((d_qkv, out_k, up_g1, up_s0, down_got))
    up_g0 = flip(up_s0, X)
    up_sent = add_half(up_k1, up_g1, up_k1.shape[0], 0)
    up_got = flip(up_sent, ZH)
    *out_g, out_k = after((*out_g, out_k), up_sent)
    out_s1, out_s0, out_k = fold_tokens(out_k, out_g)
    out_g1 = flip(out_s1, Y)
    out_g0 = flip(out_s0, Y)
    d_qkv, out_k = after((d_qkv, out_k))
    qkv_s1, qkv_s0, qkv_k1, qkv_k0 = weight_grad(first, [d_qkv], mine, feature_block, us=10)
    qkv_g1 = flip(qkv_s1, X)
    mixed, qkv_k1 = after((mixed, qkv_k1))
    proj_s, proj_k = head_grad(mixed, g, mine)
    out_g1, out_k, up_g0, proj_s, qkv_s0 = after((out_g1, out_k, up_g0, proj_s, qkv_s0))
    qkv_g0 = flip(qkv_s0, X)
    proj_g = flip(proj_s, X)
    out_sent = add_half(out_k, out_g1, count, 1)
    out_got = flip(out_sent, ZL)

    d_up, d_qkv = after((d_up, d_qkv), out_sent)
    *edge_s, edge_k, sums = edge_sum(d_up, w_up, d_qkv, w_qkv, x, stats, gains)

    *edge_s, edge_k, qkv_g1, up_got, out_g0, sums = after((*edge_s, edge_k, qkv_g1, up_got, out_g0, sums))
    edge_g = [flip(v, CORE) for v in edge_s]
    qkv_sent = add_half(qkv_k1, qkv_g1, qkv_k1.shape[0], 0)
    qkv_got = flip(qkv_sent, ZH)
    up_got, edge_k = after((up_got, edge_k), qkv_sent)
    up_sum = (up_k0 + up_g0.astype(F32) + up_got.astype(F32)).astype(BF16)
    up_back = lay.to_columns(up_sum.reshape(8, rows, hidden))
    edge_k, sums, column_up, column_qkv = after((edge_k, sums, column_up, column_qkv), up_sum)
    column_out = jnp.sum(cotangent.astype(F32), axis=0)
    spread_up = lax.dynamic_update_slice(jnp.zeros((HEADS, hidden), F32), column_up, (here, 0))
    spread_up = spread_up.reshape(2, 2, 2, 2, 2, unit).transpose(3, 0, 1, 4, 2, 5)
    spread_qkv = lax.dynamic_update_slice(jnp.zeros((HEADS, 3 * HEAD), F32), column_qkv, (here, 0))
    spread_qkv = spread_qkv.reshape(2, 2, 2, 3, HEAD).transpose(3, 2, 0, 1, 4)
    sums = restore(sums[:4])
    flat = [v.reshape(n, -1) for v in (sums[0], sums[1], sums[2], sums[3], column_out, spread_qkv, spread_up)]
    flat = jnp.concatenate(flat, axis=1)
    edge_k, up_sum, out_got, flat = after((edge_k, up_sum, out_got, flat))
    *edge_g, edge_k = after((*edge_g, edge_k))
    edge_s1, edge_s0, edge_k = fold_tokens(edge_k, edge_g)
    edge_g1 = flip(edge_s1, Y)

    flat, up_back = after((flat, up_back))
    sums = lax.all_to_all(flat, AXIS, split_axis=0, concat_axis=0, tiled=True)
    qkv_got, qkv_g0, sums, proj_g, edge_k = after((qkv_got, qkv_g0, sums, proj_g, edge_k))
    qkv_sum = (qkv_k0 + qkv_g0.astype(F32) + qkv_got.astype(F32)).astype(BF16)
    qkv_back = lay.to_columns(qkv_sum.reshape(8, rows, 3 * HEAD))
    proj_sum = (proj_k + proj_g.astype(F32)).reshape(2, rows, width)
    proj_kept = lax.dynamic_index_in_dim(proj_sum, mzh, 0, keepdims=False).astype(BF16)
    proj_sent = lax.dynamic_index_in_dim(proj_sum, 1 - mzh, 0, keepdims=False).astype(BF16)
    proj_own = lay.exchange_heads(proj_kept)
    proj_got = lay.exchange_heads(proj_sent, 1 << ZH)
    edge_g1, edge_s0, qkv_sum, proj_sent = after((edge_g1, edge_s0, qkv_sum, proj_sent))
    edge_g0 = flip(edge_s0, Y)
    edge_sent = add_half(edge_k, edge_g1, count, 1)
    edge_got = flip(edge_sent, ZL)
    qkv_back, up_back, out_k, down_k0 = after((qkv_back, up_back, out_k, down_k0), edge_sent)
    grad_up = join_up(up_back)
    grad_qkv = join_qkv(qkv_back)
    layer_out = total([inputs, b_out, out_k, out_g0, out_got], count)
    grad_down = total([down_k0, down_g0, down_got], unit)
    edge_got, edge_g0, edge_k, layer_out, grad_down, grad_up, grad_qkv = after(
        (edge_got, edge_g0, edge_k, layer_out, grad_down, grad_up, grad_qkv)
    )
    grad_inputs = finish(edge_k, edge_g0, edge_got, x0, cotangent, mine)
    proj_own, proj_got, grad_inputs = after((proj_own, proj_got, grad_inputs))
    grad_proj = proj_own.astype(F32) + proj_got.astype(F32)
    sums = jnp.sum(sums, axis=0)
    got, at = [], 0
    for size in [rows] * 5 + [3 * rows, unit]:
        got.append(sums[at : at + size])
        at += size
    return (
        layer_out,
        grad_inputs,
        got[0],
        got[1],
        got[2],
        got[3],
        grad_qkv,
        got[5],
        grad_proj,
        got[4],
        grad_up,
        got[6],
        grad_down,
        got[4],
    )


def solution(mesh):
    tokens, rows = P(AXIS, None), P(AXIS)
    return jax.shard_map(
        local_tuned if mesh.shape[AXIS] == 32 else local_any,
        mesh=mesh,
        in_specs=(tokens, tokens, rows, rows, rows, rows, tokens, rows, tokens, rows, tokens, rows, tokens, rows, tokens),
        out_specs=(tokens, tokens, rows, rows, rows, rows, tokens, rows, tokens, rows, tokens, rows, tokens, rows),
        check_vma=False,
    )
```
